32 devices in a mesh: seq: 4 (over y, x), dp: 8 (over z, core).
Axes of the slice: x: 2, y: 2, z: 4, core: 2. Of those that a mesh axis runs over, the one named last changes fastest.
Arguments:
- tokens: bfloat16 [8, 1024, 2048], P('dp', 'seq'), may hold values from -6 to 6
- doc_ids: int32 [8, 1024], P('dp', 'seq'), may hold values from 0 to 2, as said below
- ln1_gain: bfloat16 [2048], P(('seq', 'dp')), may hold values from 0.5 to 1.5
- ln1_bias: bfloat16 [2048], P(('seq', 'dp')), may hold values from -4 to 4
- ln2_gain: bfloat16 [2048], P(('seq', 'dp')), may hold values from 0.5 to 1.5
- ln2_bias: bfloat16 [2048], P(('seq', 'dp')), may hold values from -4 to 4
- qkv_weight: bfloat16 [2048, 6144], P(('seq', 'dp')), may hold values from -0.125 to 0.125
- qkv_bias: bfloat16 [6144], P(('seq', 'dp')), may hold values from -4 to 4
- out_weight: bfloat16 [2048, 2048], P(('seq', 'dp')), may hold values from -0.75 to 0.75
- up_weight: bfloat16 [2048, 8192], P(('seq', 'dp')), may hold values from -0.125 to 0.125
- up_bias: bfloat16 [8192], P(('seq', 'dp')), may hold values from -4 to 4
- down_weight: bfloat16 [8192, 2048], P(('seq', 'dp')), may hold values from -0.0625 to 0.0625
- out_bias: bfloat16 [2048], P(('seq', 'dp')), may hold values from -4 to 4
- cotangent: bfloat16 [8, 1024, 2048], P('dp', 'seq'), may hold values from -6 to 6
Outputs:
- mixed: bfloat16 [8, 1024, 2048], P('dp', 'seq')
- input_grad: float32 [8, 1024, 2048], P('dp', 'seq')
- ln1_gain_grad: float32 [2048], P(('seq', 'dp'))
- ln1_bias_grad: float32 [2048], P(('seq', 'dp'))
- ln2_gain_grad: float32 [2048], P(('seq', 'dp'))
- ln2_bias_grad: float32 [2048], P(('seq', 'dp'))
- qkv_weight_grad: float32 [2048, 6144], P(('seq', 'dp'))
- qkv_bias_grad: float32 [6144], P(('seq', 'dp'))
- out_weight_grad: float32 [2048, 2048], P(('seq', 'dp'))
- up_weight_grad: float32 [2048, 8192], P(('seq', 'dp'))
- up_bias_grad: float32 [8192], P(('seq', 'dp'))
- down_weight_grad: float32 [8192, 2048], P(('seq', 'dp'))
- out_bias_grad: float32 [2048], P(('seq', 'dp'))
The draws below stay inside these ranges and needn't reach their ends.
Inputs may be any that keep to these rules, and one draw needn't show every extreme that they name: `doc_ids`: each row holds three documents in order: document 0 lies within the row's first 256 tokens, document 2 within its last 256, document 1 covers all tokens between.
All inputs are finite; a program needn't handle non-finite values.
Results may differ from the reference program's by a relative error of at most 0.0092.
Values may be sent and summed in bfloat16 or wider, within the bound.
A program may use at most 448 MiB of HBM per device.

```python
import math
import jax
import jax.numpy as jnp
from jax import lax

D = 2048
FF = 8192
HEADS = 8
HD = 256
ROT = 64
TOK_DEV = 256
LENGTH = 1024
BATCH = 8


def draw_doc_ids(key, part):
    key = jax.random.fold_in(key, 7)
    key_first, key_last = jax.random.split(key)
    first_end = jax.random.randint(key_first, (BATCH, 1), 1, TOK_DEV)
    last_start = LENGTH - jax.random.randint(key_last, (BATCH, 1), 1, TOK_DEV)
    index = jnp.arange(LENGTH, dtype=jnp.int32)[None, :]
    return (index >= first_end).astype(jnp.int32) + (index >= last_start).astype(jnp.int32)


def levels(key, shape, pieces, smallest, high):
    level, own = 1.0, jax.random.fold_in(key, 6)
    for position, parts in pieces:
        heights = jnp.exp(jax.random.uniform(jax.random.fold_in(own, position), (parts,), jnp.float32, smallest / len(pieces), high / len(pieces)))
        level = level * jnp.repeat(heights, shape[position] // parts).reshape([-1 if axis == position else 1 for axis in range(len(shape))])
    return level


def gaussian(own_key, shape, scale, limit, cuts=(), kind=jnp.bfloat16):
    entries = jax.random.normal(own_key, shape, jnp.float32) * scale
    if len(cuts) > 0:
        entries = levels(own_key, shape, cuts, -0.22, 0.18) * entries
    return jnp.clip(entries, min=-limit, max=limit).astype(kind)


def setup_inputs(seed: int = 0) -> dict:
    key_of = jax.random.split(jax.random.key(seed), 15)
    return {
        "tokens": gaussian(key_of[0], (BATCH, LENGTH, D), 1.0, 6.0, ((0, 8), (1, 4))),
        "doc_ids": draw_doc_ids(jax.random.fold_in(key_of[14], 71), 0),
        "ln1_gain": jnp.clip(1.0 + 0.1 * jax.random.normal(key_of[2], (D,), jnp.float32), 0.5, 1.5).astype(jnp.bfloat16),
        "ln1_bias": gaussian(key_of[3], (D,), 0.3, 4.0, ((0, 32),)),
        "ln2_gain": jnp.clip(1.0 + 0.1 * jax.random.normal(key_of[4], (D,), jnp.float32), 0.5, 1.5).astype(jnp.bfloat16),
        "ln2_bias": gaussian(key_of[5], (D,), 0.3, 4.0, ((0, 32),)),
        "qkv_weight": gaussian(key_of[6], (D, 3 * D), D ** -0.5, 0.125, ((0, 32),)),
        "qkv_bias": gaussian(key_of[7], (3 * D,), 0.3, 4.0, ((0, 32),)),
        "out_weight": gaussian(key_of[8], (D, D), (D // 32) ** -0.5, 0.75, ((0, 32),)),
        "up_weight": gaussian(key_of[9], (D, FF), D ** -0.5, 0.125, ((0, 32),)),
        "up_bias": gaussian(key_of[10], (FF,), 0.3, 4.0, ((0, 32),)),
        "down_weight": gaussian(key_of[11], (FF, D), FF ** -0.5, 0.0625, ((0, 32),)),
        "out_bias": gaussian(key_of[12], (D,), 0.3, 4.0, ((0, 32),)),
        "cotangent": gaussian(key_of[13], (BATCH, LENGTH, D), 1.0, 6.0, ((0, 8), (1, 4))),
    }


@jax.custom_vjp
def low(v):
    return lax.optimization_barrier(v.astype(jnp.bfloat16)).astype(jnp.float32)

@jax.custom_vjp
def low_back(v):
    return v

def low_keep(v):
    return (low(v), None)

def low_pass(kept, grad):
    return (grad,)

def back_keep(v):
    return (v, None)

def back_low(kept, grad):
    return (low(grad),)
low.defvjp(low_keep, low_pass)
low_back.defvjp(back_keep, back_low)
epsilon = 1e-05
highest = lax.Precision.HIGHEST

def layer_norm(values, gain_vec, shift_vec):
    center = values - lax.optimization_barrier(jnp.mean(values, -1, keepdims=True))
    spread = lax.optimization_barrier(jnp.mean(center * center, -1, keepdims=True))
    return center * lax.rsqrt(spread + epsilon) * gain_vec + shift_vec

def rotary_tables(positions, rot_dims):
    exponents = jnp.arange(rot_dims // 2).astype(jnp.float32) * (2.0 / rot_dims)
    inverse = jnp.power(10000.0, -exponents)
    phase = positions.astype(jnp.float32)[:, None] * inverse[None, :]
    return (jnp.cos(phase)[:, None, :], jnp.sin(phase)[:, None, :])

def rotate(tensor, cosine, sine_part, rot_dims):
    half_rot = rot_dims // 2
    first_half = tensor[..., :half_rot]
    second = tensor[..., half_rot:rot_dims]
    remainder = tensor[..., rot_dims:]
    return jnp.concatenate([first_half * cosine - second * sine_part, second * cosine + first_half * sine_part, remainder], -1)

def attend(block):
    queries, keys, values, doc_row = block
    seq_len = queries.shape[0]
    raw = jnp.einsum('qhd,khd->hqk', queries, keys, precision=highest) * (1.0 / math.sqrt(HD))
    raw = low_back(raw)
    index = jnp.arange(seq_len)
    allowed = (doc_row[:, None] == doc_row[None, :]) & (index[None, :] <= index[:, None])
    scores = jnp.where(allowed[None], raw, -1000000000.0)
    top = lax.optimization_barrier(jnp.max(scores, -1, keepdims=True))
    expo = jnp.exp(scores - top)
    probabilities = expo / lax.optimization_barrier(jnp.sum(expo, -1, keepdims=True))
    prob_b = low(probabilities)
    return jnp.einsum('hqk,khd->qhd', prob_b, values, precision=highest).reshape(seq_len, D)

def forward(doc_ids, inputs, gain_one, shift_one, gain_two, shift_two, w_qkv, b_qkv, w_out, w_up, b_up, w_down, b_final):
    normed_one = low(layer_norm(inputs, gain_one, shift_one))
    normed_two = low(layer_norm(inputs, gain_two, shift_two))
    proj = low_back(jnp.einsum('bld,de->ble', normed_one, w_qkv, precision=highest) + b_qkv)
    rows_n, seq_len = (inputs.shape[0], inputs.shape[1])
    cosine, sine_part = rotary_tables(jnp.arange(seq_len, dtype=jnp.int32), ROT)
    queries = low(rotate(proj[..., :D].reshape(rows_n, seq_len, HEADS, HD), cosine, sine_part, ROT))
    keys = low(rotate(proj[..., D:2 * D].reshape(rows_n, seq_len, HEADS, HD), cosine, sine_part, ROT))
    values = low(proj[..., 2 * D:].reshape(rows_n, seq_len, HEADS, HD))
    attended = lax.map(jax.checkpoint(attend), (queries, keys, values, doc_ids))
    attended = low(low_back(attended))
    upper = low_back(jnp.einsum('bld,df->blf', normed_two, w_up, precision=highest) + b_up)
    hidden = low(jax.nn.gelu(upper, approximate=False))
    branch_attn = jnp.einsum('bld,de->ble', attended, w_out, precision=highest)
    branch_ffn = jnp.einsum('blf,fe->ble', hidden, w_down, precision=highest)
    return inputs + branch_attn + branch_ffn + b_final

def reference(tokens, doc_ids, ln1_gain, ln1_bias, ln2_gain, ln2_bias, qkv_weight, qkv_bias, out_weight, up_weight, up_bias, down_weight, out_bias, cotangent):
    params = [p.astype(jnp.float32) for p in (ln1_gain, ln1_bias, ln2_gain, ln2_bias, qkv_weight, qkv_bias, out_weight, up_weight, up_bias, down_weight, out_bias)]

    def closed(inputs, *rest):
        return forward(doc_ids, inputs, *rest)
    mixed, pullback = jax.vjp(closed, tokens.astype(jnp.float32), *params)
    grads = pullback(cotangent.astype(jnp.float32))
    return (mixed.astype(jnp.bfloat16), grads[0], grads[1], grads[2], grads[3], grads[4], grads[5], grads[6], grads[7], grads[8], grads[9], grads[10], grads[11])
```

```python
import math

import jax
import jax.numpy as jnp
from jax import lax
from jax.sharding import PartitionSpec as P

HEADS = 8


epsilon = 1e-05


def layer_norm(values, gain_vec, shift_vec):
    center = values - jnp.mean(values, -1, keepdims=True)
    spread = jnp.mean(center * center, -1, keepdims=True)
    return center * lax.rsqrt(spread + epsilon) * gain_vec + shift_vec


def rotary_tables(positions, rot_dims):
    exponents = jnp.arange(rot_dims // 2).astype(jnp.float32) * (2.0 / rot_dims)
    inverse = jnp.power(10000.0, -exponents)
    phase = positions.astype(jnp.float32)[:, None] * inverse[None, :]
    return (jnp.cos(phase)[:, None, :], jnp.sin(phase)[:, None, :])


def rotate(tensor, cosine, sine_part, rot_dims):
    half_rot = rot_dims // 2
    first_half = tensor[..., :half_rot]
    second = tensor[..., half_rot:rot_dims]
    remainder = tensor[..., rot_dims:]
    return jnp.concatenate(
        [
            first_half * cosine - second * sine_part,
            second * cosine + first_half * sine_part,
            remainder,
        ],
        -1,
    )


def rotate_back(grad, cosine, sine_part, rot_dims):
    half_rot = rot_dims // 2
    first_half = grad[..., :half_rot]
    second = grad[..., half_rot:rot_dims]
    remainder = grad[..., rot_dims:]
    return jnp.concatenate(
        [
            first_half * cosine + second * sine_part,
            second * cosine - first_half * sine_part,
            remainder,
        ],
        -1,
    )


def times_transposed(left, right):
    return lax.dot_general(
        left, right, (((1,), (1,)), ((), ())), preferred_element_type=jnp.float32
    )


def inner_rows(left, right):
    return lax.dot_general(
        left, right, (((0,), (0,)), ((), ())), preferred_element_type=jnp.float32
    )


def exact_gelu(values):
    return jax.nn.gelu(values, approximate=False)


BF = jnp.bfloat16
F32 = jnp.float32
ALL = ("seq", "dp")


def dot(left, right):
    return jnp.dot(left, right, preferred_element_type=F32)


def shards(
    tokens,
    doc_ids,
    ln1_gain,
    ln1_bias,
    ln2_gain,
    ln2_bias,
    qkv_weight,
    qkv_bias,
    out_weight,
    up_weight,
    up_bias,
    down_weight,
    out_bias,
    cotangent,
):
    seq_n = lax.axis_size("seq")
    dp_n = lax.axis_size("dp")
    seq_i = lax.axis_index("seq")
    tok_rows, width = tokens.shape[1:]
    length = tok_rows * seq_n
    head_dim = width // HEADS
    heads = HEADS // seq_n
    local = heads * head_dim
    ff = up_weight.shape[1] // seq_n
    rot_dims = head_dim // 4
    scale = 1.0 / math.sqrt(head_dim)

    rows = qkv_weight.shape[0]
    qkv_cut = qkv_weight.reshape(rows, 3, seq_n, local).transpose(2, 0, 1, 3).reshape(seq_n, rows, 3 * local)
    up_cut = up_weight.reshape(rows, seq_n, ff).transpose(1, 0, 2)
    qkv_cut = lax.all_to_all(qkv_cut, "seq", 0, 0, tiled=True)
    up_cut = lax.all_to_all(up_cut, "seq", 0, 0, tiled=True)

    def full(cut):
        return lax.all_gather(cut, "dp", axis=1, tiled=True).reshape(width, -1)

    x_row = lax.all_gather(tokens[0], "seq", axis=0, tiled=True)
    gy = lax.all_gather(cotangent[0], "seq", axis=0, tiled=True)
    small = lax.all_gather(
        jnp.concatenate([ln1_gain, ln1_bias, ln2_gain, ln2_bias, out_bias, qkv_bias, up_bias]),
        ALL,
        axis=0,
    ).astype(F32)
    cuts, at = [], 0
    for v in (ln1_gain, ln1_bias, ln2_gain, ln2_bias, out_bias, qkv_bias, up_bias):
        cuts.append(small[:, at : at + v.shape[0]].reshape(-1))
        at += v.shape[0]
    gain_one, shift_one, gain_two, shift_two, out_shift, qkv_shift, up_shift = cuts
    qkv_shift = lax.dynamic_index_in_dim(
        qkv_shift.reshape(3, seq_n, local), seq_i, 1, False
    ).reshape(-1)
    up_shift = lax.dynamic_slice_in_dim(up_shift, seq_i * ff, ff)
    up_full = full(up_cut)
    qkv_full = full(qkv_cut)
    out_full = lax.all_gather(out_weight, "dp", axis=0, tiled=True)
    down_full = lax.all_gather(down_weight, "dp", axis=0, tiled=True)
    doc_all = lax.all_gather(doc_ids[0].astype(BF), "seq", axis=0, tiled=True)

    inputs = x_row.astype(F32)
    mean = jnp.mean(inputs, -1, keepdims=True)
    center = inputs - mean
    inv = lax.rsqrt(jnp.mean(center * center, -1, keepdims=True) + epsilon)
    xhat = center * inv
    normed_one = (xhat * gain_one + shift_one).astype(BF)
    normed_two = (xhat * gain_two + shift_two).astype(BF)

    upper = dot(normed_two, up_full) + up_shift
    hidden = exact_gelu(upper).astype(BF)
    proj = dot(normed_one, qkv_full) + qkv_shift
    positions = jnp.arange(length, dtype=jnp.int32)
    cosine, sine_part = rotary_tables(positions, rot_dims)
    pq, pk, pv = [proj[:, i * local : (i + 1) * local].reshape(length, heads, head_dim) for i in range(3)]
    queries = rotate(pq, cosine, sine_part, rot_dims).astype(BF)
    keys = rotate(pk, cosine, sine_part, rot_dims).astype(BF)
    values = pv.astype(BF)
    allowed = (doc_all[None, :] == doc_all[:, None]) & (positions[None, :] <= positions[:, None])
    raw = jnp.einsum("qhd,khd->hqk", queries, keys, preferred_element_type=F32) * scale
    scores = jnp.where(allowed[None], raw, -1000000000.0)
    top = jnp.max(scores, -1, keepdims=True)
    expo = jnp.exp(scores - top)
    probs = expo / jnp.sum(expo, -1, keepdims=True)
    prob_b = probs.astype(BF)
    attended = jnp.einsum("hqk,khd->qhd", prob_b, values, preferred_element_type=F32)
    attended = attended.reshape(length, local).astype(BF)
    mixed_part = dot(attended, out_full) + dot(hidden, down_full)
    mixed_sum = lax.psum_scatter(mixed_part.astype(BF), "seq", scatter_dimension=0, tiled=True)
    own = tokens[0].astype(F32)
    mixed = (own + mixed_sum.astype(F32) + out_shift).astype(BF)[None]

    out_term = inner_rows(attended, gy)
    down_term = inner_rows(hidden, gy)
    grad_attn = times_transposed(gy, out_full).astype(BF).reshape(length, heads, head_dim)
    grad_hidden = times_transposed(gy, down_full)
    grad_upper = jax.vjp(exact_gelu, upper)[1](grad_hidden)[0].astype(BF)
    grad_probs = jnp.einsum("qhd,khd->hqk", grad_attn, values, preferred_element_type=F32)
    inner = jnp.sum(grad_probs * probs, -1, keepdims=True)
    grad_scores = (probs * (grad_probs - inner)).astype(BF)
    grad_q = jnp.einsum("hqk,khd->qhd", grad_scores, keys, preferred_element_type=F32) * scale
    grad_k = jnp.einsum("hqk,qhd->khd", grad_scores, queries, preferred_element_type=F32) * scale
    grad_v = jnp.einsum("hqk,qhd->khd", prob_b, grad_attn, preferred_element_type=F32)
    grad_proj = jnp.concatenate(
        [
            rotate_back(grad_q, cosine, sine_part, rot_dims).reshape(length, local),
            rotate_back(grad_k, cosine, sine_part, rot_dims).reshape(length, local),
            grad_v.reshape(length, local),
        ],
        1,
    ).astype(BF)
    qkv_term = inner_rows(normed_one, grad_proj)
    up_term = inner_rows(normed_two, grad_upper)
    grad_one = times_transposed(grad_proj, qkv_full)
    grad_two = times_transposed(grad_upper, up_full)
    wide = grad_one * gain_one + grad_two * gain_two
    wide_sum = lax.psum_scatter(wide.astype(BF), "seq", scatter_dimension=0, tiled=True).astype(F32)
    own_center = own - jnp.mean(own, -1, keepdims=True)
    own_inv = lax.rsqrt(jnp.mean(own_center * own_center, -1, keepdims=True) + epsilon)
    own_hat = own_center * own_inv
    input_grad = cotangent[0].astype(F32) + own_inv * (
        wide_sum
        - jnp.mean(wide_sum, -1, keepdims=True)
        - own_hat * jnp.mean(wide_sum * own_hat, -1, keepdims=True)
    )

    def owned(term):
        cut = term.astype(BF).reshape(seq_n, dp_n, rows, -1)
        cut = lax.psum_scatter(cut, "dp", scatter_dimension=1, tiled=False)
        return lax.all_to_all(cut, "seq", 0, 0, tiled=True).astype(F32)

    up_grad = owned(up_term).transpose(1, 0, 2).reshape(rows, -1)
    qkv_grad = owned(qkv_term).reshape(seq_n, rows, 3, local).transpose(1, 2, 0, 3).reshape(rows, -1)
    out_grad = lax.psum_scatter(out_term.astype(BF), "dp", scatter_dimension=0, tiled=True).astype(F32)
    down_grad = lax.psum_scatter(down_term.astype(BF), "dp", scatter_dimension=0, tiled=True).astype(F32)

    def spread(part):
        out = jnp.zeros((part.shape[0], seq_n, part.shape[1]), F32)
        return lax.dynamic_update_slice_in_dim(out, part[:, None], seq_i, 1).reshape(-1)

    own_gy = cotangent[0].astype(F32)
    pieces = [
        jnp.sum(grad_one * xhat, 0),
        jnp.sum(grad_one, 0),
        jnp.sum(grad_two * xhat, 0),
        jnp.sum(grad_two, 0),
        jnp.sum(own_gy, 0),
        spread(jnp.sum(grad_proj.astype(F32), 0).reshape(3, local)),
        spread(jnp.sum(grad_upper.astype(F32), 0).reshape(1, ff)),
    ]
    n = seq_n * dp_n
    packed = jnp.concatenate([p.reshape(n, -1) for p in pieces], 1)
    packed = lax.psum_scatter(packed, ALL, scatter_dimension=0, tiled=False)
    cuts, at = [], 0
    for p in pieces:
        k = p.shape[0] // n
        cuts.append(packed[at : at + k])
        at += k
    g1, b1, g2, b2, ob, qb, ub = cuts
    return (mixed, input_grad[None], g1, b1, g2, b2, qkv_grad, qb, out_grad, up_grad, ub, down_grad, ob)


def solution(mesh):
    in_specs = (
        P("dp", "seq", None),
        P("dp", "seq"),
        P(("seq", "dp")),
        P(("seq", "dp")),
        P(("seq", "dp")),
        P(("seq", "dp")),
        P(("seq", "dp"), None),
        P(("seq", "dp")),
        P(("seq", "dp"), None),
        P(("seq", "dp"), None),
        P(("seq", "dp")),
        P(("seq", "dp"), None),
        P(("seq", "dp")),
        P("dp", "seq", None),
    )
    out_specs = (
        P("dp", "seq", None),
        P("dp", "seq", None),
        P(("seq", "dp")),
        P(("seq", "dp")),
        P(("seq", "dp")),
        P(("seq", "dp")),
        P(("seq", "dp"), None),
        P(("seq", "dp")),
        P(("seq", "dp"), None),
        P(("seq", "dp"), None),
        P(("seq", "dp")),
        P(("seq", "dp"), None),
        P(("seq", "dp")),
    )
    return jax.shard_map(shards, mesh=mesh, in_specs=in_specs, out_specs=out_specs, check_vma=False)
```

```python
import functools
import math

import jax
import jax.numpy as jnp
from jax import lax
from jax.experimental import pallas as pl
from jax.experimental.pallas import tpu as pltpu
from jax.sharding import PartitionSpec as P

HEADS = 8


epsilon = 1e-05


def layer_norm(values, gain_vec, shift_vec):
    center = values - jnp.mean(values, -1, keepdims=True)
    spread = jnp.mean(center * center, -1, keepdims=True)
    return center * lax.rsqrt(spread + epsilon) * gain_vec + shift_vec


def rotary_tables(positions, rot_dims):
    exponents = jnp.arange(rot_dims // 2).astype(jnp.float32) * (2.0 / rot_dims)
    inverse = jnp.power(10000.0, -exponents)
    phase = positions.astype(jnp.float32)[:, None] * inverse[None, :]
    return (jnp.cos(phase)[:, None, :], jnp.sin(phase)[:, None, :])


def rotate(tensor, cosine, sine_part, rot_dims):
    half_rot = rot_dims // 2
    first_half = tensor[..., :half_rot]
    second = tensor[..., half_rot:rot_dims]
    remainder = tensor[..., rot_dims:]
    return jnp.concatenate(
        [
            first_half * cosine - second * sine_part,
            second * cosine + first_half * sine_part,
            remainder,
        ],
        -1,
    )


def rotate_back(grad, cosine, sine_part, rot_dims):
    half_rot = rot_dims // 2
    first_half = grad[..., :half_rot]
    second = grad[..., half_rot:rot_dims]
    remainder = grad[..., rot_dims:]
    return jnp.concatenate(
        [
            first_half * cosine + second * sine_part,
            second * cosine - first_half * sine_part,
            remainder,
        ],
        -1,
    )


def times_transposed(left, right):
    return lax.dot_general(
        left, right, (((1,), (1,)), ((), ())), preferred_element_type=jnp.float32
    )


def inner_rows(left, right):
    return lax.dot_general(
        left, right, (((0,), (0,)), ((), ())), preferred_element_type=jnp.float32
    )


def exact_gelu(values):
    return jax.nn.gelu(values, approximate=False)


BF = jnp.bfloat16
F32 = jnp.float32
ALL = ("seq", "dp")


def dot(left, right):
    return jnp.dot(left, right, preferred_element_type=F32)


MESH = pl.DeviceIdType.MESH


class Net:
    def __init__(self, seq_n, dp_n, send_sems, recv_sems):
        self.S, self.DP, self.Z = seq_n, dp_n, dp_n // 2
        self.s, self.d = lax.axis_index("seq"), lax.axis_index("dp")
        self.z, self.c = self.d // 2, lax.rem(self.d, 2)
        self.send_sems, self.recv_sems, self.used = send_sems, recv_sems, 0
        self.sent = []

    def seq_peer(self, s):
        return (s, self.d)

    def line_peer(self, z):
        return (self.s, 2 * z + self.c)

    def partner(self):
        return (self.s, 2 * self.z + 1 - self.c)

    def copy(self, src, dst, device):
        i = self.used
        self.used += 1
        return pltpu.make_async_remote_copy(
            src_ref=src,
            dst_ref=dst,
            send_sem=self.send_sems.at[i],
            recv_sem=self.recv_sems.at[i],
            device_id=device,
            device_id_type=MESH,
        )

    def send(self, copy, when=None):
        self.sent.append((copy, when))
        run(when, copy.start)

    def drain(self):
        for copy, when in self.sent:
            run(when, copy.wait_send)
        self.sent = []

    def barrier(self, every_dp):
        sem = pltpu.get_barrier_semaphore()

        def greet(device):
            pl.semaphore_signal(sem, inc=1, device_id=device, device_id_type=MESH)

        for k in range(1, self.S):
            greet(self.seq_peer(lax.rem(self.s + k, self.S)))
        if every_dp:
            for k in range(1, self.DP):
                greet((self.s, lax.rem(self.d + k, self.DP)))
            count = self.S - 1 + self.DP - 1
        else:
            greet(self.partner())
            run(self.z > 0, lambda: greet(self.line_peer(self.z - 1)))
            run(self.z < self.Z - 1, lambda: greet(self.line_peer(self.z + 1)))
            count = self.S + (self.z > 0).astype(jnp.int32) + (self.z < self.Z - 1).astype(jnp.int32)
        pl.semaphore_wait(sem, count)


def run(when, action):
    if when is None:
        action()
    else:
        pl.when(when)(lambda: action())


class Local:
    def __init__(self, sems):
        self.sems, self.used, self.open = sems, 0, []

    def start(self, src, dst):
        copy = pltpu.make_async_copy(src, dst, self.sems.at[self.used])
        self.used += 1
        copy.start()
        return copy

    def through(self, pairs):
        loads = [(self.start(src, buf), buf, dst) for src, buf, dst in pairs]
        stores = []
        for load, buf, dst in loads:
            load.wait()
            stores.append(self.start(buf, dst))
        return stores


class Exchange:
    def __init__(self, net, src, slot):
        self.net, self.arrivals = net, []
        for k in range(1, net.S):
            to, source = lax.rem(net.s + k, net.S), lax.rem(net.s + net.S - k, net.S)
            copy = net.copy(src(to), slot(net.s), net.seq_peer(to))
            net.send(copy)
            self.arrivals.append((copy, slot(source)))

    def wait(self):
        for copy, _ in self.arrivals:
            copy.wait_recv()
        self.arrivals = []


class GatherSeq:
    def __init__(self, net, src, slot):
        self.net, self.slot = net, slot
        s = net.s
        if net.S == 4:
            self.a = s + 1 - 2 * lax.rem(s, 2)
            self.b = lax.rem(s + 2, 4)
            self.near = [net.copy(src, slot(s, None), net.seq_peer(p)) for p in (self.a, self.b)]
            for copy in self.near:
                net.send(copy)
        else:
            self.exchange = Exchange(net, lambda to: src, lambda k: slot(k, None))

    def relay(self):
        net = self.net
        if net.S == 4:
            self.far = [
                net.copy(self.slot(self.a, 0), self.slot(self.a, 0), net.seq_peer(self.b)),
                net.copy(self.slot(self.b, 1), self.slot(self.b, 1), net.seq_peer(self.a)),
            ]
            for near, far in zip(self.near, self.far):
                near.wait_recv()
                net.send(far)

    def wait(self):
        if self.net.S == 4:
            for copy in self.far:
                copy.wait_recv()
        else:
            self.exchange.wait()


class GatherLine:
    def __init__(self, net, slab, own=None):
        self.net, self.slab = net, slab
        z, c, Z = net.z, net.c, net.Z
        own = slab(net.d) if own is None else own
        self.right, self.left, self.core = [], [], []
        for t in range(Z):
            for side, lst in ((1, self.right), (-1, self.left)):
                src = own if t == 0 else slab(2 * jnp.clip(z - side * t, 0, Z - 1) + c)
                dst = slab(2 * jnp.clip(z - side * t, 0, Z - 1) + c)
                there = (z - t >= 0) if side == 1 else (z + t <= Z - 1)
                may = (z < Z - 1) if side == 1 else (z > 0)
                lst.append([None if t == Z - 1 else net.copy(src, dst, net.line_peer(jnp.clip(z + side, 0, Z - 1))), there & may, there])
                if t == 0 and side == -1:
                    lst[-1].append(None)
                else:
                    lst[-1].append(net.copy(src, dst, net.partner()))
        self.step(0)

    def step(self, t):
        for lst in (self.right, self.left):
            copy, sends, there, core = lst[t]
            if t > 0:
                arrived = lst[t - 1][0]
                run(there, arrived.wait_recv)
            if copy is not None:
                self.net.send(copy, sends)
            if core is not None:
                self.net.send(core, None if t == 0 else there)

    def wait(self):
        for t in range(self.net.Z):
            for lst in (self.right, self.left):
                _, _, there, core = lst[t]
                if core is not None:
                    run(None if t == 0 else there, core.wait_recv)


def add_slabs(dst, left, right, scale_rows=16):
    blocks, rows = dst.shape[0], dst.shape[1]
    per = rows // scale_rows

    @pl.loop(0, blocks * per)
    def _(i):
        at = (i // per, pl.ds(pl.multiple_of(lax.rem(i, per) * scale_rows, scale_rows), scale_rows), slice(None))
        dst[at] = (left[at].astype(F32) + right[at].astype(F32)).astype(dst.dtype)


class ReduceLine:
    def __init__(self, net, part, own, mate, from_left, from_right, local):
        self.net, self.own, self.mate = net, own, mate
        self.from_left, self.from_right = from_left, from_right
        z, c, Z = net.z, net.c, net.Z
        order = []
        for t in range((Z + 1) // 2):
            order += [Z - 1 - t] + ([t] if t != Z - 1 - t else [])
        self.loads, self.swaps = {}, {}
        for zd in order:
            swap = net.copy(part(2 * zd + 1 - c), mate.at[zd], net.partner())
            net.send(swap)
            self.swaps[zd] = swap
            self.loads[zd] = local.start(part(2 * zd + c), own.at[zd])
        self.order = order
        self.base = net.used
        net.used += 2 * (Z - 1)

    def hop(self, side, t):
        net = self.net
        last = net.Z - 1
        if side == 1:
            src, dst, i = self.own.at[last - t], self.from_left.at[t], self.base + t
        else:
            src, dst, i = self.own.at[t], self.from_right.at[t], self.base + last + t
        return pltpu.make_async_remote_copy(
            src_ref=src,
            dst_ref=dst,
            send_sem=net.send_sems.at[i],
            recv_sem=net.recv_sems.at[i],
            device_id=net.line_peer(jnp.clip(net.z + side, 0, last)),
            device_id_type=MESH,
        )

    def pair(self):
        net, done = self.net, set()
        right, left = net.Z - 1, 0
        for zd in self.order:
            self.loads[zd].wait()
            self.swaps[zd].wait_recv()
            add_slabs(self.own.at[zd], self.own.at[zd], self.mate.at[zd])
            done.add(zd)
            while right > 0 and right in done:
                net.send(self.hop(1, net.Z - 1 - right), net.z == 0)
                right -= 1
            while left < net.Z - 1 and left in done:
                net.send(self.hop(-1, left), net.z == net.Z - 1)
                left += 1

    def step(self, n):
        net = self.net
        z, last = net.z, net.Z - 1
        for side, far, buf in ((1, z, self.from_left), (-1, last - z, self.from_right)):
            t = jnp.clip(n - far, 0, last - 1)
            here = (far >= 1) & (far <= n)
            through = here & (n < last)
            place = last - t if side == 1 else t
            hop = self.hop(side, t)
            run(here, hop.wait_recv)
            if n < last:
                run(through, lambda: add_slabs(self.own.at[place], self.own.at[place], buf.at[t]))
                net.send(hop, through)

    def total(self, out):
        net = self.net
        z, Z = net.z, net.Z
        blocks, rows = out.shape[0], out.shape[1]
        per = rows // 16

        def body(use_left, use_right):
            @pl.loop(0, blocks * per)
            def _(i):
                at = (i // per, pl.ds(pl.multiple_of(lax.rem(i, per) * 16, 16), 16), slice(None))
                value = self.own.at[z][at].astype(F32)
                if use_left:
                    value = value + self.from_left.at[Z - 1 - z][at].astype(F32)
                if use_right:
                    value = value + self.from_right.at[z][at].astype(F32)
                out[at] = value

        run(z == 0, lambda: body(False, True))
        run(z == Z - 1, lambda: body(True, False))
        if Z > 2:
            run((z > 0) & (z < Z - 1), lambda: body(True, True))


def gather_kernel(seq_n, dp_n, x, gy, up, qkv, out_w, down_w, small, x_all, gy_all, up_all, qkv_all, out_all, down_all, small_all, send_sems, recv_sems, local_sems, *bufs):
    net = Net(seq_n, dp_n, send_sems, recv_sems)
    local = Local(local_sems)
    s, d = net.s, net.d
    half = x.shape[0] // 2
    net.barrier(True)
    smalls = []
    for k in range(1, dp_n):
        to, source = lax.rem(d + k, dp_n), lax.rem(d + dp_n - k, dp_n)
        copy = net.copy(small, small_all.at[s, d], (s, to))
        net.send(copy)
        smalls.append(copy)
    out_line = GatherLine(net, lambda k: out_all.at[k], out_w)
    up_swap = Exchange(net, lambda k: up.at[k], lambda k: up_all.at[k, d])
    rows = lambda h: slice(None) if h is None else pl.ds(h * half, half)
    own = [
        (up.at[s], up_all.at[s, d]),
        (qkv.at[s], qkv_all.at[s, d]),
        (small, small_all.at[s, d]),
        (x, x_all.at[s]),
        (gy, gy_all.at[s]),
        (out_w, out_all.at[d]),
        (down_w, down_all.at[d]),
    ]
    mine = local.through([(src, buf, dst) for (src, dst), buf in zip(own, bufs)])
    out_line.step(1)
    up_swap.wait()
    for copy in mine:
        copy.wait()
    up_line = GatherLine(net, lambda k: up_all.at[:, k])
    x_seq = GatherSeq(net, x, lambda k, h: x_all.at[k, rows(h)])
    qkv_swap = Exchange(net, lambda k: qkv.at[k], lambda k: qkv_all.at[k, d])
    for t in range(2, net.Z):
        out_line.step(t)
    for copy in smalls:
        copy.wait_recv()
    small_seq = Exchange(net, lambda k: small_all.at[s], lambda k: small_all.at[k])
    up_line.step(1)
    qkv_swap.wait()
    x_seq.relay()
    gy_seq = GatherSeq(net, gy, lambda k, h: gy_all.at[k, rows(h)])
    qkv_line = GatherLine(net, lambda k: qkv_all.at[:, k])
    for t in range(2, net.Z):
        up_line.step(t)
    gy_seq.relay()
    qkv_line.step(1)
    down_line = GatherLine(net, lambda k: down_all.at[k], down_w)
    for t in range(2, net.Z):
        qkv_line.step(t)
    for t in range(1, net.Z):
        down_line.step(t)
    small_seq.wait()
    x_seq.wait()
    gy_seq.wait()
    for line in (out_line, up_line, qkv_line, down_line):
        line.wait()
    net.drain()


ANY = pl.BlockSpec(memory_space=pl.ANY)


def gather_all(seq_n, dp_n, x, gy, up, qkv, out_w, down_w, small):
    n = seq_n + 2 * dp_n + 16 * seq_n + 4 * 4 * dp_n
    shape = jax.ShapeDtypeStruct
    return pl.pallas_call(
        functools.partial(gather_kernel, seq_n, dp_n),
        out_shape=(
            shape((seq_n,) + x.shape, BF),
            shape((seq_n,) + x.shape, BF),
            shape((seq_n, dp_n) + up.shape[1:], BF),
            shape((seq_n, dp_n) + qkv.shape[1:], BF),
            shape((dp_n,) + out_w.shape, BF),
            shape((dp_n,) + down_w.shape, BF),
            shape((seq_n, dp_n) + small.shape, BF),
        ),
        in_specs=[ANY] * 7,
        out_specs=[ANY] * 7,
        scratch_shapes=[pltpu.SemaphoreType.DMA((n,)), pltpu.SemaphoreType.DMA((n,)), pltpu.SemaphoreType.DMA((16,))]
        + [pltpu.VMEM(v, BF) for v in (up.shape[1:], qkv.shape[1:], small.shape, x.shape, gy.shape, out_w.shape, down_w.shape)],
        compiler_params=pltpu.CompilerParams(collective_id=0, has_side_effects=True, vmem_limit_bytes=32 * 1024 * 1024),
        name="gather_all",
    )(x, gy, up, qkv, out_w, down_w, small)


def reduce_kernel(seq_n, dp_n, up, qkv, out_t, down_t, mixed, wide, up_out, qkv_out, out_out, down_out, mixed_in, wide_in, send_sems, recv_sems, local_sems, *bufs):
    net = Net(seq_n, dp_n, send_sems, recv_sems)
    local = Local(local_sems)
    s = net.s
    up_f, qkv_f, out_f, down_f = bufs[:4]
    lines = [bufs[4 + 4 * i : 8 + 4 * i] for i in range(4)]
    net.barrier(False)
    up_line = ReduceLine(net, lambda k: up.at[:, k], *lines[0], local)
    wide_x = Exchange(net, lambda k: wide.at[k], lambda k: wide_in.at[k])
    mixed_x = Exchange(net, lambda k: mixed.at[k], lambda k: mixed_in.at[k])
    mine = [local.start(wide.at[s], wide_in.at[s]), local.start(mixed.at[s], mixed_in.at[s])]
    Z = net.Z
    up_line.pair()
    down_line = ReduceLine(net, lambda k: down_t.at[pl.ds(k, 1)], *lines[2], local)
    up_line.step(1)
    down_line.pair()
    for n in range(2, Z):
        up_line.step(n)
    up_line.total(up_f)
    ff, loc = up_f.shape[2], qkv_f.shape[2] // 3
    up_cols = lambda k: up_out.at[:, pl.ds(pl.multiple_of(k * ff, 128), ff)]
    up_x = Exchange(net, lambda k: up_f.at[k], up_cols)
    mine.append(local.start(up_f.at[s], up_cols(s)))
    qkv_line = ReduceLine(net, lambda k: qkv.at[:, k], *lines[1], local)
    down_line.step(1)
    qkv_line.pair()
    for n in range(2, Z):
        down_line.step(n)
    down_line.total(down_f)
    mine.append(local.start(down_f, down_out))
    out_line = ReduceLine(net, lambda k: out_t.at[pl.ds(k, 1)], *lines[3], local)
    qkv_line.step(1)
    out_line.pair()
    for n in range(2, Z):
        qkv_line.step(n)
    qkv_line.total(qkv_f)
    qkv_x = []
    for j in range(3):
        cols = lambda k, j=j: qkv_out.at[:, pl.ds(pl.multiple_of((j * seq_n + k) * loc, 128), loc)]
        qkv_x.append(Exchange(net, lambda k, j=j: qkv_f.at[k, :, pl.ds(j * loc, loc)], cols))
        mine.append(local.start(qkv_f.at[s, :, pl.ds(j * loc, loc)], cols(s)))
    for n in range(1, Z):
        out_line.step(n)
    out_line.total(out_f)
    mine.append(local.start(out_f, out_out))
    for x in [wide_x, mixed_x, up_x] + qkv_x:
        x.wait()
    for copy in mine:
        copy.wait()
    net.drain()


def reduce_all(seq_n, dp_n, up, qkv, out_t, down_t, mixed, wide):
    n = 24 * seq_n + 4 * 6 * dp_n
    shape = jax.ShapeDtypeStruct
    Z = dp_n // 2
    r, ff, loc3 = up.shape[2], up.shape[3], qkv.shape[3]
    slabs = [(seq_n, r, ff), (seq_n, r, loc3), (1,) + down_t.shape[1:], (1,) + out_t.shape[1:]]
    bufs = [pltpu.VMEM(slabs[i], F32) for i in (0, 1, 3, 2)]
    for slab in slabs:
        bufs += [pltpu.VMEM((Z,) + slab, BF)] * 2 + [pltpu.VMEM((Z - 1,) + slab, BF)] * 2
    return pl.pallas_call(
        functools.partial(reduce_kernel, seq_n, dp_n),
        out_shape=(
            shape((r, seq_n * ff), F32),
            shape((r, seq_n * loc3), F32),
            shape((1,) + out_t.shape[1:], F32),
            shape((1,) + down_t.shape[1:], F32),
            shape(mixed.shape, BF),
            shape(wide.shape, BF),
        ),
        in_specs=[ANY] * 6,
        out_specs=[ANY] * 6,
        scratch_shapes=[pltpu.SemaphoreType.DMA((n,)), pltpu.SemaphoreType.DMA((n,)), pltpu.SemaphoreType.DMA((8 * dp_n,))] + bufs,
        compiler_params=pltpu.CompilerParams(collective_id=1, has_side_effects=True, vmem_limit_bytes=60 * 1024 * 1024),
        name="reduce_all",
    )(up, qkv, out_t, down_t, mixed, wide)


def shards(
    tokens,
    doc_ids,
    ln1_gain,
    ln1_bias,
    ln2_gain,
    ln2_bias,
    qkv_weight,
    qkv_bias,
    out_weight,
    up_weight,
    up_bias,
    down_weight,
    out_bias,
    cotangent,
):
    seq_n = lax.axis_size("seq")
    dp_n = lax.axis_size("dp")
    seq_i = lax.axis_index("seq")
    tok_rows, width = tokens.shape[1:]
    length = tok_rows * seq_n
    head_dim = width // HEADS
    heads = HEADS // seq_n
    local = heads * head_dim
    ff = up_weight.shape[1] // seq_n
    rot_dims = head_dim // 4
    scale = 1.0 / math.sqrt(head_dim)

    rows = qkv_weight.shape[0]
    qkv_cut = qkv_weight.reshape(rows, 3, seq_n, local).transpose(2, 0, 1, 3).reshape(seq_n, rows, 3 * local)
    up_cut = up_weight.reshape(rows, seq_n, ff).transpose(1, 0, 2)
    small = jnp.concatenate(
        [ln1_gain, ln1_bias, ln2_gain, ln2_bias, out_bias, qkv_bias, up_bias, doc_ids[0].astype(BF)]
    )
    own_small = small.shape[0]
    lanes = 128
    tall = -(-own_small // (16 * lanes)) * 16
    small = jnp.pad(small, (0, tall * lanes - own_small)).reshape(tall, lanes)
    x_row, gy, up_full, qkv_full, out_full, down_full, small = gather_all(
        seq_n, dp_n, tokens[0], cotangent[0], up_cut, qkv_cut, out_weight, down_weight, small
    )
    x_row, gy = x_row.reshape(length, width), gy.reshape(length, width)
    up_full, qkv_full = up_full.reshape(width, ff), qkv_full.reshape(width, 3 * local)
    out_full, down_full = out_full.reshape(local, width), down_full.reshape(ff, width)
    small = small.reshape(seq_n, dp_n, -1)
    doc_all = lax.dynamic_index_in_dim(small[:, :, own_small - tok_rows : own_small], lax.axis_index("dp"), 1, False).reshape(-1)
    small = small.reshape(seq_n * dp_n, -1).astype(F32)
    cuts, at = [], 0
    for v in (ln1_gain, ln1_bias, ln2_gain, ln2_bias, out_bias, qkv_bias, up_bias):
        cuts.append(small[:, at : at + v.shape[0]].reshape(-1))
        at += v.shape[0]
    gain_one, shift_one, gain_two, shift_two, out_shift, qkv_shift, up_shift = cuts
    qkv_shift = lax.dynamic_index_in_dim(
        qkv_shift.reshape(3, seq_n, local), seq_i, 1, False
    ).reshape(-1)
    up_shift = lax.dynamic_slice_in_dim(up_shift, seq_i * ff, ff)

    inputs = x_row.astype(F32)
    mean = jnp.mean(inputs, -1, keepdims=True)
    center = inputs - mean
    inv = lax.rsqrt(jnp.mean(center * center, -1, keepdims=True) + epsilon)
    xhat = center * inv
    normed_one = (xhat * gain_one + shift_one).astype(BF)
    normed_two = (xhat * gain_two + shift_two).astype(BF)

    upper = dot(normed_two, up_full) + up_shift
    hidden = exact_gelu(upper).astype(BF)
    proj = dot(normed_one, qkv_full) + qkv_shift
    positions = jnp.arange(length, dtype=jnp.int32)
    cosine, sine_part = rotary_tables(positions, rot_dims)
    pq, pk, pv = [proj[:, i * local : (i + 1) * local].reshape(length, heads, head_dim) for i in range(3)]
    queries = rotate(pq, cosine, sine_part, rot_dims).astype(BF)
    keys = rotate(pk, cosine, sine_part, rot_dims).astype(BF)
    values = pv.astype(BF)
    allowed = (doc_all[None, :] == doc_all[:, None]) & (positions[None, :] <= positions[:, None])
    raw = jnp.einsum("qhd,khd->hqk", queries, keys, preferred_element_type=F32) * scale
    scores = jnp.where(allowed[None], raw, -1000000000.0)
    top = jnp.max(scores, -1, keepdims=True)
    expo = jnp.exp(scores - top)
    probs = expo / jnp.sum(expo, -1, keepdims=True)
    prob_b = probs.astype(BF)
    attended = jnp.einsum("hqk,khd->qhd", prob_b, values, preferred_element_type=F32)
    attended = attended.reshape(length, local).astype(BF)
    mixed_part = dot(attended, out_full) + dot(hidden, down_full)
    own = tokens[0].astype(F32)

    out_term = inner_rows(attended, gy)
    down_term = inner_rows(hidden, gy)
    grad_attn = times_transposed(gy, out_full).astype(BF).reshape(length, heads, head_dim)
    grad_hidden = times_transposed(gy, down_full)
    grad_upper = jax.vjp(exact_gelu, upper)[1](grad_hidden)[0].astype(BF)
    grad_probs = jnp.einsum("qhd,khd->hqk", grad_attn, values, preferred_element_type=F32)
    inner = jnp.sum(grad_probs * probs, -1, keepdims=True)
    grad_scores = (probs * (grad_probs - inner)).astype(BF)
    grad_q = jnp.einsum("hqk,khd->qhd", grad_scores, keys, preferred_element_type=F32) * scale
    grad_k = jnp.einsum("hqk,qhd->khd", grad_scores, queries, preferred_element_type=F32) * scale
    grad_v = jnp.einsum("hqk,qhd->khd", prob_b, grad_attn, preferred_element_type=F32)
    grad_proj = jnp.concatenate(
        [
            rotate_back(grad_q, cosine, sine_part, rot_dims).reshape(length, local),
            rotate_back(grad_k, cosine, sine_part, rot_dims).reshape(length, local),
            grad_v.reshape(length, local),
        ],
        1,
    ).astype(BF)
    qkv_term = inner_rows(normed_one, grad_proj)
    up_term = inner_rows(normed_two, grad_upper)
    grad_one = times_transposed(grad_proj, qkv_full)
    grad_two = times_transposed(grad_upper, up_full)
    wide = grad_one * gain_one + grad_two * gain_two
    cut = (seq_n, dp_n, rows, -1)
    blocks = (seq_n, tok_rows, width)
    up_grad, qkv_grad, out_grad, down_grad, mixed_in, wide_in = reduce_all(
        seq_n,
        dp_n,
        up_term.astype(BF).reshape(cut),
        qkv_term.astype(BF).reshape(cut),
        out_term.astype(BF).reshape(dp_n, -1, width),
        down_term.astype(BF).reshape(dp_n, -1, width),
        mixed_part.astype(BF).reshape(blocks),
        wide.astype(BF).reshape(blocks),
    )
    out_grad, down_grad = out_grad[0], down_grad[0]
    mixed = (own + jnp.sum(mixed_in.astype(F32), 0) + out_shift).astype(BF)[None]
    wide_sum = jnp.sum(wide_in.astype(F32), 0)
    own_center = own - jnp.mean(own, -1, keepdims=True)
    own_inv = lax.rsqrt(jnp.mean(own_center * own_center, -1, keepdims=True) + epsilon)
    own_hat = own_center * own_inv
    input_grad = cotangent[0].astype(F32) + own_inv * (
        wide_sum
        - jnp.mean(wide_sum, -1, keepdims=True)
        - own_hat * jnp.mean(wide_sum * own_hat, -1, keepdims=True)
    )

    def spread(part):
        out = jnp.zeros((part.shape[0], seq_n, part.shape[1]), F32)
        return lax.dynamic_update_slice_in_dim(out, part[:, None], seq_i, 1).reshape(-1)

    own_gy = cotangent[0].astype(F32)
    pieces = [
        jnp.sum(grad_one * xhat, 0),
        jnp.sum(grad_one, 0),
        jnp.sum(grad_two * xhat, 0),
        jnp.sum(grad_two, 0),
        jnp.sum(own_gy, 0),
        spread(jnp.sum(grad_proj.astype(F32), 0).reshape(3, local)),
        spread(jnp.sum(grad_upper.astype(F32), 0).reshape(1, ff)),
    ]
    n = seq_n * dp_n
    packed = jnp.concatenate([p.reshape(n, -1) for p in pieces], 1)
    packed = lax.psum_scatter(packed, ALL, scatter_dimension=0, tiled=False)
    cuts, at = [], 0
    for p in pieces:
        k = p.shape[0] // n
        cuts.append(packed[at : at + k])
        at += k
    g1, b1, g2, b2, ob, qb, ub = cuts
    return (mixed, input_grad[None], g1, b1, g2, b2, qkv_grad, qb, out_grad, up_grad, ub, down_grad, ob)


def solution(mesh):
    in_specs = (
        P("dp", "seq", None),
        P("dp", "seq"),
        P(("seq", "dp")),
        P(("seq", "dp")),
        P(("seq", "dp")),
        P(("seq", "dp")),
        P(("seq", "dp"), None),
        P(("seq", "dp")),
        P(("seq", "dp"), None),
        P(("seq", "dp"), None),
        P(("seq", "dp")),
        P(("seq", "dp"), None),
        P(("seq", "dp")),
        P("dp", "seq", None),
    )
    out_specs = (
        P("dp", "seq", None),
        P("dp", "seq", None),
        P(("seq", "dp")),
        P(("seq", "dp")),
        P(("seq", "dp")),
        P(("seq", "dp")),
        P(("seq", "dp"), None),
        P(("seq", "dp")),
        P(("seq", "dp"), None),
        P(("seq", "dp"), None),
        P(("seq", "dp")),
        P(("seq", "dp"), None),
        P(("seq", "dp")),
    )
    return jax.shard_map(shards, mesh=mesh, in_specs=in_specs, out_specs=out_specs, check_vma=False)
```

```python
import functools
import math

import jax
import jax.numpy as jnp
from jax import lax
from jax.experimental import pallas as pl
from jax.experimental.pallas import tpu as pltpu
from jax.sharding import PartitionSpec as P

HEADS = 8


epsilon = 1e-05


def rotary_tables(positions, rot_dims):
    exponents = jnp.arange(rot_dims // 2).astype(jnp.float32) * (2.0 / rot_dims)
    inverse = jnp.power(10000.0, -exponents)
    phase = positions.astype(jnp.float32)[:, None] * inverse[None, :]
    return jnp.cos(phase), jnp.sin(phase)


BF = jnp.bfloat16
F32 = jnp.float32


def dot(left, right):
    return jnp.dot(left, right, preferred_element_type=F32)


MESH = pl.DeviceIdType.MESH


class Net:
    def __init__(self, seq_n, dp_n, send_sems, recv_sems):
        self.S, self.DP, self.Z = seq_n, dp_n, dp_n // 2
        self.s, self.d = lax.axis_index("seq"), lax.axis_index("dp")
        self.z, self.c = self.d // 2, lax.rem(self.d, 2)
        self.send_sems, self.recv_sems, self.used = send_sems, recv_sems, 0
        self.sent = []

    def seq_peer(self, s):
        return (s, self.d)

    def line_peer(self, z):
        return (self.s, 2 * z + self.c)

    def partner(self):
        return (self.s, 2 * self.z + 1 - self.c)

    def copy(self, src, dst, device):
        i = self.used
        self.used += 1
        return pltpu.make_async_remote_copy(
            src_ref=src,
            dst_ref=dst,
            send_sem=self.send_sems.at[i],
            recv_sem=self.recv_sems.at[i],
            device_id=device,
            device_id_type=MESH,
        )

    def send(self, copy, when=None):
        self.sent.append((copy, when))
        run(when, copy.start)

    def drain(self):
        for copy, when in self.sent:
            run(when, copy.wait_send)
        self.sent = []

    def barrier(self, every_dp):
        sem = pltpu.get_barrier_semaphore()

        def greet(device):
            pl.semaphore_signal(sem, inc=1, device_id=device, device_id_type=MESH)

        for k in range(1, self.S):
            greet(self.seq_peer(lax.rem(self.s + k, self.S)))
        if every_dp:
            for k in range(1, self.DP):
                greet((self.s, lax.rem(self.d + k, self.DP)))
            count = self.S - 1 + self.DP - 1
        else:
            greet(self.partner())
            run(self.z > 0, lambda: greet(self.line_peer(self.z - 1)))
            run(self.z < self.Z - 1, lambda: greet(self.line_peer(self.z + 1)))
            count = self.S + (self.z > 0).astype(jnp.int32) + (self.z < self.Z - 1).astype(jnp.int32)
        pl.semaphore_wait(sem, count)


def run(when, action):
    if when is None:
        action()
    else:
        pl.when(when)(lambda: action())


class Local:
    def __init__(self, sems):
        self.sems, self.used, self.open = sems, 0, []

    def make(self, src, dst):
        copy = pltpu.make_async_copy(src, dst, self.sems.at[self.used])
        self.used += 1
        return copy

    def start(self, src, dst):
        copy = self.make(src, dst)
        copy.start()
        return copy

    def through(self, pairs):
        loads = [(self.start(src, buf), buf, dst) for src, buf, dst in pairs]
        stores = []
        for load, buf, dst in loads:
            load.wait()
            stores.append(self.start(buf, dst))
        return stores


class Exchange:
    def __init__(self, net, src, slot, by_turn=False):
        self.arrivals = []
        for k in range(1, net.S):
            to = lax.rem(net.s + k, net.S)
            copy = net.copy(src(to), slot(k - 1 if by_turn else net.s), net.seq_peer(to))
            net.send(copy)
            self.arrivals.append(copy)

    def wait(self):
        for copy in self.arrivals:
            copy.wait_recv()


class GatherSeq:
    def __init__(self, net, src, slot):
        self.net, self.slot = net, slot
        s = net.s
        if net.S == 4:
            self.a = s + 1 - 2 * lax.rem(s, 2)
            self.b = lax.rem(s + 2, 4)
            self.near = [net.copy(src, slot(s, None), net.seq_peer(p)) for p in (self.a, self.b)]
            for copy in self.near:
                net.send(copy)
        else:
            self.exchange = Exchange(net, lambda to: src, lambda k: slot(k, None))

    def relay(self):
        net = self.net
        if net.S == 4:
            self.far = [
                net.copy(self.slot(self.a, 0), self.slot(self.a, 0), net.seq_peer(self.b)),
                net.copy(self.slot(self.b, 1), self.slot(self.b, 1), net.seq_peer(self.a)),
            ]
            for near, far in zip(self.near, self.far):
                near.wait_recv()
                net.send(far)

    def wait(self):
        if self.net.S == 4:
            for copy in self.far:
                copy.wait_recv()
        else:
            self.exchange.wait()


class GatherLine:
    def __init__(self, net, slab, own=None):
        self.net, self.slab = net, slab
        z, c, Z = net.z, net.c, net.Z
        own = slab(net.d) if own is None else own
        self.right, self.left, self.core = [], [], []
        for t in range(Z):
            for side, lst in ((1, self.right), (-1, self.left)):
                src = own if t == 0 else slab(2 * jnp.clip(z - side * t, 0, Z - 1) + c)
                dst = slab(2 * jnp.clip(z - side * t, 0, Z - 1) + c)
                there = (z - t >= 0) if side == 1 else (z + t <= Z - 1)
                may = (z < Z - 1) if side == 1 else (z > 0)
                lst.append([None if t == Z - 1 else net.copy(src, dst, net.line_peer(jnp.clip(z + side, 0, Z - 1))), there & may, there])
                if t == 0 and side == -1:
                    lst[-1].append(None)
                else:
                    lst[-1].append(net.copy(src, dst, net.partner()))

    def early(self):
        self.net.send(self.right[0][0], self.net.z == 0)
        self.net.send(self.left[0][0], self.net.z == self.net.Z - 1)

    def start(self):
        net = self.net
        net.send(self.right[0][0], (net.z > 0) & (net.z < net.Z - 1))
        net.send(self.left[0][0], (net.z > 0) & (net.z < net.Z - 1))
        net.send(self.right[0][3])

    def step(self, t):
        for lst in (self.right, self.left):
            copy, sends, there, core = lst[t]
            if t > 0:
                arrived = lst[t - 1][0]
                run(there, arrived.wait_recv)
            if copy is not None:
                self.net.send(copy, sends)
            if core is not None:
                self.net.send(core, None if t == 0 else there)

    def wait(self):
        for t in range(self.net.Z):
            for lst in (self.right, self.left):
                _, _, there, core = lst[t]
                if core is not None:
                    run(None if t == 0 else there, core.wait_recv)


def add_slabs(dst, left, right, scale_rows=16):
    blocks, rows = dst.shape[0], dst.shape[1]
    per = rows // scale_rows

    @pl.loop(0, blocks * per)
    def _(i):
        at = (i // per, pl.ds(pl.multiple_of(lax.rem(i, per) * scale_rows, scale_rows), scale_rows), slice(None))
        dst[at] = (left[at].astype(F32) + right[at].astype(F32)).astype(dst.dtype)


class ReduceLine:
    def __init__(self, net, part, own, mate, from_left, from_right, local):
        self.net, self.own, self.mate, self.local = net, own, mate, local
        self.from_left, self.from_right = from_left, from_right
        z, c, Z = net.z, net.c, net.Z
        order = []
        for t in range((Z + 1) // 2):
            order += [Z - 1 - t] + ([t] if t != Z - 1 - t else [])
        self.loads, self.swaps = {}, {}
        for zd in order:
            swap = net.copy(part(2 * zd + 1 - c), mate.at[zd], net.partner())
            net.send(swap)
            self.swaps[zd] = swap
            self.loads[zd] = local.start(part(2 * zd + c), own.at[zd])
        self.order = order
        self.base = net.used
        net.used += 2 * (Z - 1)

    def hop(self, side, t):
        net = self.net
        last = net.Z - 1
        if side == 1:
            src, dst, i = self.own.at[last - t], self.from_left.at[t], self.base + t
        else:
            src, dst, i = self.own.at[t], self.from_right.at[t], self.base + last + t
        return pltpu.make_async_remote_copy(
            src_ref=src,
            dst_ref=dst,
            send_sem=net.send_sems.at[i],
            recv_sem=net.recv_sems.at[i],
            device_id=net.line_peer(jnp.clip(net.z + side, 0, last)),
            device_id_type=MESH,
        )

    def pair(self):
        net, done = self.net, set()
        right, left = net.Z - 1, 0
        for zd in self.order:
            self.loads[zd].wait()
            self.swaps[zd].wait_recv()
            add_slabs(self.own.at[zd], self.own.at[zd], self.mate.at[zd])
            done.add(zd)
            while right > 0 and right in done:
                net.send(self.hop(1, net.Z - 1 - right), net.z == 0)
                right -= 1
            while left < net.Z - 1 and left in done:
                net.send(self.hop(-1, left), net.z == net.Z - 1)
                left += 1

    def step(self, n):
        net = self.net
        z, last = net.z, net.Z - 1
        for side, far, buf in ((1, z, self.from_left), (-1, last - z, self.from_right)):
            t = jnp.clip(n - far, 0, last - 1)
            here = (far >= 1) & (far <= n)
            through = here & (n < last)
            place = last - t if side == 1 else t
            hop = self.hop(side, t)
            run(here, hop.wait_recv)
            if n < last:
                held = self.mate.at[0 if side == 1 else 1]
                load = self.local.make(buf.at[t], held)

                def add():
                    load.start()
                    load.wait()
                    add_slabs(self.own.at[place], self.own.at[place], held)

                run(through, add)
                net.send(hop, through)

    def total(self, out):
        net = self.net
        z, Z = net.z, net.Z
        blocks, rows = out.shape[0], out.shape[1]
        per = rows // 16
        left = self.local.make(self.from_left.at[jnp.clip(Z - 1 - z, 0, Z - 2)], self.mate.at[0])
        right = self.local.make(self.from_right.at[jnp.clip(z, 0, Z - 2)], self.mate.at[1])
        run(z > 0, left.start)
        run(z < Z - 1, right.start)
        run(z > 0, left.wait)
        run(z < Z - 1, right.wait)

        def body(use_left, use_right):
            @pl.loop(0, blocks * per)
            def _(i):
                at = (i // per, pl.ds(pl.multiple_of(lax.rem(i, per) * 16, 16), 16), slice(None))
                value = self.own.at[z][at].astype(F32)
                if use_left:
                    value = value + self.mate[(0,) + at].astype(F32)
                if use_right:
                    value = value + self.mate[(1,) + at].astype(F32)
                out[at] = value.astype(out.dtype)

        run(z == 0, lambda: body(False, True))
        run(z == Z - 1, lambda: body(True, False))
        if Z > 2:
            run((z > 0) & (z < Z - 1), lambda: body(True, True))


def first_kernel(seq_n, dp_n, x, gy, up, qkv, out_w, small, x_all, gy_all, up_all, qkv_own, out_all, small_all, send_sems, recv_sems, local_sems, *bufs):
    net = Net(seq_n, dp_n, send_sems, recv_sems)
    local = Local(local_sems)
    s, d = net.s, net.d
    half = x.shape[0] // 2
    rows = lambda h: slice(None) if h is None else pl.ds(h * half, half)
    net.barrier(True)
    smalls = []
    for k in range(1, dp_n):
        copy = net.copy(small, small_all.at[s, d], (s, lax.rem(d + k, dp_n)))
        net.send(copy)
        smalls.append(copy)
    out_line = GatherLine(net, lambda k: out_all.at[k], out_w)
    out_line.early()
    out_line.start()
    up_swap = Exchange(net, lambda k: up.at[k], lambda k: up_all.at[k, d])
    own = [
        (up.at[s], up_all.at[s, d]),
        (small, small_all.at[s, d]),
        (x, x_all.at[s]),
        (gy, gy_all.at[s]),
        (out_w, out_all.at[d]),
        (qkv.at[s], qkv_own.at[s]),
    ]
    mine = local.through([(src, buf, dst) for (src, dst), buf in zip(own, bufs)])
    out_line.step(1)
    up_swap.wait()
    for copy in mine:
        copy.wait()
    up_line = GatherLine(net, lambda k: up_all.at[:, k])
    up_line.early()
    up_line.start()
    x_seq = GatherSeq(net, x, lambda k, h: x_all.at[k, rows(h)])
    for t in range(2, net.Z):
        out_line.step(t)
    for copy in smalls:
        copy.wait_recv()
    small_seq = Exchange(net, lambda k: small_all.at[s], lambda k: small_all.at[k])
    up_line.step(1)
    x_seq.relay()
    gy_seq = GatherSeq(net, gy, lambda k, h: gy_all.at[k, rows(h)])
    for t in range(2, net.Z):
        up_line.step(t)
    gy_seq.relay()
    qkv_swap = Exchange(net, lambda k: qkv.at[k], lambda k: qkv_own.at[k])
    small_seq.wait()
    x_seq.wait()
    out_line.wait()
    up_line.wait()
    gy_seq.wait()
    qkv_swap.wait()
    net.drain()


ANY = pl.BlockSpec(memory_space=pl.ANY)
MIB = 1024 * 1024
shape = jax.ShapeDtypeStruct


def gather_first(seq_n, dp_n, x, gy, up, qkv, out_w, small):
    n = 4 * seq_n + 2 * dp_n + 8 * dp_n + 16
    return pl.pallas_call(
        functools.partial(first_kernel, seq_n, dp_n),
        out_shape=(
            shape((seq_n,) + x.shape, BF),
            shape((seq_n,) + x.shape, BF),
            shape((seq_n, dp_n) + up.shape[1:], BF),
            shape(qkv.shape, BF),
            shape((dp_n,) + out_w.shape, BF),
            shape((seq_n, dp_n) + small.shape, BF),
        ),
        in_specs=[ANY] * 6,
        out_specs=[ANY] * 6,
        scratch_shapes=[pltpu.SemaphoreType.DMA((n,)), pltpu.SemaphoreType.DMA((n,)), pltpu.SemaphoreType.DMA((16,))]
        + [pltpu.VMEM(v, BF) for v in (up.shape[1:], small.shape, x.shape, gy.shape, out_w.shape, qkv.shape[1:])],
        compiler_params=pltpu.CompilerParams(collective_id=0, has_side_effects=True, vmem_limit_bytes=32 * MIB),
        name="gather_first",
    )(x, gy, up, qkv, out_w, small)


def nt(left, right):
    return lax.dot_general(left, right, (((1,), (1,)), ((), ())), preferred_element_type=F32)


def tn(left, right):
    return lax.dot_general(left, right, (((0,), (0,)), ((), ())), preferred_element_type=F32)


def turn(value, cosine, ahead, behind):
    half = 32
    return value * cosine + pltpu.roll(value, 128 - half, 1) * ahead + pltpu.roll(value, half, 1) * behind


def stream(body, grid, ins, outs):
    def spec(entry):
        ref, block, index = entry[:3]
        mode = pl.Buffered(1) if len(entry) > 3 else None
        return pl.BlockSpec(block, index, pipeline_mode=mode) if mode else pl.BlockSpec(block, index)

    pltpu.emit_pipeline(
        body, grid=grid, in_specs=[spec(e) for e in ins], out_specs=[spec(e) for e in outs]
    )(*[e[0] for e in ins], *[e[0] for e in outs])


INS = ["n1", "n2", "x", "gy", "up_all", "out_all", "qkv_own", "down_w", "up_b", "qkv_b", "out_b", "gains", "mean", "inv"]
INS += ["tables", "doc_row", "doc_col", "own_rows"]
OUTS = ["mixed_out", "input_grad", "up_out", "qkv_out", "out_red", "down_red", "small_red"]
TEMPS = ["qkv_all", "down_all", "hidden", "slope", "grad_up", "heads", "gatt", "att", "gproj", "wide_f", "mixed", "wide"]
TEMPS += ["p_up", "p_qkv", "p_out", "p_down", "up_red", "qkv_red", "mixed_in", "wide_in"]


ORDER = ["q.early", "q.start", "UP", "q.s1", "d.early", "DG", "ds.start", "q.s2", "d.start", "GATT", "ds.pair", "q.s3"]
ORDER += ["q.wait", "QKV", "d.s1", "ATT", "QG", "qs.start", "d.s2", "qs.pair", "ds.s1", "d.s3", "d.wait", "SLOPE", "UG"]
ORDER += ["us.start", "qs.s1", "MIX", "qs.s2", "mx.start", "us.pair", "ONE", "ds.s2", "qs.s3", "qs.tot", "qx.start", "TWO"]
ORDER += ["sm.first", "wx.start", "us.s1", "us.s2", "mx.wait", "MEND", "OG", "os.start", "sm.start", "qx.wait", "WQ"]
ORDER += ["os.pair", "os.s1", "us.s3", "us.tot", "ux.start", "os.s2", "ds.s3", "wx.wait", "IEND", "ds.tot", "os.s3"]
ORDER += ["os.tot", "sm.wait", "ux.wait", "WU"]


def layer_kernel(seq_n, dp_n, dims, *refs):
    names = INS + OUTS + TEMPS
    g = dict(zip(names, refs[: len(names)]))
    refs = refs[len(names) :]
    hops, refs = refs[:8], refs[8:]
    send_sems, recv_sems, local_sems, sm, sm_dp, sm_sum, dk_acc, dv_acc, up_f, qkv_f, out_f, down_f = refs[:12]
    halves = refs[12:]
    L, D, ff, H, r, ro, rd = dims
    hd, T, CH = 256, 256, 512
    l = H * hd
    net = Net(seq_n, dp_n, send_sems, recv_sems)
    local = Local(local_sems)
    S, Z, s, d = net.S, net.Z, net.s, net.d
    tok = L // S
    scale = 1.0 / math.sqrt(hd)
    const = lambda *nd: (lambda *i: (0,) * nd[0])

    def whole(ref):
        return (ref, ref.shape, const(len(ref.shape)), 1)

    per = dp_n * r // T
    d_rows = lambda ref: (ref, (1, T // r, r, ref.shape[3]), lambda i: (lax.div(i, per), lax.rem(i, per), 0, 0))
    lanes = lambda ref: (ref, (ref.shape[0], T), lambda i: (0, i))

    def line(i, part):
        return ReduceLine(net, part, halves[2 * i], halves[2 * i + 1], hops[2 * i], hops[2 * i + 1], local)

    def up_phase():
        def body(n2, w, b, hidden, slope):
            wv = w[...].reshape(D, T)

            @pl.loop(0, L // CH)
            def _(i):
                at = pl.ds(pl.multiple_of(i * CH, CH), CH)
                u = dot(n2[at, :], wv) + b[...]
                phi = 0.5 + 0.5 * lax.erf(u * math.sqrt(0.5))
                hidden[at, :] = (u * phi).astype(BF)
                slope[at, :] = (phi + u * (jnp.exp(-0.5 * u * u) * (1.0 / math.sqrt(2.0 * math.pi)))).astype(BF)

        stream(
            body,
            (ff // T,),
            [whole(g["n2"]), (g["up_all"], (S, dp_n, r, T), lambda i: (0, 0, 0, i)), lanes(g["up_b"])],
            [lanes(g["hidden"]), lanes(g["slope"])],
        )

    def outer_phase(left, right, out, block_rows, n):
        def body(a, b, o):
            width = o.shape[-1]
            step = min(width, 1024)

            @pl.loop(0, width // step)
            def _(j):
                at = pl.ds(pl.multiple_of(j * step, step), step)
                o[(slice(None),) * (len(o.shape) - 1) + (at,)] = tn(a[...], b[:, at]).astype(BF).reshape(o.shape[:-1] + (step,))

        stream(
            body,
            (n,),
            [lanes(left), whole(right)],
            [(out, (T // block_rows, block_rows, D), lambda i: (i, 0, 0)) if len(out.shape) == 3 else d_rows(out)],
        )

    def qkv_grad_phase():
        def body(a, b, o):
            for j in range(3):
                o[:, :, :, j * l : (j + 1) * l] = tn(a[...], b[j]).astype(BF).reshape(o.shape[:-1] + (l,))

            @pl.when(pl.program_id(0) == 0)
            def _():
                for j in range(3):
                    sm[6:7, j * l : (j + 1) * l] = jnp.sum(b[j].astype(F32), 0, keepdims=True)

        stream(body, (D // T,), [lanes(g["n1"]), whole(g["gproj"])], [d_rows(g["p_qkv"])])

    def gatt_phase():
        def body(gy, w, o):
            o[0] = nt(gy[...], w[...].reshape(T, D)).astype(BF)

        stream(
            body,
            (H,),
            [whole(g["gy"]), (g["out_all"], (T // ro, ro, D), lambda i: (i, 0, 0))],
            [(g["gatt"], (1, L, hd), lambda i: (i, 0, 0))],
        )

    def qkv_phase():
        def body(n1, w, b, tab, o):
            j = pl.program_id(0)
            wv = w[...].reshape(D, T)

            @pl.loop(0, L // CH)
            def _(i):
                at = pl.ds(pl.multiple_of(i * CH, CH), CH)
                p = dot(n1[at, :], wv) + b[...]
                o[0, at, 128:] = p[:, 128:].astype(BF)

                @pl.when(j < 2 * H)
                def _():
                    o[0, at, :128] = turn(p[:, :128], tab[0, at, :], tab[1, at, :], tab[2, at, :]).astype(BF)

                @pl.when(j >= 2 * H)
                def _():
                    o[0, at, :128] = p[:, :128].astype(BF)

        stream(
            body,
            (3 * H,),
            [whole(g["n1"]), (g["qkv_all"], (S, dp_n, r, T), lambda i: (0, 0, 0, i)), lanes(g["qkv_b"]), whole(g["tables"])],
            [(g["heads"], (1, L, hd), lambda i: (i, 0, 0))],
        )

    def att_phase():
        def body(q, k, v, ga, tab, drow, dcol, att, dq, dk, dv):
            i = pl.program_id(1)
            qt, kt, vt, gt = q[0], k[0], v[0], ga[0]
            raw = nt(qt, kt) * scale
            at = pl.ds(pl.multiple_of(i * T, T), T)
            query = lax.broadcasted_iota(jnp.int32, (T, L), 0) + i * T
            key = lax.broadcasted_iota(jnp.int32, (T, L), 1)
            allowed = (dcol[at, :] == drow[...]) & (key <= query)
            raw = jnp.where(allowed, raw, -1000000000.0)
            e = jnp.exp(raw - jnp.max(raw, -1, keepdims=True))
            p = e / jnp.sum(e, -1, keepdims=True)
            pb = p.astype(BF)
            att[...] = dot(pb, vt).astype(BF)
            gp = nt(gt, vt)
            ds = (p * (gp - jnp.sum(gp * p, -1, keepdims=True))).astype(BF)
            gq = dot(ds, kt) * scale
            back = lambda t, rows: turn(t, tab[0, rows, :], -tab[1, rows, :], -tab[2, rows, :])
            dq[0, :, :128] = back(gq[:, :128], at).astype(BF)
            dq[0, :, 128:] = gq[:, 128:].astype(BF)

            @pl.when(i == 0)
            def _():
                dk_acc[...] = jnp.zeros_like(dk_acc)
                dv_acc[...] = jnp.zeros_like(dv_acc)

            dk_acc[...] += tn(ds, qt)
            dv_acc[...] += tn(pb, gt)

            @pl.when(i == L // T - 1)
            def _():
                gk = dk_acc[...] * scale
                dk[0, :, :128] = back(gk[:, :128], slice(None)).astype(BF)
                dk[0, :, 128:] = gk[:, 128:].astype(BF)
                dv[0] = dv_acc[...].astype(BF)

        hv, gp = g["heads"], g["gproj"]
        stream(
            body,
            (H, L // T),
            [
                (hv, (1, T, hd), lambda h, i: (h, i, 0)),
                (hv, (1, L, hd), lambda h, i: (H + h, 0, 0)),
                (hv, (1, L, hd), lambda h, i: (2 * H + h, 0, 0)),
                (g["gatt"], (1, T, hd), lambda h, i: (h, i, 0)),
                whole(g["tables"]),
                whole(g["doc_row"]),
                whole(g["doc_col"]),
            ],
            [
                (g["att"], (T, hd), lambda h, i: (i, h)),
                (gp.at[pl.ds(0, 1)], (1, T, hd), lambda h, i: (0, i, h)),
                (gp.at[pl.ds(1, 1)], (1, L, hd), lambda h, i: (0, 0, h)),
                (gp.at[pl.ds(2, 1)], (1, L, hd), lambda h, i: (0, 0, h)),
            ],
        )

    def norm_sums(grad, x, mean, inv, row, i):
        hat = (x.astype(F32) - mean) * inv
        at = pl.ds(pl.multiple_of(i * T, T), T)
        sm[row : row + 1, at] += jnp.sum(grad * hat, 0, keepdims=True)
        sm[row + 1 : row + 2, at] += jnp.sum(grad, 0, keepdims=True)

    def one_phase():
        def body(gp, w, x, mean, inv, gain, wide):
            i = pl.program_id(0)
            wv = w[...].reshape(T, 3 * l)

            @pl.loop(0, L // CH)
            def _(m):
                at = pl.ds(pl.multiple_of(m * CH, CH), CH)
                grad = nt(gp[0, at, :], wv[:, :l]) + nt(gp[1, at, :], wv[:, l : 2 * l]) + nt(gp[2, at, :], wv[:, 2 * l :])
                norm_sums(grad, x[at, :], mean[at, :], inv[at, :], 0, i)
                wide[at, :] = grad * gain[0:1, :]

        stream(
            body,
            (D // T,),
            [whole(g["gproj"]), d_rows(g["qkv_all"]), lanes(g["x"]), whole(g["mean"]), whole(g["inv"]), lanes(g["gains"])],
            [lanes(g["wide_f"])],
        )

    def two_phase():
        def body(gu, w, x, mean, inv, gain, first, wide):
            i = pl.program_id(0)
            wv = w[...].reshape(T, ff)

            @pl.loop(0, L // tok)
            def _(m):
                at = pl.ds(pl.multiple_of(m * tok, tok), tok)
                grad = nt(gu[at, :], wv)
                norm_sums(grad, x[at, :], mean[at, :], inv[at, :], 2, i)
                wide[m] = (first[at, :] + grad * gain[1:2, :]).astype(BF)

        stream(
            body,
            (D // T,),
            [whole(g["grad_up"]), d_rows(g["up_all"]), lanes(g["x"]), whole(g["mean"]), whole(g["inv"]), lanes(g["gains"]), lanes(g["wide_f"])],
            [(g["wide"], (S, tok, T), lambda i: (0, 0, i))],
        )

    def mixed_phase():
        def body(hidden, w, att, wo, o):
            wv, wov = w[...].reshape(ff, T), wo[...].reshape(l, T)

            @pl.loop(0, L // tok)
            def _(m):
                at = pl.ds(pl.multiple_of(m * tok, tok), tok)
                o[m] = (dot(hidden[at, :], wv) + dot(att[at, :], wov)).astype(BF)

        stream(
            body,
            (D // T,),
            [
                whole(g["hidden"]),
                (g["down_all"], (dp_n, rd, T), lambda i: (0, 0, i)),
                whole(g["att"]),
                (g["out_all"], (dp_n, ro, T), lambda i: (0, 0, i)),
            ],
            [(g["mixed"], (S, tok, T), lambda i: (0, 0, i))],
        )

    def slope_phase():
        def body(gy, w, slope, o):
            i = pl.program_id(0)
            wv = w[...].reshape(T, D)
            cols = pl.ds(pl.multiple_of(i * T, T), T)

            @pl.loop(0, L // CH)
            def _(m):
                at = pl.ds(pl.multiple_of(m * CH, CH), CH)
                gu = (nt(gy[at, :], wv) * slope[at, :].astype(F32)).astype(BF)
                o[at, :] = gu
                sm[5:6, cols] += jnp.sum(gu.astype(F32), 0, keepdims=True)

        stream(
            body,
            (ff // T,),
            [whole(g["gy"]), (g["down_all"], (T // rd, rd, D), lambda i: (i, 0, 0)), lanes(g["slope"])],
            [lanes(g["grad_up"])],
        )

    def mixed_end():
        def body(x, b, own, came, o):
            total = x[...].astype(F32) + b[...] + own[0].astype(F32)
            for k in range(S - 1):
                total = total + came[k].astype(F32)
            o[0] = total.astype(BF)

        part = min(128, tok)
        rows = lambda ref: (ref, (part, D), lambda i: (i, 0))
        stream(
            body,
            (tok // part,),
            [
                rows(g["x"].at[pl.ds(pl.multiple_of(s * tok, tok), tok)]),
                whole(g["out_b"]),
                (g["mixed"].at[pl.ds(s, 1)], (1, part, D), lambda i: (0, i, 0)),
                (g["mixed_in"], (S - 1, part, D), lambda i: (0, i, 0)),
            ],
            [(g["mixed_out"], (1, part, D), lambda i: (0, i, 0))],
        )

    def input_end():
        def body(x, gy, mean, inv, own, came, o):
            hat = (x[...].astype(F32) - mean[...]) * inv[...]
            total = own[0].astype(F32)
            for k in range(S - 1):
                total = total + came[k].astype(F32)
            total = total - jnp.mean(total, -1, keepdims=True) - hat * jnp.mean(total * hat, -1, keepdims=True)
            o[0] = gy[...].astype(F32) + inv[...] * total

        part = min(128, tok)
        mine_rows = lambda ref: ref.at[pl.ds(pl.multiple_of(s * tok, tok), tok)]
        rows = lambda ref: (mine_rows(ref), (part, ref.shape[1]), lambda i: (i, 0))
        stream(
            body,
            (tok // part,),
            [
                rows(g["x"]),
                rows(g["gy"]),
                rows(g["mean"]),
                rows(g["inv"]),
                (g["wide"].at[pl.ds(s, 1)], (1, part, D), lambda i: (0, i, 0)),
                (g["wide_in"], (S - 1, part, D), lambda i: (0, i, 0)),
            ],
            [(g["input_grad"], (1, part, D), lambda i: (0, i, 0))],
        )

    def widen(ref, out, parts):
        def body(a, o):
            o[...] = a[0].astype(F32)

        w = ref.shape[2] // parts
        stream(
            body,
            (S, parts),
            [(ref, (1, r, w), lambda k, j: (k, 0, j))],
            [(out, (r, w), lambda k, j: (0, j * S + k))],
        )

    acts, made = {}, {}

    def steps(name, obj, extra):
        middle = {"s1": [1], "s2": list(range(2, Z - 1)), "s3": [Z - 1]}
        for key, ts in middle.items():
            acts[name + "." + key] = lambda ts=ts: [made[name].step(t) for t in ts]
        for key in extra:
            acts[name + "." + key] = lambda key=key: getattr(made[name], key)()

    def gather(name, slab, own):
        made[name] = GatherLine(net, slab, own)
        steps(name, made[name], ["early", "start", "wait"])

    def reduce(name, i, part, total):
        def start():
            made[name] = line(i, part)

        steps(name, None, ["pair"])
        acts[name + ".start"] = start
        acts[name + ".tot"] = lambda: made[name].total(total)

    def exchange(name, src, slot, by_turn=False):
        def start():
            made[name] = Exchange(net, src, slot, by_turn)

        acts[name + ".start"] = start
        acts[name + ".wait"] = lambda: made[name].wait()

    def also(name, before=None, after=None):
        act = acts[name]

        def both():
            if before:
                before()
            act()
            if after:
                after()

        acts[name] = both

    def keep(name, src, dst):
        made[name] = local.start(src, dst)

    gather("q", lambda k: g["qkv_all"].at[:, k], g["qkv_own"])
    gather("d", lambda k: g["down_all"].at[k], g["down_w"])
    reduce("ds", 0, lambda k: g["p_down"].at[pl.ds(k, 1)], down_f)
    reduce("qs", 1, lambda k: g["p_qkv"].at[:, k], qkv_f)
    reduce("os", 2, lambda k: g["p_out"].at[pl.ds(k, 1)], out_f)
    reduce("us", 3, lambda k: g["p_up"].at[:, k], up_f)
    also("ds.tot", after=lambda: keep("ds.out", down_f, g["down_red"]))
    also("os.tot", after=lambda: keep("os.out", out_f, g["out_red"]))
    exchange("mx", lambda k: g["mixed"].at[k], lambda k: g["mixed_in"].at[k], True)
    exchange("wx", lambda k: g["wide"].at[k], lambda k: g["wide_in"].at[k], True)
    exchange("qx", lambda k: qkv_f.at[k], lambda k: g["qkv_red"].at[k])
    exchange("ux", lambda k: up_f.at[k], lambda k: g["up_red"].at[k])
    exchange("sm", lambda k: sm_sum, lambda k: g["small_red"].at[k])
    for x, buf, red in (("qx", qkv_f, "qkv_red"), ("ux", up_f, "up_red")):
        also(x + ".start", after=lambda x=x, buf=buf, red=red: keep(x + ".own", buf.at[s], g[red].at[s]))
        also(x + ".wait", after=lambda x=x: made[x + ".own"].wait())

    def small_first():
        made["sums"] = []
        for k in range(1, dp_n):
            copy = net.copy(sm, sm_dp.at[d], (s, lax.rem(d + k, dp_n)))
            net.send(copy)
            made["sums"].append((copy, lax.rem(d + dp_n - k, dp_n)))

    def small_second():
        sm_sum[...] = sm[...]
        for copy, source in made["sums"]:
            copy.wait_recv()
            sm_sum[...] += sm_dp[source]

    also("sm.start", small_second, lambda: keep("sm.own", sm_sum, g["small_red"].at[s]))
    acts["sm.first"] = small_first
    acts["UP"] = up_phase
    acts["DG"] = lambda: outer_phase(g["hidden"], g["gy"], g["p_down"], rd, ff // T)
    acts["GATT"] = gatt_phase
    acts["QKV"] = qkv_phase
    acts["ATT"] = att_phase
    acts["QG"] = qkv_grad_phase
    acts["OG"] = lambda: outer_phase(g["att"], g["gy"], g["p_out"], ro, H)
    acts["SLOPE"] = slope_phase
    acts["UG"] = lambda: outer_phase(g["n2"], g["grad_up"], g["p_up"], r, D // T)
    acts["ONE"], acts["TWO"], acts["MIX"] = one_phase, two_phase, mixed_phase
    acts["MEND"], acts["IEND"] = mixed_end, input_end
    acts["WQ"] = lambda: widen(g["qkv_red"], g["qkv_out"], 3)
    acts["WU"] = lambda: widen(g["up_red"], g["up_out"], 1)

    net.barrier(True)
    loads = [(g["qkv_own"], qkv_f, g["qkv_all"].at[:, d]), (g["down_w"], halves[0].at[0, 0], g["down_all"].at[d])]
    placed = local.through(loads)
    sm[...] = jnp.zeros_like(sm)
    sm[4:5, :] = g["own_rows"][...]
    for name in ORDER:
        acts[name]()
        if name == "UP":
            for copy in placed:
                copy.wait()
    for name in ("ds.out", "os.out", "sm.own"):
        made[name].wait()
    net.drain()


def layer(seq_n, dp_n, dims, args):
    L, D, ff, H, r, ro, rd = dims
    l, Z = H * 256, dp_n // 2
    tok = L // seq_n
    outs = {
        "up_red": ((seq_n, r, ff), BF),
        "qkv_red": ((seq_n, r, 3 * l), BF),
        "out_red": ((1, ro, D), F32),
        "down_red": ((1, rd, D), F32),
        "mixed_in": ((seq_n - 1, tok, D), BF),
        "wide_in": ((seq_n - 1, tok, D), BF),
        "mixed_out": ((1, tok, D), BF),
        "input_grad": ((1, tok, D), F32),
        "up_out": ((r, seq_n * ff), F32),
        "qkv_out": ((r, seq_n * 3 * l), F32),
        "small_red": ((seq_n, 8, D), F32),
        "qkv_all": ((seq_n, dp_n, r, 3 * l), BF),
        "down_all": ((dp_n, rd, D), BF),
        "hidden": ((L, ff), BF),
        "slope": ((L, ff), BF),
        "grad_up": ((L, ff), BF),
        "heads": ((3 * H, L, 256), BF),
        "gatt": ((H, L, 256), BF),
        "att": ((L, l), BF),
        "gproj": ((3, L, l), BF),
        "wide_f": ((L, D), F32),
        "mixed": ((seq_n, tok, D), BF),
        "wide": ((seq_n, tok, D), BF),
        "p_up": ((seq_n, dp_n, r, ff), BF),
        "p_qkv": ((seq_n, dp_n, r, 3 * l), BF),
        "p_out": ((dp_n, ro, D), BF),
        "p_down": ((dp_n, rd, D), BF),
    }
    slabs = [(1, rd, D), (seq_n, r, 3 * l), (1, ro, D), (seq_n, r, ff)]
    out_shape = [shape(*outs[name]) for name in OUTS + TEMPS]
    for slab in slabs:
        out_shape += [shape((Z - 1,) + slab, BF)] * 2
    n = 16 * seq_n + 4 * dp_n + 4 * 8 * dp_n
    size = max(math.prod(slab) for slab in slabs)
    scratch = [
        pltpu.SemaphoreType.DMA((n,)),
        pltpu.SemaphoreType.DMA((n,)),
        pltpu.SemaphoreType.DMA((16 * dp_n,)),
        pltpu.VMEM((8, D), F32),
        pltpu.VMEM((dp_n, 8, D), F32),
        pltpu.VMEM((8, D), F32),
        pltpu.VMEM((L, 256), F32),
        pltpu.VMEM((L, 256), F32),
        pltpu.VMEM(slabs[3], BF),
        pltpu.VMEM(slabs[1], BF),
        pltpu.VMEM(slabs[2], F32),
        pltpu.VMEM(slabs[0], F32),
    ]
    for slab in slabs:
        scratch += [pltpu.VMEM((Z,) + slab, BF)] * 2
    result = pl.pallas_call(
        functools.partial(layer_kernel, seq_n, dp_n, dims),
        out_shape=out_shape,
        in_specs=[ANY if name != "own_rows" else pl.BlockSpec(memory_space=pltpu.VMEM) for name in INS],
        out_specs=[ANY] * len(out_shape),
        scratch_shapes=scratch,
        compiler_params=pltpu.CompilerParams(collective_id=1, has_side_effects=True, vmem_limit_bytes=62 * MIB),
        name="layer",
    )(*[args[name] for name in INS])
    return dict(zip(OUTS, result))


def shards(
    tokens,
    doc_ids,
    ln1_gain,
    ln1_bias,
    ln2_gain,
    ln2_bias,
    qkv_weight,
    qkv_bias,
    out_weight,
    up_weight,
    up_bias,
    down_weight,
    out_bias,
    cotangent,
):
    seq_n = lax.axis_size("seq")
    dp_n = lax.axis_size("dp")
    seq_i = lax.axis_index("seq")
    tok_rows, width = tokens.shape[1:]
    length = tok_rows * seq_n
    head_dim = width // HEADS
    heads = HEADS // seq_n
    local = heads * head_dim
    ff = up_weight.shape[1] // seq_n
    rot_dims = head_dim // 4
    scale = 1.0 / math.sqrt(head_dim)

    rows = qkv_weight.shape[0]
    qkv_cut = qkv_weight.reshape(rows, 3, seq_n, local).transpose(2, 0, 1, 3).reshape(seq_n, rows, 3 * local)
    up_cut = up_weight.reshape(rows, seq_n, ff).transpose(1, 0, 2)
    small = jnp.concatenate(
        [ln1_gain, ln1_bias, ln2_gain, ln2_bias, out_bias, qkv_bias, up_bias, doc_ids[0].astype(BF)]
    )
    own_small = small.shape[0]
    tall = -(-own_small // (16 * 128)) * 16
    small = jnp.pad(small, (0, tall * 128 - own_small)).reshape(tall, 128)
    x_row, gy, up_all, qkv_own, out_all, small = gather_first(
        seq_n, dp_n, tokens[0], cotangent[0], up_cut, qkv_cut, out_weight, small
    )
    x_row, gy = x_row.reshape(length, width), gy.reshape(length, width)
    small = small.reshape(seq_n, dp_n, -1)
    docs = small[:, :, own_small - tok_rows : own_small]
    docs = lax.dynamic_index_in_dim(docs, lax.axis_index("dp"), 1, False).reshape(-1).astype(F32)
    small = small.reshape(seq_n * dp_n, -1).astype(F32)
    cuts, at = [], 0
    for v in (ln1_gain, ln1_bias, ln2_gain, ln2_bias, out_bias, qkv_bias, up_bias):
        cuts.append(small[:, at : at + v.shape[0]].reshape(-1))
        at += v.shape[0]
    gain_one, shift_one, gain_two, shift_two, out_shift, qkv_shift, up_shift = cuts
    qkv_shift = lax.dynamic_index_in_dim(qkv_shift.reshape(3, seq_n, local), seq_i, 1, False).reshape(1, -1)
    up_shift = lax.dynamic_slice_in_dim(up_shift, seq_i * ff, ff)[None]

    inputs = x_row.astype(F32)
    mean = jnp.mean(inputs, -1, keepdims=True)
    center = inputs - mean
    inv = lax.rsqrt(jnp.mean(center * center, -1, keepdims=True) + epsilon)
    xhat = center * inv
    cosine, sine = rotary_tables(jnp.arange(length, dtype=jnp.int32), rot_dims)
    half, none = rot_dims // 2, jnp.zeros((length, 128 - rot_dims), F32)
    zero = jnp.zeros((length, half), F32)
    tables = jnp.stack(
        [
            jnp.concatenate([cosine, cosine, none + 1.0], 1),
            jnp.concatenate([-sine, zero, none], 1),
            jnp.concatenate([zero, sine, none], 1),
        ]
    )
    got = layer(
        seq_n,
        dp_n,
        (length, width, ff, heads, rows, out_weight.shape[0], down_weight.shape[0]),
        {
            "n1": (xhat * gain_one + shift_one).astype(BF),
            "n2": (xhat * gain_two + shift_two).astype(BF),
            "x": x_row,
            "gy": gy,
            "up_all": up_all,
            "out_all": out_all,
            "qkv_own": qkv_own,
            "down_w": down_weight,
            "up_b": up_shift,
            "qkv_b": qkv_shift,
            "out_b": out_shift[None],
            "gains": jnp.stack([gain_one, gain_two]),
            "mean": mean,
            "inv": inv,
            "tables": tables,
            "doc_row": docs[None],
            "doc_col": docs[:, None],
            "own_rows": jnp.sum(cotangent[0].astype(F32), 0, keepdims=True),
        },
    )
    sums = got["small_red"]
    n = seq_n * dp_n
    place = seq_i * dp_n + lax.axis_index("dp")

    def mine(vector):
        return lax.dynamic_index_in_dim(vector.reshape(n, -1), place, 0, False)

    lns = jnp.sum(sums[:, :5], 0)
    g1, b1, g2, b2, ob = [mine(lns[k]) for k in range(5)]
    ub = mine(sums[:, 5, :ff])
    qb = mine(sums[:, 6, : 3 * local].reshape(seq_n, 3, local).transpose(1, 0, 2))
    return (
        got["mixed_out"],
        got["input_grad"],
        g1,
        b1,
        g2,
        b2,
        got["qkv_out"],
        qb,
        got["out_red"][0],
        got["up_out"],
        ub,
        got["down_red"][0],
        ob,
    )


def solution(mesh):
    in_specs = (
        P("dp", "seq", None),
        P("dp", "seq"),
        P(("seq", "dp")),
        P(("seq", "dp")),
        P(("seq", "dp")),
        P(("seq", "dp")),
        P(("seq", "dp"), None),
        P(("seq", "dp")),
        P(("seq", "dp"), None),
        P(("seq", "dp"), None),
        P(("seq", "dp")),
        P(("seq", "dp"), None),
        P(("seq", "dp")),
        P("dp", "seq", None),
    )
    out_specs = (
        P("dp", "seq", None),
        P("dp", "seq", None),
        P(("seq", "dp")),
        P(("seq", "dp")),
        P(("seq", "dp")),
        P(("seq", "dp")),
        P(("seq", "dp"), None),
        P(("seq", "dp")),
        P(("seq", "dp"), None),
        P(("seq", "dp"), None),
        P(("seq", "dp")),
        P(("seq", "dp"), None),
        P(("seq", "dp")),
    )
    return jax.shard_map(shards, mesh=mesh, in_specs=in_specs, out_specs=out_specs, check_vma=False)
```

```python
import functools
import math

import jax
import jax.numpy as jnp
import numpy as np
from jax import lax
from jax.experimental import pallas as pl
from jax.experimental.pallas import tpu as pltpu
from jax.sharding import PartitionSpec as P

HEADS = 8
BF = jnp.bfloat16
F32 = jnp.float32


epsilon = 1e-05


def rotary_rows(length, rot_dims):
    half = rot_dims // 2
    exponents = np.arange(half, dtype=np.float32) * np.float32(2.0 / rot_dims)
    inverse = np.power(np.float32(10000.0), -exponents).astype(np.float32)
    phase = (np.arange(length, dtype=np.float32)[:, None] * inverse[None, :]).astype(np.float64)
    tables = np.zeros((3, length, 128), np.float32)
    tables[0] = 1.0
    tables[0, :, :half] = tables[0, :, half:rot_dims] = np.cos(phase)
    tables[1, :, :half] = -np.sin(phase)
    tables[2, :, half:rot_dims] = np.sin(phase)
    return tables


def dot(left, right):
    return jnp.dot(left, right, preferred_element_type=F32)


MESH = pl.DeviceIdType.MESH


def run(when, action):
    if when is None:
        action()
    else:
        pl.when(when)(lambda: action())


class Net:
    def __init__(self, seq_n, dp_n, send_sems, recv_sems, local_sems):
        self.S, self.DP, self.Z = seq_n, dp_n, dp_n // 2
        self.s, self.d = lax.axis_index("seq"), lax.axis_index("dp")
        self.z, self.c = self.d // 2, lax.rem(self.d, 2)
        self.send_sems, self.recv_sems, self.used = send_sems, recv_sems, 0
        self.local_sems, self.local_used = local_sems, 0
        self.sent = []

    def seq_peer(self, s):
        return (s, self.d)

    def line_peer(self, z):
        return (self.s, 2 * jnp.clip(z, 0, self.Z - 1) + self.c)

    def partner(self):
        return (self.s, 2 * self.z + 1 - self.c)

    def copy(self, src, dst, device):
        self.used += 1
        return self.copy_at(self.used - 1, src, dst, device)

    def copy_at(self, i, src, dst, device):
        return pltpu.make_async_remote_copy(
            src_ref=src,
            dst_ref=dst,
            send_sem=self.send_sems.at[i],
            recv_sem=self.recv_sems.at[i],
            device_id=device,
            device_id_type=MESH,
        )

    def send(self, copy, when=None):
        self.sent.append((copy, when))
        run(when, copy.start)

    def drain(self):
        for copy, when in self.sent:
            run(when, copy.wait_send)

    def near(self, src, dst):
        self.local_used += 1
        return pltpu.make_async_copy(src, dst, self.local_sems.at[self.local_used - 1])

    def barrier(self):
        sem = pltpu.get_barrier_semaphore()
        peers = [self.seq_peer(lax.rem(self.s + k, self.S)) for k in range(1, self.S)]
        peers += [(self.s, lax.rem(self.d + k, self.DP)) for k in range(1, self.DP)]
        for device in peers:
            pl.semaphore_signal(sem, inc=1, device_id=device, device_id_type=MESH)
        pl.semaphore_wait(sem, len(peers))


class Bounce:
    def __init__(self, net, triples):
        self.loads = [net.near(src, buf) for src, buf, _ in triples]
        self.stores = [net.near(buf, dst) for _, buf, dst in triples]

    def start(self):
        for copy in self.loads:
            copy.start()

    def finish(self):
        for load, store in zip(self.loads, self.stores):
            load.wait()
            store.start()
        for store in self.stores:
            store.wait()


class Exchange:
    def __init__(self, net, src, slot, by_turn=False, own=False):
        self.net, self.copies = net, []
        for k in range(1, net.S):
            to = lax.rem(net.s + k, net.S)
            self.copies.append(net.copy(src(to), slot(k - 1 if by_turn else net.s), net.seq_peer(to)))
        self.own = net.near(src(net.s), slot(net.s)) if own else None

    def start(self):
        for copy in self.copies:
            self.net.send(copy)
        if self.own is not None:
            self.own.start()

    def wait(self):
        for copy in self.copies:
            copy.wait_recv()
        if self.own is not None:
            self.own.wait()


class GatherSeq:
    def __init__(self, net, src, slot):
        self.net, self.square = net, net.S == 4
        if self.square:
            s = net.s
            a, b = s + 1 - 2 * lax.rem(s, 2), lax.rem(s + 2, 4)
            self.first = [net.copy(src, slot(s, None), net.seq_peer(p)) for p in (a, b)]
            self.second = [
                net.copy(slot(a, 0), slot(a, 0), net.seq_peer(b)),
                net.copy(slot(b, 1), slot(b, 1), net.seq_peer(a)),
            ]
        else:
            self.direct = Exchange(net, lambda to: src, lambda k: slot(k, None))

    def start(self):
        if self.square:
            for copy in self.first:
                self.net.send(copy)
        else:
            self.direct.start()

    def relay(self):
        if self.square:
            for came, onward in zip(self.first, self.second):
                came.wait_recv()
                self.net.send(onward)

    def wait(self):
        if self.square:
            for copy in self.second:
                copy.wait_recv()
        else:
            self.direct.wait()


class Line:
    def go(self, part):
        last = self.net.Z - 1
        for t in ([1], range(2, last), [last])[part - 1]:
            self.step(t)


class GatherLine(Line):
    def __init__(self, net, slab, own=None):
        self.net = net
        z, c, last = net.z, net.c, net.Z - 1
        own = slab(net.d) if own is None else own
        self.right, self.left = [], []
        for t in range(net.Z):
            for side, hops in ((1, self.right), (-1, self.left)):
                place = slab(2 * jnp.clip(z - side * t, 0, last) + c)
                src = own if t == 0 else place
                there = z >= t if side == 1 else z <= last - t
                onward = z < last if side == 1 else z > 0
                copy = None if t == last else net.copy(src, place, net.line_peer(z + side))
                core = None if t == 0 and side == -1 else net.copy(src, place, net.partner())
                hops.append((copy, there & onward, core, None if t == 0 else there))

    def early(self):
        self.net.send(self.right[0][0], self.net.z == 0)
        self.net.send(self.left[0][0], self.net.z == self.net.Z - 1)

    def start(self):
        inside = (self.net.z > 0) & (self.net.z < self.net.Z - 1)
        self.net.send(self.right[0][0], inside)
        self.net.send(self.left[0][0], inside)
        self.net.send(self.right[0][2])

    def step(self, t):
        for hops in (self.right, self.left):
            copy, sends, core, there = hops[t]
            run(there, hops[t - 1][0].wait_recv)
            if copy is not None:
                self.net.send(copy, sends)
            self.net.send(core, there)

    def wait(self):
        for hops in (self.right, self.left):
            for _, _, core, there in hops:
                if core is not None:
                    run(there, core.wait_recv)


def add_slabs(dst, left, right):
    blocks, rows = dst.shape[0], dst.shape[1]
    per = rows // 16

    @pl.loop(0, blocks * per)
    def _(i):
        at = (i // per, pl.ds(pl.multiple_of(lax.rem(i, per) * 16, 16), 16), slice(None))
        dst[at] = (left[at].astype(F32) + right[at].astype(F32)).astype(dst.dtype)


class ReduceLine(Line):
    def __init__(self, net, part, own, mate, from_left, from_right):
        self.net, self.own, self.mate, self.bufs = net, own, mate, (from_left, from_right)
        z, c, Z = net.z, net.c, net.Z
        self.order = []
        for t in range((Z + 1) // 2):
            self.order += [Z - 1 - t] + ([t] if t != Z - 1 - t else [])
        self.swaps = {k: net.copy(part(2 * k + 1 - c), mate.at[k], net.partner()) for k in self.order}
        self.loads = {k: net.near(part(2 * k + c), own.at[k]) for k in self.order}
        self.base = net.used
        net.used += 2 * (Z - 1)
        ends = (jnp.clip(Z - 1 - z, 0, Z - 2), jnp.clip(z, 0, Z - 2))
        self.last = [net.near(buf.at[t], mate.at[i]) for i, (buf, t) in enumerate(zip(self.bufs, ends))]

    def start(self):
        for k in self.order:
            self.net.send(self.swaps[k])
            self.loads[k].start()

    def hop(self, side, t):
        net, last = self.net, self.net.Z - 1
        place, way = (last - t, 0) if side == 1 else (t, 1)
        return net.copy_at(
            self.base + way * last + t, self.own.at[place], self.bufs[way].at[t], net.line_peer(net.z + side)
        )

    def pair(self):
        net, done = self.net, set()
        last = net.Z - 1
        right, left = last, 0
        for k in self.order:
            self.loads[k].wait()
            self.swaps[k].wait_recv()
            add_slabs(self.own.at[k], self.own.at[k], self.mate.at[k])
            done.add(k)
            while right > 0 and right in done:
                net.send(self.hop(1, last - right), net.z == 0)
                right -= 1
            while left < last and left in done:
                net.send(self.hop(-1, left), net.z == last)
                left += 1

    def step(self, n):
        net = self.net
        z, last = net.z, net.Z - 1
        for side, far, way in ((1, z, 0), (-1, last - z, 1)):
            t = jnp.clip(n - far, 0, last - 1)
            here = (far >= 1) & (far <= n)
            hop = self.hop(side, t)
            run(here, hop.wait_recv)
            if n < last:
                place, held = last - t if side == 1 else t, self.mate.at[way]
                load = net.near(self.bufs[way].at[t], held)

                def add():
                    load.start()
                    load.wait()
                    add_slabs(self.own.at[place], self.own.at[place], held)

                run(here, add)
                net.send(hop, here)

    def total(self, out):
        z, last = self.net.z, self.net.Z - 1
        here = (z > 0, z < last)
        for copy, when in zip(self.last, here):
            run(when, copy.start)
        for copy, when in zip(self.last, here):
            run(when, copy.wait)
        per = out.shape[1] // 16

        def body(ways):
            @pl.loop(0, out.shape[0] * per)
            def _(i):
                at = (i // per, pl.ds(pl.multiple_of(lax.rem(i, per) * 16, 16), 16), slice(None))
                value = self.own.at[z][at].astype(F32)
                for way in ways:
                    value = value + self.mate[(way,) + at].astype(F32)
                out[at] = value.astype(out.dtype)

        run(z == 0, lambda: body((1,)))
        run(z == last, lambda: body((0,)))
        if last > 1:
            run((z > 0) & (z < last), lambda: body((0, 1)))


ANY = pl.BlockSpec(memory_space=pl.ANY)
MIB = 1024 * 1024
T, CH = 256, 512
shape = jax.ShapeDtypeStruct


def nt(left, right):
    return lax.dot_general(left, right, (((1,), (1,)), ((), ())), preferred_element_type=F32)


def tn(left, right):
    return lax.dot_general(left, right, (((0,), (0,)), ((), ())), preferred_element_type=F32)


def turn(value, cosine, ahead, behind):
    half = 32
    return value * cosine + pltpu.roll(value, 128 - half, 1) * ahead + pltpu.roll(value, half, 1) * behind


def stream(body, grid, ins, outs):
    def spec(entry):
        block, index = entry[1:3]
        return pl.BlockSpec(block, index, pipeline_mode=pl.Buffered(1)) if len(entry) > 3 else pl.BlockSpec(block, index)

    pltpu.emit_pipeline(
        body, grid=grid, in_specs=[spec(e) for e in ins], out_specs=[spec(e) for e in outs]
    )(*[e[0] for e in ins], *[e[0] for e in outs])


def whole(ref):
    return (ref, ref.shape, lambda *i: (0,) * len(ref.shape), 1)


def lanes(ref, width=T):
    return (ref, (ref.shape[0], width), lambda i: (0, i))


def chunks(rows, size):
    return lambda body: pl.loop(0, rows // size)(lambda i: body(pl.ds(pl.multiple_of(i * size, size), size), i))


def layer_kernel(seq_n, dp_n, dims, n_ins, n_outs, *refs):
    ins, outs = refs[:n_ins], refs[n_ins : n_ins + n_outs]
    scratch = refs[n_ins + n_outs :]
    x_own, gy_own, up_cut, qkv_cut, out_w, down_w, small, tables = ins
    mixed_out, input_grad, up_out, qkv_out, out_red, down_red, small_red = outs[:7]
    x, gy, n1, n2, qkv_all, out_all, heads, gatt, att, gproj, wide_f, mixed, wide = outs[7:20]
    p_qkv, p_out, qkv_red, mixed_in, wide_in = outs[20:25]
    up_all, down_all, hidden, slope, grad_up, p_up, p_down, up_red = [outs[25 + 2 * i : 27 + 2 * i] for i in range(8)]
    hops = outs[41:]
    sems, scratch = scratch[:3], scratch[3:]
    small_v, vec, up_b, qkv_b, doc_row, doc_col, mean_v, inv_v, sm, sm_dp, sm_sum, dk_acc, dv_acc = scratch[:13]
    x_v, gy_v, out_v, up_v, qkv_v, qkv_f, out_f, down_f = scratch[13:21]
    up_f, scratch = scratch[21:23], scratch[23:]
    L, D, ff, H, r, ro, rd = dims
    hd = T
    l, ffh, rdh, half_n = H * hd, ff // 2, rd // 2, 2
    net = Net(seq_n, dp_n, *sems)
    S, Z, s, d = net.S, net.Z, net.s, net.d
    tok = L // S
    scale = 1.0 / math.sqrt(hd)
    per = dp_n * r // T
    own_rows = pl.ds(pl.multiple_of(s * tok, tok), tok)

    def d_rows(ref):
        return (ref, (1, T // r, r, ref.shape[3]), lambda i: (lax.div(i, per), lax.rem(i, per), 0, 0))

    def reduce(i, part):
        return ReduceLine(net, part, scratch[2 * i], scratch[2 * i + 1], hops[2 * i], hops[2 * i + 1])

    def seq_rows(ref):
        def slot(k, h):
            size = tok if h is None else tok // 2
            return ref.at[pl.ds(pl.multiple_of(k * tok + (h or 0) * size, size), size)]

        return slot

    halves = range(half_n)
    x_g, gy_g = GatherSeq(net, x_own, seq_rows(x)), GatherSeq(net, gy_own, seq_rows(gy))
    su = [Exchange(net, lambda k, h=h: up_cut.at[h, k], lambda k, h=h: up_all[h].at[k, d]) for h in halves]
    sq = Exchange(net, lambda k: qkv_cut.at[k], lambda k: qkv_all.at[k, d])
    o_g = GatherLine(net, lambda k: out_all.at[k], out_w)
    q_g = GatherLine(net, lambda k: qkv_all.at[:, k])
    u_g = [GatherLine(net, lambda k, h=h: up_all[h].at[:, k]) for h in halves]
    down_rows = [down_w.at[pl.ds(h * rdh, rdh)] for h in halves]
    d_g = [GatherLine(net, lambda k, h=h: down_all[h].at[k], down_rows[h]) for h in halves]
    ds = [reduce(h, lambda k, h=h: p_down[h].at[pl.ds(k, 1)]) for h in halves]
    us = [reduce(2 + h, lambda k, h=h: p_up[h].at[:, k]) for h in halves]
    qs = reduce(4, lambda k: p_qkv.at[:, k])
    os = reduce(5, lambda k: p_out.at[pl.ds(k, 1)])
    mx = Exchange(net, lambda k: mixed.at[k], lambda k: mixed_in.at[k], by_turn=True)
    wx = Exchange(net, lambda k: wide.at[k], lambda k: wide_in.at[k], by_turn=True)
    qx = Exchange(net, lambda k: qkv_f.at[k], lambda k: qkv_red.at[k], own=True)
    ux = [Exchange(net, lambda k, h=h: up_f[h].at[k], lambda k, h=h: up_red[h].at[k], own=True) for h in halves]
    sf = Exchange(net, lambda k: small_v.at[s], lambda k: small_v.at[k])
    sm_x = Exchange(net, lambda k: sm_sum, lambda k: small_red.at[k], own=True)
    small_to = [lax.rem(d + k, dp_n) for k in range(1, dp_n)]
    small_from = [lax.rem(d + dp_n - k, dp_n) for k in range(1, dp_n)]
    sf_dp = [net.copy(small, small_v.at[s, d], (s, to)) for to in small_to]
    sm_to = [net.copy(sm, sm_dp.at[d], (s, to)) for to in small_to]
    sf_own = net.near(small, small_v.at[s, d])
    loc = Bounce(
        net,
        [(up_cut.at[h, s], up_v.at[h], up_all[h].at[s, d]) for h in halves]
        + [
            (qkv_cut.at[s], qkv_v, qkv_all.at[s, d]),
            (x_own, x_v, x.at[own_rows]),
            (gy_own, gy_v, gy.at[own_rows]),
            (out_w, out_v, out_all.at[d]),
        ]
        + [(down_rows[h], scratch[2 * h].at[0, 0], down_all[h].at[d]) for h in halves],
    )
    out_copies = [net.near(out_f, out_red)] + [net.near(down_f.at[:, pl.ds(h * rdh, rdh)], down_red.at[:, pl.ds(h * rdh, rdh)]) for h in halves]

    def small_first():
        sf_own.start()
        for copy in sf_dp:
            net.send(copy)

    def small_second():
        sf_own.wait()
        for copy in sf_dp:
            copy.wait_recv()
        sf.start()

    def sums_first():
        for copy in sm_to:
            net.send(copy)

    def sums_second():
        sm_sum[...] = sm[...]
        for copy, source in zip(sm_to, small_from):
            copy.wait_recv()
            sm_sum[...] += sm_dp[source]
        sm_x.start()

    def pieces(out, row, found):
        lane = lax.broadcasted_iota(jnp.int32, (1, 128), 1) // r
        q = 128 // r
        for p in range(len(found) // q):
            value = small_v[found[p * q]]
            for k in range(1, q):
                value = jnp.where(lane == k, small_v[found[p * q + k]], value)
            out[row : row + 1, 128 * p : 128 * p + 128] = value

    def unpack():
        sf.wait()
        for j in range(5):
            pieces(vec, j, [(i // dp_n, i % dp_n, slice(j, j + 1)) for i in range(seq_n * dp_n)])
        for h in halves:
            pieces(up_b, h, [(s, m // 2, slice(8 + 2 * h + m % 2, 9 + 2 * h + m % 2)) for m in range(2 * dp_n)])
        found = []
        for j in range(3):
            for m in range(l // r):
                piece = j * (D // r) + s * (l // r) + m
                owner = lax.div(piece, 3)
                found.append((lax.div(owner, dp_n), lax.rem(owner, dp_n), pl.ds(5 + lax.rem(piece, 3), 1)))
        pieces(qkv_b, 0, found)
        for k in range(S):
            for j in range(tok // 128):
                row = small_v[k, d, 12 + j : 13 + j]
                at = k * tok + j * 128
                doc_row[0:1, at : at + 128] = row
                doc_col[at : at + 128, :] = jnp.transpose(jnp.broadcast_to(row, (128, 128)))
        sm[...] = jnp.zeros_like(sm)
        sm[4:5, :] = jnp.sum(gy_v[...].astype(F32), 0, keepdims=True)

    def norm_phase():
        def body(xb, a, b):
            i = pl.program_id(0)
            at = pl.ds(pl.multiple_of(i * T, T), T)
            wide_x = xb[...].astype(F32)
            mean = jnp.mean(wide_x, -1, keepdims=True)
            center = wide_x - mean
            inv = lax.rsqrt(jnp.mean(center * center, -1, keepdims=True) + epsilon)
            mean_v[at, :] = mean
            inv_v[at, :] = inv
            hat = center * inv
            a[...] = (hat * vec[0:1, :] + vec[1:2, :]).astype(BF)
            b[...] = (hat * vec[2:3, :] + vec[3:4, :]).astype(BF)

        rows = lambda ref: (ref, (T, D), lambda i: (i, 0))
        stream(body, (L // T,), [rows(x)], [rows(n1), rows(n2)])

    def up_phase(h):
        def body(a, w, hid, slo):
            wv = w[...].reshape(D, T)
            bias = up_b[h : h + 1, pl.ds(pl.multiple_of(pl.program_id(0) * T, T), T)]

            @chunks(L, CH)
            def _(at, i):
                u = dot(a[at, :], wv) + bias
                phi = 0.5 + 0.5 * lax.erf(u * math.sqrt(0.5))
                hid[at, :] = (u * phi).astype(BF)
                slo[at, :] = (phi + u * (jnp.exp(-0.5 * u * u) * (1.0 / math.sqrt(2.0 * math.pi)))).astype(BF)

        w = (up_all[h], (S, dp_n, r, T), lambda i: (0, 0, 0, i))
        stream(body, (ffh // T,), [whole(n2), w], [lanes(hidden[h]), lanes(slope[h])])

    def outer_phase(left, right, out):
        def body(a, b, o):
            width = o.shape[-1]
            step = min(width, 1024)

            @chunks(width, step)
            def _(at, j):
                o[(slice(None),) * (len(o.shape) - 1) + (at,)] = tn(a[...], b[:, at]).astype(BF).reshape(o.shape[:-1] + (step,))

        if len(out.shape) == 3:
            target = (out, (T // out.shape[1], out.shape[1], D), lambda i: (i, 0, 0))
        else:
            target = d_rows(out)
        stream(body, (left.shape[1] // T,), [lanes(left), whole(right)], [target])

    def qkv_grad_phase():
        def body(a, b, o):
            for j in range(3):
                o[:, :, :, j * l : (j + 1) * l] = tn(a[...], b[j]).astype(BF).reshape(o.shape[:-1] + (l,))

            @pl.when(pl.program_id(0) == 0)
            def _():
                for j in range(3):
                    sm[6:7, j * l : (j + 1) * l] = jnp.sum(b[j].astype(F32), 0, keepdims=True)

        stream(body, (D // T,), [lanes(n1), whole(gproj)], [d_rows(p_qkv)])

    def gatt_phase():
        def body(a, w, o):
            o[0] = nt(a[...], w[...].reshape(T, D)).astype(BF)

        w = (out_all, (T // ro, ro, D), lambda i: (i, 0, 0))
        stream(body, (H,), [whole(gy), w], [(gatt, (1, L, hd), lambda i: (i, 0, 0))])

    def qkv_phase():
        def body(a, w, tab, o):
            j = pl.program_id(0)
            wv = w[...].reshape(D, T)
            bias = qkv_b[0:1, pl.ds(pl.multiple_of(j * T, T), T)]

            @chunks(L, CH)
            def _(at, i):
                p = dot(a[at, :], wv) + bias
                o[0, at, 128:] = p[:, 128:].astype(BF)

                @pl.when(j < 2 * H)
                def _():
                    o[0, at, :128] = turn(p[:, :128], tab[0, at, :], tab[1, at, :], tab[2, at, :]).astype(BF)

                @pl.when(j >= 2 * H)
                def _():
                    o[0, at, :128] = p[:, :128].astype(BF)

        w = (qkv_all, (S, dp_n, r, T), lambda i: (0, 0, 0, i))
        stream(body, (3 * H,), [whole(n1), w, whole(tables)], [(heads, (1, L, hd), lambda i: (i, 0, 0))])

    def att_phase():
        def body(q, k, v, ga, tab, out, dq, dk, dv):
            i = pl.program_id(1)
            qt, kt, vt, gt = q[0], k[0], v[0], ga[0]
            raw = nt(qt, kt) * scale
            at = pl.ds(pl.multiple_of(i * T, T), T)
            query = lax.broadcasted_iota(jnp.int32, (T, L), 0) + i * T
            key = lax.broadcasted_iota(jnp.int32, (T, L), 1)
            allowed = (doc_col[at, 0:1] == doc_row[0:1, :]) & (key <= query)
            raw = jnp.where(allowed, raw, -1000000000.0)
            e = jnp.exp(raw - jnp.max(raw, -1, keepdims=True))
            p = e / jnp.sum(e, -1, keepdims=True)
            pb = p.astype(BF)
            out[...] = dot(pb, vt).astype(BF)
            gp = nt(gt, vt)
            gs = (p * (gp - jnp.sum(gp * p, -1, keepdims=True))).astype(BF)
            gq = dot(gs, kt) * scale
            back = lambda t, rows: turn(t, tab[0, rows, :], -tab[1, rows, :], -tab[2, rows, :])
            dq[0, :, :128] = back(gq[:, :128], at).astype(BF)
            dq[0, :, 128:] = gq[:, 128:].astype(BF)

            @pl.when(i == 0)
            def _():
                dk_acc[...] = jnp.zeros_like(dk_acc)
                dv_acc[...] = jnp.zeros_like(dv_acc)

            dk_acc[...] += tn(gs, qt)
            dv_acc[...] += tn(pb, gt)

            @pl.when(i == L // T - 1)
            def _():
                gk = dk_acc[...] * scale
                dk[0, :, :128] = back(gk[:, :128], slice(None)).astype(BF)
                dk[0, :, 128:] = gk[:, 128:].astype(BF)
                dv[0] = dv_acc[...].astype(BF)

        tile = (1, T, hd)
        full = (1, L, hd)
        stream(
            body,
            (H, L // T),
            [
                (heads, tile, lambda h, i: (h, i, 0)),
                (heads, full, lambda h, i: (H + h, 0, 0)),
                (heads, full, lambda h, i: (2 * H + h, 0, 0)),
                (gatt, tile, lambda h, i: (h, i, 0)),
                whole(tables),
            ],
            [
                (att, (T, hd), lambda h, i: (i, h)),
                (gproj.at[pl.ds(0, 1)], tile, lambda h, i: (0, i, h)),
                (gproj.at[pl.ds(1, 1)], full, lambda h, i: (0, 0, h)),
                (gproj.at[pl.ds(2, 1)], full, lambda h, i: (0, 0, h)),
            ],
        )

    def norm_sums(grad, xb, at, row, cols):
        hat = (xb[at, :].astype(F32) - mean_v[at, :]) * inv_v[at, :]
        sm[row : row + 1, cols] += jnp.sum(grad * hat, 0, keepdims=True)
        sm[row + 1 : row + 2, cols] += jnp.sum(grad, 0, keepdims=True)

    def one_phase():
        def body(gp, w, xb, o):
            cols = pl.ds(pl.multiple_of(pl.program_id(0) * T, T), T)
            wv = w[...].reshape(T, 3 * l)

            @chunks(L, CH)
            def _(at, m):
                grad = nt(gp[0, at, :], wv[:, :l]) + nt(gp[1, at, :], wv[:, l : 2 * l]) + nt(gp[2, at, :], wv[:, 2 * l :])
                norm_sums(grad, xb, at, 0, cols)
                o[at, :] = grad * vec[0:1, cols]

        stream(body, (D // T,), [whole(gproj), d_rows(qkv_all), lanes(x)], [lanes(wide_f)])

    def two_phase():
        def body(ga, gb, wa, wb, xb, first, o):
            cols = pl.ds(pl.multiple_of(pl.program_id(0) * T, T), T)
            wav, wbv = wa[...].reshape(T, ffh), wb[...].reshape(T, ffh)

            @chunks(L, tok)
            def _(at, m):
                grad = nt(ga[at, :], wav) + nt(gb[at, :], wbv)
                norm_sums(grad, xb, at, 2, cols)
                o[m] = (first[at, :] + grad * vec[2:3, cols]).astype(BF)

        stream(
            body,
            (D // T,),
            [whole(grad_up[0]), whole(grad_up[1]), d_rows(up_all[0]), d_rows(up_all[1]), lanes(x), lanes(wide_f)],
            [(wide, (S, tok, T), lambda i: (0, 0, i))],
        )

    def mixed_phase():
        def body(ha, hb, wa, wb, a, wo, o):
            wav, wbv, wov = wa[...].reshape(ffh, T), wb[...].reshape(ffh, T), wo[...].reshape(l, T)

            @chunks(L, tok)
            def _(at, m):
                o[m] = (dot(ha[at, :], wav) + dot(hb[at, :], wbv) + dot(a[at, :], wov)).astype(BF)

        cols = lambda ref: (ref, ref.shape[:2] + (T,), lambda i: (0, 0, i))
        stream(
            body,
            (D // T,),
            [whole(hidden[0]), whole(hidden[1]), cols(down_all[0]), cols(down_all[1]), whole(att), cols(out_all)],
            [(mixed, (S, tok, T), lambda i: (0, 0, i))],
        )

    def slope_phase(h):
        def body(a, w, slo, o):
            i = pl.program_id(0)
            wv = w[...].reshape(T, D)
            cols = pl.ds(pl.multiple_of(h * ffh + i * T, T), T)

            @chunks(L, CH)
            def _(at, m):
                gu = (nt(a[at, :], wv) * slo[at, :].astype(F32)).astype(BF)
                o[at, :] = gu
                sm[5:6, cols] += jnp.sum(gu.astype(F32), 0, keepdims=True)

        w = (down_all[h], (T // rdh, rdh, D), lambda i: (i, 0, 0))
        stream(body, (ffh // T,), [whole(gy), w, lanes(slope[h])], [lanes(grad_up[h])])

    part = min(128, tok)
    tiles = lambda ref, lead: (ref, (lead, part, D), lambda i: (0, i, 0))
    mine = lambda ref: (ref.at[own_rows], (part, D), lambda i: (i, 0))

    def mixed_end():
        def body(xb, own, came, o):
            total = xb[...].astype(F32) + vec[4:5, :] + own[0].astype(F32)
            for k in range(S - 1):
                total = total + came[k].astype(F32)
            o[0] = total.astype(BF)

        own = tiles(mixed.at[pl.ds(s, 1)], 1)
        stream(body, (tok // part,), [mine(x), own, tiles(mixed_in, S - 1)], [tiles(mixed_out, 1)])

    def input_end():
        def body(xb, gb, own, came, o):
            at = pl.ds(pl.multiple_of(s * tok + pl.program_id(0) * part, part), part)
            inv = inv_v[at, :]
            hat = (xb[...].astype(F32) - mean_v[at, :]) * inv
            total = own[0].astype(F32)
            for k in range(S - 1):
                total = total + came[k].astype(F32)
            total = total - jnp.mean(total, -1, keepdims=True) - hat * jnp.mean(total * hat, -1, keepdims=True)
            o[0] = gb[...].astype(F32) + inv * total

        own = tiles(wide.at[pl.ds(s, 1)], 1)
        stream(body, (tok // part,), [mine(x), mine(gy), own, tiles(wide_in, S - 1)], [tiles(input_grad, 1)])

    def qkv_end():
        def body(a, o):
            o[...] = a[0].astype(F32)

        stream(body, (S, 3), [(qkv_red, (1, r, l), lambda k, j: (k, 0, j))], [(qkv_out, (r, l), lambda k, j: (0, j * S + k))])

    def up_end():
        def body(a, b, o):
            for k in range(dp_n):
                for h, src in enumerate((a, b)):
                    o[:, k * rd + h * rdh : k * rd + (h + 1) * rdh] = src[0, :, k * rdh : (k + 1) * rdh].astype(F32)

        block = lambda ref: (ref, (1, r, ffh), lambda k: (k, 0, 0))
        stream(body, (S,), [block(up_red[0]), block(up_red[1])], [(up_out, (r, ff), lambda k: (0, k))])

    net.barrier()
    loc.start()
    small_first()
    o_g.early()
    loc.finish()
    sq.start()
    o_g.start()
    o_g.go(1)
    x_g.start()
    su[0].start()
    sq.wait()
    q_g.early()
    q_g.start()
    o_g.go(2)
    small_second()
    x_g.relay()
    q_g.go(1)
    o_g.go(3)
    o_g.wait()
    gy_g.start()
    x_g.wait()
    su[0].wait()
    u_g[0].early()
    q_g.go(2)
    unpack()
    norm_phase()
    d_g[0].early()
    d_g[0].start()
    su[1].start()
    q_g.go(3)
    gy_g.relay()
    u_g[0].start()
    q_g.wait()
    qkv_phase()
    d_g[1].early()
    d_g[0].go(1)
    d_g[1].start()
    gy_g.wait()
    gatt_phase()
    u_g[0].go(1)
    su[1].wait()
    u_g[1].early()
    u_g[1].start()
    att_phase()
    qkv_grad_phase()
    qs.start()
    d_g[0].go(2)
    outer_phase(att, gy, p_out)
    os.start()
    u_g[0].go(2)
    qs.pair()
    u_g[1].go(1)
    one_phase()
    u_g[0].go(3)
    d_g[0].go(3)
    os.pair()
    u_g[0].wait()
    up_phase(0)
    u_g[1].go(2)
    d_g[1].go(1)
    d_g[0].wait()
    slope_phase(0)
    u_g[1].go(3)
    outer_phase(n2, grad_up[0], p_up[0])
    us[0].start()
    u_g[1].wait()
    qs.go(1)
    d_g[1].go(2)
    up_phase(1)
    us[0].pair()
    d_g[1].go(3)
    outer_phase(hidden[0], gy, p_down[0])
    d_g[1].wait()
    qs.go(2)
    mixed_phase()
    mx.start()
    ds[0].start()
    os.go(1)
    qs.go(3)
    qs.total(qkv_f)
    ds[0].pair()
    us[0].go(1)
    slope_phase(1)
    outer_phase(n2, grad_up[1], p_up[1])
    us[1].start()
    qx.start()
    os.go(2)
    us[0].go(2)
    ds[0].go(1)
    us[1].pair()
    two_phase()
    sums_first()
    wx.start()
    us[1].go(1)
    outer_phase(hidden[1], gy, p_down[1])
    ds[0].go(2)
    ds[1].start()
    sums_second()
    us[1].go(2)
    qx.wait()
    qkv_end()
    ds[1].pair()
    os.go(3)
    ds[1].go(1)
    us[0].go(3)
    us[0].total(up_f[0])
    ux[0].start()
    wx.wait()
    us[1].go(3)
    os.total(out_f)
    out_copies[0].start()
    ds[0].go(3)
    us[1].total(up_f[1])
    ds[1].go(2)
    ux[1].start()
    mx.wait()
    mixed_end()
    input_end()
    ds[0].total(down_f.at[:, pl.ds(0 * rdh, rdh)])
    out_copies[1].start()
    ux[1].wait()
    ux[0].wait()
    up_end()
    ds[1].go(3)
    ds[1].total(down_f.at[:, pl.ds(1 * rdh, rdh)])
    out_copies[2].start()
    sm_x.wait()
    for copy in out_copies:
        copy.wait()
    net.drain()


def layer(seq_n, dp_n, dims, args):
    L, D, ff, H, r, ro, rd = dims
    l, Z, ffh, rdh = H * T, dp_n // 2, ff // 2, rd // 2
    tok = L // seq_n
    seq_tok, up_slab, qkv_slab = (seq_n, tok, D), (seq_n, r, ffh), (seq_n, r, 3 * l)
    outs = [((1, tok, D), BF), ((1, tok, D), F32), ((r, seq_n * ff), F32), ((r, seq_n * 3 * l), F32)]
    outs += [((1, ro, D), F32), ((1, rd, D), F32), ((seq_n, 8, D), F32)]
    outs += [((L, D), BF)] * 4
    outs += [((seq_n, dp_n, r, 3 * l), BF), ((dp_n, ro, D), BF), ((3 * H, L, T), BF), ((H, L, T), BF)]
    outs += [((L, l), BF), ((3, L, l), BF), ((L, D), F32), (seq_tok, BF), (seq_tok, BF)]
    outs += [((seq_n, dp_n, r, 3 * l), BF), ((dp_n, ro, D), BF), (qkv_slab, BF)]
    outs += [((seq_n - 1, tok, D), BF)] * 2
    up_full, down_full, act = (seq_n, dp_n, r, ffh), (dp_n, rdh, D), (L, ffh)
    for v in (up_full, down_full, act, act, act, up_full, down_full, up_slab):
        outs += [(v, BF)] * 2
    slabs = [(1, rdh, D)] * 2 + [up_slab] * 2 + [qkv_slab, (1, ro, D)]
    for slab in slabs:
        outs += [((Z - 1,) + slab, BF)] * 2
    out_shape = [shape(*o) for o in outs]
    n = 6 * (4 * Z - 3) + 6 * (3 * Z - 2) + 10 * (seq_n - 1) + 2 * max(4, seq_n - 1) + 2 * (dp_n - 1)
    vmem = [((seq_n, dp_n, 16, 128), F32), ((8, D), F32), ((8, ffh), F32), ((8, 3 * l), F32), ((8, L), F32), ((L, 128), F32)]
    vmem += [((L, 1), F32), ((L, 1), F32), ((8, D), F32), ((dp_n, 8, D), F32), ((8, D), F32), ((L, T), F32), ((L, T), F32)]
    vmem += [((tok, D), BF), ((tok, D), BF), ((ro, D), BF), ((2, r, ffh), BF), ((r, 3 * l), BF)]
    vmem += [(qkv_slab, BF), ((1, ro, D), F32), ((1, rd, D), F32), (up_slab, BF), (up_slab, BF)]
    for slab in slabs:
        vmem += [((Z,) + slab, BF)] * 2
    scratch = [pltpu.SemaphoreType.DMA((k,)) for k in (n, n, 32 + 6 * (3 * Z - 2))] + [pltpu.VMEM(*v) for v in vmem]
    return pl.pallas_call(
        functools.partial(layer_kernel, seq_n, dp_n, dims, len(args), len(outs)),
        out_shape=out_shape,
        in_specs=[ANY] * len(args),
        out_specs=[ANY] * len(outs),
        scratch_shapes=scratch,
        compiler_params=pltpu.CompilerParams(collective_id=0, has_side_effects=True, vmem_limit_bytes=62 * MIB),
        name="layer",
    )(*args)[:7]


def shards(
    tokens,
    doc_ids,
    ln1_gain,
    ln1_bias,
    ln2_gain,
    ln2_bias,
    qkv_weight,
    qkv_bias,
    out_weight,
    up_weight,
    up_bias,
    down_weight,
    out_bias,
    cotangent,
):
    seq_n = lax.axis_size("seq")
    dp_n = lax.axis_size("dp")
    seq_i = lax.axis_index("seq")
    tok_rows, width = tokens.shape[1:]
    length = tok_rows * seq_n
    head_dim = width // HEADS
    heads = HEADS // seq_n
    local = heads * head_dim
    ff = up_weight.shape[1] // seq_n
    rot_dims = head_dim // 4
    rows, ff_half = qkv_weight.shape[0], ff // 2
    per_down = down_weight.shape[0]
    qkv_cut = qkv_weight.reshape(rows, 3, seq_n, local).transpose(2, 0, 1, 3).reshape(seq_n, rows, 3 * local)
    up_cut = up_weight.reshape(rows, seq_n, dp_n, 2, per_down // 2).transpose(3, 1, 0, 2, 4)
    up_cut = up_cut.reshape(2, seq_n, rows, ff_half)
    pieces = jnp.concatenate([ln1_gain, ln1_bias, ln2_gain, ln2_bias, out_bias, qkv_bias, up_bias]).reshape(-1, rows)
    pieces = jnp.tile(pieces.astype(F32), (1, 128 // rows))
    docs = doc_ids.astype(F32).reshape(-1, 128)
    small = jnp.concatenate([pieces, docs, jnp.zeros((16 - pieces.shape[0] - docs.shape[0], 128), F32)])
    mixed, input_grad, up_grad, qkv_grad, out_grad, down_grad, sums = layer(
        seq_n,
        dp_n,
        (length, width, ff, heads, rows, out_weight.shape[0], per_down),
        (
            tokens[0],
            cotangent[0],
            up_cut,
            qkv_cut,
            out_weight,
            down_weight,
            small,
            jnp.asarray(rotary_rows(length, rot_dims)),
        ),
    )
    n = seq_n * dp_n
    place = seq_i * dp_n + lax.axis_index("dp")

    def mine(vector):
        return lax.dynamic_index_in_dim(vector.reshape(n, -1), place, 0, False)

    lns = jnp.sum(sums[:, :5], 0)
    g1, b1, g2, b2, ob = [mine(lns[k]) for k in range(5)]
    ub = mine(sums[:, 5, :ff].reshape(seq_n, 2, dp_n, -1).transpose(0, 2, 1, 3))
    qb = mine(sums[:, 6, : 3 * local].reshape(seq_n, 3, local).transpose(1, 0, 2))
    return (mixed, input_grad, g1, b1, g2, b2, qkv_grad, qb, out_grad[0], up_grad, ub, down_grad[0], ob)


def solution(mesh):
    in_specs = (
        P("dp", "seq", None),
        P("dp", "seq"),
        P(("seq", "dp")),
        P(("seq", "dp")),
        P(("seq", "dp")),
        P(("seq", "dp")),
        P(("seq", "dp"), None),
        P(("seq", "dp")),
        P(("seq", "dp"), None),
        P(("seq", "dp"), None),
        P(("seq", "dp")),
        P(("seq", "dp"), None),
        P(("seq", "dp")),
        P("dp", "seq", None),
    )
    out_specs = (
        P("dp", "seq", None),
        P("dp", "seq", None),
        P(("seq", "dp")),
        P(("seq", "dp")),
        P(("seq", "dp")),
        P(("seq", "dp")),
        P(("seq", "dp"), None),
        P(("seq", "dp")),
        P(("seq", "dp"), None),
        P(("seq", "dp"), None),
        P(("seq", "dp")),
        P(("seq", "dp"), None),
        P(("seq", "dp")),
    )
    return jax.shard_map(shards, mesh=mesh, in_specs=in_specs, out_specs=out_specs, check_vma=False)
```

```python
import functools
import math

import jax
import jax.numpy as jnp
import numpy as np
from jax import lax
from jax.experimental import pallas as pl
from jax.experimental.pallas import tpu as pltpu
from jax.sharding import PartitionSpec as P

HEADS = 8
BF = jnp.bfloat16
F32 = jnp.float32


epsilon = 1e-05


def rotary_rows(length, rot_dims):
    half = rot_dims // 2
    exponents = np.arange(half, dtype=np.float32) * np.float32(2.0 / rot_dims)
    inverse = np.power(np.float32(10000.0), -exponents).astype(np.float32)
    phase = (np.arange(length, dtype=np.float32)[:, None] * inverse[None, :]).astype(np.float64)
    tables = np.zeros((2, length, 128), np.float32)
    tables[0] = 1.0
    tables[0, :, :half] = tables[0, :, half:rot_dims] = np.cos(phase)
    tables[1, :, :half] = -np.sin(phase)
    tables[1, :, half:rot_dims] = np.sin(phase)
    return tables


def dot(left, right):
    return jnp.dot(left, right, preferred_element_type=F32)


MESH = pl.DeviceIdType.MESH


def run(when, action):
    if when is None:
        action()
    else:
        pl.when(when)(lambda: action())


class Net:
    def __init__(self, seq_n, dp_n, send_sems, recv_sems, local_sems):
        self.S, self.DP, self.Z = seq_n, dp_n, dp_n // 2
        self.s, self.d = lax.axis_index("seq"), lax.axis_index("dp")
        self.z, self.c = self.d // 2, lax.rem(self.d, 2)
        self.send_sems, self.recv_sems, self.used = send_sems, recv_sems, 0
        self.local_sems, self.local_used = local_sems, 0
        self.sent = []

    def seq_peer(self, s):
        return (s, self.d)

    def line_peer(self, z):
        return (self.s, 2 * jnp.clip(z, 0, self.Z - 1) + self.c)

    def partner(self):
        return (self.s, 2 * self.z + 1 - self.c)

    def copy(self, src, dst, device):
        self.used += 1
        return self.copy_at(self.used - 1, src, dst, device)

    def copy_at(self, i, src, dst, device):
        return pltpu.make_async_remote_copy(
            src_ref=src,
            dst_ref=dst,
            send_sem=self.send_sems.at[i],
            recv_sem=self.recv_sems.at[i],
            device_id=device,
            device_id_type=MESH,
        )

    def send(self, copy, when=None):
        self.sent.append((copy, when))
        run(when, copy.start)

    def drain(self):
        for copy, when in self.sent:
            run(when, copy.wait_send)

    def near(self, src, dst):
        self.local_used += 1
        return pltpu.make_async_copy(src, dst, self.local_sems.at[self.local_used - 1])

    def barrier(self):
        sem = pltpu.get_barrier_semaphore()
        peers = [self.seq_peer(lax.rem(self.s + k, self.S)) for k in range(1, self.S)]
        peers += [(self.s, lax.rem(self.d + k, self.DP)) for k in range(1, self.DP)]
        for device in peers:
            pl.semaphore_signal(sem, inc=1, device_id=device, device_id_type=MESH)
        pl.semaphore_wait(sem, len(peers))


class Place:
    def __init__(self, net, direct, through):
        self.direct = [net.near(src, dst) for src, dst in direct]
        self.loads = [net.near(src, buf) for src, buf, _ in through]
        self.stores = [net.near(buf, dst) for _, buf, dst in through]

    def start(self):
        for copy in self.loads + self.direct:
            copy.start()

    def finish(self):
        for load, store in zip(self.loads, self.stores):
            load.wait()
            store.start()
        for copy in self.stores + self.direct:
            copy.wait()


class Exchange:
    def __init__(self, net, src, slot, by_turn=False, own=False):
        self.net, self.copies = net, []
        for k in range(1, net.S):
            to = lax.rem(net.s + k, net.S)
            self.copies.append(net.copy(src(to), slot(k - 1 if by_turn else net.s), net.seq_peer(to)))
        self.own = net.near(src(net.s), slot(net.s)) if own else None

    def start(self):
        for copy in self.copies:
            self.net.send(copy)
        if self.own is not None:
            self.own.start()

    def wait(self):
        for copy in self.copies:
            copy.wait_recv()
        if self.own is not None:
            self.own.wait()


class GatherSeq:
    def __init__(self, net, src, slot):
        self.net, self.square = net, net.S == 4
        if self.square:
            s = net.s
            a, b = s + 1 - 2 * lax.rem(s, 2), lax.rem(s + 2, 4)
            self.first = [net.copy(src, slot(s, None), net.seq_peer(p)) for p in (a, b)]
            self.second = [
                net.copy(slot(a, 0), slot(a, 0), net.seq_peer(b)),
                net.copy(slot(b, 1), slot(b, 1), net.seq_peer(a)),
            ]
        else:
            self.direct = Exchange(net, lambda to: src, lambda k: slot(k, None))

    def start(self):
        if self.square:
            for copy in self.first:
                self.net.send(copy)
        else:
            self.direct.start()

    def relay(self):
        if self.square:
            for came, onward in zip(self.first, self.second):
                came.wait_recv()
                self.net.send(onward)

    def wait(self):
        if self.square:
            for copy in self.second:
                copy.wait_recv()
        else:
            self.direct.wait()


class SumSeq:
    def __init__(self, net, src, came, onward, held):
        self.net, self.src, self.came, self.onward, self.held, self.square = net, src, came, onward, held, net.S == 4
        if not self.square:
            self.direct = Exchange(net, lambda k: src.at[k], lambda k: came.at[k], by_turn=True)
            return
        s, half = net.s, src.shape[1] // 2
        a, b, across = s + 1 - 2 * lax.rem(s, 2), lax.rem(s + 2, 4), 3 - s
        self.ways = (b, a)
        part = lambda k, h: src.at[k, pl.ds(h * half, half)]
        self.first = []
        for h, near in ((0, a), (1, b)):
            for i, block in enumerate((near, across)):
                self.first.append(net.copy(part(block, h), came.at[2 * h + i], net.seq_peer(near)))
        self.second = [net.copy(held.at[h], onward.at[h], net.seq_peer(to)) for h, to in ((0, b), (1, a))]

    def start(self):
        if self.square:
            for i in (1, 3, 0, 2):
                self.net.send(self.first[i])
        else:
            self.direct.start()

    def mid(self):
        if not self.square:
            return
        b, a = self.ways
        half, width = self.held.shape[1:]
        for i in (1, 3):
            self.first[i].wait_recv()

        def body(own, other, o):
            o[...] = (own[...].astype(F32) + other[...].astype(F32)).astype(BF)

        block = (1, half, width)
        stream(
            body,
            (2,),
            [
                (self.src, block, lambda h: (jnp.where(h == 0, b, a), h, 0)),
                (self.came, block, lambda h: (2 * h + 1, 0, 0)),
            ],
            [(self.held, block, lambda h: (h, 0, 0))],
        )
        for copy in self.second:
            self.net.send(copy)

    def wait(self):
        if self.square:
            for i in (0, 2):
                self.first[i].wait_recv()
            for copy in self.second:
                copy.wait_recv()
        else:
            self.direct.wait()

    def ins(self, rows):
        if self.square:
            block = (1, rows, self.src.shape[2])
            return [(self.came, block, lambda i: (2 * i, 0, 0)), (self.onward, block, lambda i: (i, 0, 0))]
        return [(self.came, (self.net.S - 1, rows, self.src.shape[2]), lambda i: (0, i, 0))]


class Line:
    def go(self, part):
        last = self.net.Z - 1
        for t in ([1], range(2, last), [last])[part - 1]:
            self.step(t)


class GatherLine(Line):
    def __init__(self, net, slab, own=None):
        self.net = net
        z, c, last = net.z, net.c, net.Z - 1
        own = slab(net.d) if own is None else own
        self.right, self.left = [], []
        for t in range(net.Z):
            for side, hops in ((1, self.right), (-1, self.left)):
                place = slab(2 * jnp.clip(z - side * t, 0, last) + c)
                src = own if t == 0 else place
                there = z >= t if side == 1 else z <= last - t
                onward = z < last if side == 1 else z > 0
                copy = None if t == last else net.copy(src, place, net.line_peer(z + side))
                core = None if t == 0 and side == -1 else net.copy(src, place, net.partner())
                hops.append((copy, there & onward, core, None if t == 0 else there))

    def early(self):
        self.net.send(self.right[0][0], self.net.z == 0)
        self.net.send(self.left[0][0], self.net.z == self.net.Z - 1)

    def start(self):
        inside = (self.net.z > 0) & (self.net.z < self.net.Z - 1)
        self.net.send(self.right[0][0], inside)
        self.net.send(self.left[0][0], inside)
        self.net.send(self.right[0][2])

    def step(self, t):
        for hops in (self.right, self.left):
            copy, sends, core, there = hops[t]
            run(there, hops[t - 1][0].wait_recv)
            if copy is not None:
                self.net.send(copy, sends)
            self.net.send(core, there)

    def wait(self):
        for hops in (self.right, self.left):
            for _, _, core, there in hops:
                if core is not None:
                    run(there, core.wait_recv)


def add_slabs(dst, left, right):
    blocks, rows = dst.shape[0], dst.shape[1]
    per = rows // 16

    @pl.loop(0, blocks * per)
    def _(i):
        at = (i // per, pl.ds(pl.multiple_of(lax.rem(i, per) * 16, 16), 16), slice(None))
        dst[at] = (left[at].astype(F32) + right[at].astype(F32)).astype(dst.dtype)


class ReduceLine(Line):
    def __init__(self, net, part, own, mate, from_left, from_right):
        self.net, self.own, self.mate, self.bufs = net, own, mate, (from_left, from_right)
        z, c, Z = net.z, net.c, net.Z
        self.order = []
        for t in range((Z + 1) // 2):
            self.order += [Z - 1 - t] + ([t] if t != Z - 1 - t else [])
        self.swaps = {k: net.copy(part(2 * k + 1 - c), mate.at[k], net.partner()) for k in self.order}
        self.loads = {k: net.near(part(2 * k + c), own.at[k]) for k in self.order}
        self.base = net.used
        net.used += 2 * (Z - 1)
        ends = (jnp.clip(Z - 1 - z, 0, Z - 2), jnp.clip(z, 0, Z - 2))
        self.last = [net.near(buf.at[t], mate.at[i]) for i, (buf, t) in enumerate(zip(self.bufs, ends))]

    def start(self):
        for k in self.order:
            self.net.send(self.swaps[k])
            self.loads[k].start()

    def hop(self, side, t):
        net, last = self.net, self.net.Z - 1
        place, way = (last - t, 0) if side == 1 else (t, 1)
        return net.copy_at(
            self.base + way * last + t, self.own.at[place], self.bufs[way].at[t], net.line_peer(net.z + side)
        )

    def pair(self):
        net, done = self.net, set()
        last = net.Z - 1
        right, left = last, 0
        for k in self.order:
            self.loads[k].wait()
            self.swaps[k].wait_recv()
            add_slabs(self.own.at[k], self.own.at[k], self.mate.at[k])
            done.add(k)
            while right > 0 and right in done:
                net.send(self.hop(1, last - right), net.z == 0)
                right -= 1
            while left < last and left in done:
                net.send(self.hop(-1, left), net.z == last)
                left += 1

    def step(self, n):
        net = self.net
        z, last = net.z, net.Z - 1
        for side, far, way in ((1, z, 0), (-1, last - z, 1)):
            t = jnp.clip(n - far, 0, last - 1)
            here = (far >= 1) & (far <= n)
            hop = self.hop(side, t)
            run(here, hop.wait_recv)
            if n < last:
                place, held = last - t if side == 1 else t, self.mate.at[way]
                load = net.near(self.bufs[way].at[t], held)

                def add():
                    load.start()
                    load.wait()
                    add_slabs(self.own.at[place], self.own.at[place], held)

                run(here, add)
                net.send(hop, here)

    def total(self, out=None):
        z, last = self.net.z, self.net.Z - 1
        out = self.own.at[z] if out is None else out
        here = (z > 0, z < last)
        for copy, when in zip(self.last, here):
            run(when, copy.start)
        for copy, when in zip(self.last, here):
            run(when, copy.wait)
        per = out.shape[1] // 16

        def body(ways):
            @pl.loop(0, out.shape[0] * per)
            def _(i):
                at = (i // per, pl.ds(pl.multiple_of(lax.rem(i, per) * 16, 16), 16), slice(None))
                value = self.own.at[z][at].astype(F32)
                for way in ways:
                    value = value + self.mate[(way,) + at].astype(F32)
                out[at] = value.astype(out.dtype)

        run(z == 0, lambda: body((1,)))
        run(z == last, lambda: body((0,)))
        if last > 1:
            run((z > 0) & (z < last), lambda: body((0, 1)))


ANY = pl.BlockSpec(memory_space=pl.ANY)
MIB = 1024 * 1024
HD = 256
shape = jax.ShapeDtypeStruct


def nt(left, right):
    return lax.dot_general(left, right, (((1,), (1,)), ((), ())), preferred_element_type=F32)


def tn(left, right):
    return lax.dot_general(left, right, (((0,), (0,)), ((), ())), preferred_element_type=F32)


def turn(value, cosine, sine):
    half = HD // 8
    first = lax.broadcasted_iota(jnp.int32, value.shape, 1) < half
    other = jnp.where(first, pltpu.roll(value, 128 - half, 1), pltpu.roll(value, half, 1))
    return value * cosine + other * sine


def stream(body, grid, ins, outs):
    def spec(entry):
        block, index = entry[1:3]
        return pl.BlockSpec(block, index, pipeline_mode=pl.Buffered(1)) if len(entry) > 3 else pl.BlockSpec(block, index)

    pltpu.emit_pipeline(
        body, grid=grid, in_specs=[spec(e) for e in ins], out_specs=[spec(e) for e in outs]
    )(*[e[0] for e in ins], *[e[0] for e in outs])


def whole(ref):
    return (ref, ref.shape, lambda *i: (0,) * len(ref.shape), 1)


def chunks(rows, size):
    return lambda body: pl.loop(0, rows // size)(lambda i: body(pl.ds(pl.multiple_of(i * size, size), size), i))


def layer_kernel(seq_n, dp_n, dims, n_ins, n_outs, *refs):
    ins, outs = refs[:n_ins], refs[n_ins : n_ins + n_outs]
    scratch = refs[n_ins + n_outs :]
    x_own, gy_own, up_cut, qkv_cut, out_w, down_w, small, tables = ins
    mixed_out, input_grad, up_out, qkv_out, out_red, down_red, small_red = outs[:7]
    x, qkv_all, out_all, heads, gatt, wide_f, mixed, wide, p_qkv, p_out, qkv_red = outs[7:18]
    mixed_bufs, wide_bufs = outs[18:21], outs[21:24]
    up_all, down_all, slope, p_up, p_down, up_red = [outs[24 + 2 * i : 26 + 2 * i] for i in range(6)]
    hops = outs[36:]
    sems, scratch = scratch[:3], scratch[3:]
    small_v, vec, up_b, qkv_b, doc_row, cols_v, sm, sm_dp, sm_sum, dk_acc, dv_acc = scratch[:11]
    out_f, down_f, tab, gy, n1, n2, hidden, att, gproj = scratch[11:20]
    scratch = scratch[20:]
    mean_at, inv_at, doc_at = [slice(k, k + 1) for k in range(3)]
    grad_up = n1
    L, D, ff, H, r, ro, rd = dims
    hd = HD
    T, CH = (HD, 512) if L <= 1024 else (HD // 2, 256)
    l, ffh, rdh, half_n = H * hd, ff // 2, rd // 2, 2
    net = Net(seq_n, dp_n, *sems)
    S, Z, s, d = net.S, net.Z, net.s, net.d
    tok = L // S
    scale = 1.0 / math.sqrt(hd)
    per = dp_n * r // T
    own_rows = pl.ds(pl.multiple_of(s * tok, tok), tok)

    def lanes(ref):
        return (ref, (ref.shape[0], T), lambda i: (0, i))

    def d_rows(ref):
        return (ref, (1, T // r, r, ref.shape[3]), lambda i: (lax.div(i, per), lax.rem(i, per), 0, 0))

    def reduce(i, part):
        return ReduceLine(net, part, scratch[2 * i], scratch[2 * i + 1], hops[2 * i], hops[2 * i + 1])

    def seq_rows(ref):
        def slot(k, h):
            size = tok if h is None else tok // 2
            return ref.at[pl.ds(pl.multiple_of(k * tok + (h or 0) * size, size), size)]

        return slot

    halves = range(half_n)
    x_g, gy_g = GatherSeq(net, x_own, seq_rows(x)), GatherSeq(net, gy_own, seq_rows(gy))
    su = [Exchange(net, lambda k, h=h: up_cut.at[h, k], lambda k, h=h: up_all[h].at[k, d]) for h in halves]
    sq = Exchange(net, lambda k: qkv_cut.at[k], lambda k: qkv_all.at[k, d])
    o_g = GatherLine(net, lambda k: out_all.at[k], out_w)
    q_g = GatherLine(net, lambda k: qkv_all.at[:, k])
    u_g = [GatherLine(net, lambda k, h=h: up_all[h].at[:, k]) for h in halves]
    down_rows = [down_w.at[pl.ds(h * rdh, rdh)] for h in halves]
    d_g = [GatherLine(net, lambda k, h=h: down_all[h].at[k], down_rows[h]) for h in halves]
    ds = [reduce(h, lambda k, h=h: p_down[h].at[pl.ds(k, 1)]) for h in halves]
    us = [reduce(2 + h, lambda k, h=h: p_up[h].at[:, k]) for h in halves]
    qs = reduce(4, lambda k: p_qkv.at[:, k])
    os = reduce(5, lambda k: p_out.at[pl.ds(k, 1)])
    mx = SumSeq(net, mixed, *mixed_bufs)
    wx = SumSeq(net, wide, *wide_bufs)
    qx = Exchange(net, lambda k: qs.own.at[net.z, k], lambda k: qkv_red.at[k], own=True)
    ux = [Exchange(net, lambda k, h=h: us[h].own.at[net.z, k], lambda k, h=h: up_red[h].at[k], own=True) for h in halves]
    sf = Exchange(net, lambda k: small_v.at[s], lambda k: small_v.at[k])
    sm_x = Exchange(net, lambda k: sm_sum, lambda k: small_red.at[k], own=True)
    small_to = [lax.rem(d + k, dp_n) for k in range(1, dp_n)]
    small_from = [lax.rem(d + dp_n - k, dp_n) for k in range(1, dp_n)]
    sf_dp = [net.copy(small, small_v.at[s, d], (s, to)) for to in small_to]
    sm_to = [net.copy(sm, sm_dp.at[d], (s, to)) for to in small_to]
    sf_own = net.near(small, small_v.at[s, d])
    spot = lambda at, rows, width: n1.at[pl.ds(at, rows), pl.ds(0, width)]
    loc = Place(
        net,
        [(gy_own, gy.at[own_rows]), (tables, tab)],
        [(up_cut.at[h, s], spot(tok + ro + h * r, r, ffh), up_all[h].at[s, d]) for h in halves]
        + [(qkv_cut.at[s], spot(tok + ro + 2 * r, r, 3 * l), qkv_all.at[s, d])]
        + [(x_own, spot(0, tok, D), x.at[own_rows]), (out_w, spot(tok, ro, D), out_all.at[d])]
        + [(down_rows[h], scratch[2 * h].at[0, 0], down_all[h].at[d]) for h in halves],
    )
    out_copies = [net.near(out_f, out_red)] + [net.near(down_f, down_red.at[:, pl.ds(h * rdh, rdh)]) for h in halves]
    begun = []

    def out_total():
        os.total(out_f)
        out_copies[0].start()

    def down_total(h):
        for copy in begun:
            copy.wait()
        ds[h].total(down_f)
        out_copies[1 + h].start()
        begun[:] = [out_copies[1 + h]]

    def small_first():
        sf_own.start()
        for copy in sf_dp:
            net.send(copy)

    def small_second():
        sf_own.wait()
        for copy in sf_dp:
            copy.wait_recv()
        sf.start()

    def sums_first():
        for copy in sm_to:
            net.send(copy)

    def sums_second():
        sm_sum[...] = sm[...]
        for copy, source in zip(sm_to, small_from):
            copy.wait_recv()
            sm_sum[...] += sm_dp[source]
        sm_x.start()

    def pieces(out, row, found):
        lane = lax.broadcasted_iota(jnp.int32, (1, 128), 1) // r
        q = 128 // r
        for p in range(len(found) // q):
            value = small_v[found[p * q]]
            for k in range(1, q):
                value = jnp.where(lane == k, small_v[found[p * q + k]], value)
            out[row : row + 1, 128 * p : 128 * p + 128] = value

    def unpack():
        sf.wait()
        for j in range(5):
            pieces(vec, j, [(i // dp_n, i % dp_n, slice(j, j + 1)) for i in range(seq_n * dp_n)])
        for h in halves:
            pieces(up_b, h, [(s, m // 2, slice(8 + 2 * h + m % 2, 9 + 2 * h + m % 2)) for m in range(2 * dp_n)])
        found = []
        for j in range(3):
            for m in range(l // r):
                piece = j * (D // r) + s * (l // r) + m
                owner = lax.div(piece, 3)
                found.append((lax.div(owner, dp_n), lax.rem(owner, dp_n), pl.ds(5 + lax.rem(piece, 3), 1)))
        pieces(qkv_b, 0, found)
        for k in range(S):
            for j in range(tok // 128):
                row = small_v[k, d, 12 + j : 13 + j]
                at = k * tok + j * 128
                doc_row[0:1, at : at + 128] = row
                cols_v[at : at + 128, :] = jnp.transpose(jnp.broadcast_to(row, (128, 128)))
        sm[...] = jnp.zeros_like(sm)
        sm[4:5, :] = jnp.sum(gy[own_rows, :].astype(F32), 0, keepdims=True)

    def cols_of(base=0):
        return pl.ds(pl.multiple_of(base + pl.program_id(0) * T, T), T)

    def norm_phase():
        def body(xb):
            i = pl.program_id(0)
            at = pl.ds(pl.multiple_of(i * T, T), T)
            wide_x = xb[...].astype(F32)
            mean = jnp.mean(wide_x, -1, keepdims=True)
            center = wide_x - mean
            inv = lax.rsqrt(jnp.mean(center * center, -1, keepdims=True) + epsilon)
            cols_v[at, mean_at] = mean
            cols_v[at, inv_at] = inv
            hat = center * inv
            n1[at, :] = (hat * vec[0:1, :] + vec[1:2, :]).astype(BF)
            n2[at, :] = (hat * vec[2:3, :] + vec[3:4, :]).astype(BF)

        stream(body, (L // T,), [(x, (T, D), lambda i: (i, 0))], [])

    def up_phase(h):
        def body(w, slo):
            cols = cols_of(h * ffh)
            bias = up_b[h : h + 1, cols_of()]

            @chunks(L, CH)
            def _(at, i):
                u = dot(n2[at, :], w[...].reshape(D, T)) + bias
                phi = 0.5 + 0.5 * lax.erf(u * math.sqrt(0.5))
                hidden[at, cols] = (u * phi).astype(BF)
                slo[at, :] = (phi + u * (jnp.exp(-0.5 * u * u) * (1.0 / math.sqrt(2.0 * math.pi)))).astype(BF)

        stream(body, (ffh // T,), [(up_all[h], (S, dp_n, r, T), lambda i: (0, 0, 0, i))], [lanes(slope[h])])

    def outer_phase(left, base, n, right, out):
        def body(o):
            width = o.shape[-1]
            step = min(width, 1024)

            @chunks(width, step)
            def _(at, j):
                value = tn(left[:, cols_of(base)], right[:, at])
                o[(slice(None),) * (len(o.shape) - 1) + (at,)] = value.astype(BF).reshape(o.shape[:-1] + (step,))

        if len(out.shape) == 3:
            target = (out, (T // out.shape[1], out.shape[1], D), lambda i: (i, 0, 0))
        else:
            target = d_rows(out)
        stream(body, (n,), [], [target])

    def down_grad_phase(h):
        outer_phase(hidden, h * ffh, ffh // T, gy, p_down[h])

    def up_grad_phase(h):
        outer_phase(n2, 0, D // T, grad_up.at[:, pl.ds(h * ffh, ffh)], p_up[h])

    def out_grad_phase():
        outer_phase(att, 0, l // T, gy, p_out)

    def qkv_grad_phase():
        def body(o):
            for j in range(3):
                o[:, :, :, j * l : (j + 1) * l] = tn(n1[:, cols_of()], gproj[j]).astype(BF).reshape(o.shape[:-1] + (l,))

        for j in range(3):
            sm[6:7, j * l : (j + 1) * l] = jnp.sum(gproj[j].astype(F32), 0, keepdims=True)
        stream(body, (D // T,), [], [d_rows(p_qkv)])

    def gatt_phase():
        def body(w, o):
            @chunks(L, CH)
            def _(at, i):
                o[0, at, :] = nt(gy[at, :], w[...].reshape(hd, D)).astype(BF)

        w = (out_all, (hd // ro, ro, D), lambda i: (i, 0, 0))
        stream(body, (H,), [w], [(gatt, (1, L, hd), lambda i: (i, 0, 0))])

    def qkv_phase():
        def body(w, o):
            j = pl.program_id(0)
            bias = qkv_b[0:1, pl.ds(pl.multiple_of(j * hd, hd), hd)]

            @chunks(L, CH)
            def _(at, i):
                p = dot(n1[at, :], w[...].reshape(D, hd)) + bias
                o[0, at, 128:] = p[:, 128:].astype(BF)

                @pl.when(j < 2 * H)
                def _():
                    o[0, at, :128] = turn(p[:, :128], tab[0, at, :], tab[1, at, :]).astype(BF)

                @pl.when(j >= 2 * H)
                def _():
                    o[0, at, :128] = p[:, :128].astype(BF)

        w = (qkv_all, (S, dp_n, r, hd), lambda i: (0, 0, 0, i))
        stream(body, (3 * H,), [w], [(heads, (1, L, hd), lambda i: (i, 0, 0))])

    def att_phase():
        def body(q, k, v, ga):
            h, i = pl.program_id(0), pl.program_id(1)
            cols = pl.ds(pl.multiple_of(h * hd, hd), hd)
            low = pl.ds(pl.multiple_of(h * hd, hd), 128)
            high = pl.ds(pl.multiple_of(h * hd + 128, 128), 128)
            back = lambda t, rows: turn(t, tab[0, rows, :], -tab[1, rows, :])

            @pl.when(i == 0)
            def _():
                dk_acc[...] = jnp.zeros_like(dk_acc)
                dv_acc[...] = jnp.zeros_like(dv_acc)

            def tile(c):
                n = (c + 1) * T
                at = slice(c * T, n)
                qt, kt, vt, gt = q[0], k[0, :n], v[0, :n], ga[0]
                query = lax.broadcasted_iota(jnp.int32, (T, n), 0) + c * T
                key = lax.broadcasted_iota(jnp.int32, (T, n), 1)
                allowed = (cols_v[at, doc_at] == doc_row[0:1, :n]) & (key <= query)
                raw = jnp.where(allowed, nt(qt, kt) * scale, -1000000000.0)
                e = jnp.exp(raw - jnp.max(raw, -1, keepdims=True))
                p = e / jnp.sum(e, -1, keepdims=True)
                pb = p.astype(BF)
                att[at, cols] = dot(pb, vt).astype(BF)
                gp = nt(gt, vt)
                gs = (p * (gp - jnp.sum(gp * p, -1, keepdims=True))).astype(BF)
                gq = dot(gs, kt) * scale
                gproj[0, at, low] = back(gq[:, :128], at).astype(BF)
                gproj[0, at, high] = gq[:, 128:].astype(BF)
                dk_acc[:n, :] += tn(gs, qt)
                dv_acc[:n, :] += tn(pb, gt)

            for c in range(L // T):
                pl.when(i == c)(functools.partial(tile, c))

            @pl.when(i == L // T - 1)
            def _():
                gk = dk_acc[...] * scale
                gproj[1, :, low] = back(gk[:, :128], slice(None)).astype(BF)
                gproj[1, :, high] = gk[:, 128:].astype(BF)
                gproj[2, :, cols] = dv_acc[...].astype(BF)

        block = (1, T, hd)
        full = (1, L, hd)
        stream(
            body,
            (H, L // T),
            [
                (heads, block, lambda h, i: (h, i, 0)),
                (heads, full, lambda h, i: (H + h, 0, 0)),
                (heads, full, lambda h, i: (2 * H + h, 0, 0)),
                (gatt, block, lambda h, i: (h, i, 0)),
            ],
            [],
        )

    def norm_sums(grad, xb, at, row):
        cols = cols_of()
        hat = (xb[at, :].astype(F32) - cols_v[at, mean_at]) * cols_v[at, inv_at]
        sm[row : row + 1, cols] += jnp.sum(grad * hat, 0, keepdims=True)
        sm[row + 1 : row + 2, cols] += jnp.sum(grad, 0, keepdims=True)

    def one_phase():
        def body(w, xb, o):
            @chunks(L, CH)
            def _(at, m):
                grad = 0.0
                for j in range(3):
                    grad = grad + nt(gproj[j, at, :], w[:, :, :, j * l : (j + 1) * l].reshape(T, l))
                norm_sums(grad, xb, at, 0)
                o[at, :] = grad * vec[0:1, cols_of()]

        stream(body, (D // T,), [d_rows(qkv_all), lanes(x)], [lanes(wide_f)])

    per_ch = max(1, CH // tok)

    def two_phase():
        def body(wa, wb, xb, first, o):
            @chunks(L, per_ch * tok)
            def _(at, m):
                grad = nt(grad_up[at, :ffh], wa[...].reshape(T, ffh)) + nt(grad_up[at, ffh:ff], wb[...].reshape(T, ffh))
                norm_sums(grad, xb, at, 2)
                value = first[at, :] + grad * vec[2:3, cols_of()]
                o[pl.ds(m * per_ch, per_ch)] = value.astype(BF).reshape(per_ch, tok, T)

        stream(
            body,
            (D // T,),
            [d_rows(up_all[0]), d_rows(up_all[1]), lanes(x), lanes(wide_f)],
            [(wide, (S, tok, T), lambda i: (0, 0, i))],
        )

    def mixed_phase():
        def body(wa, wb, wo, o):
            @chunks(L, per_ch * tok)
            def _(at, m):
                value = dot(hidden[at, :ffh], wa[...].reshape(ffh, T)) + dot(hidden[at, ffh:], wb[...].reshape(ffh, T))
                value = value + dot(att[at, :], wo[...].reshape(l, T))
                o[pl.ds(m * per_ch, per_ch)] = value.astype(BF).reshape(per_ch, tok, T)

        cols = lambda ref: (ref, ref.shape[:2] + (T,), lambda i: (0, 0, i))
        ws = [cols(down_all[0]), cols(down_all[1]), cols(out_all)]
        stream(body, (D // T,), ws, [(mixed, (S, tok, T), lambda i: (0, 0, i))])

    def slope_phase(h):
        def body(w, slo):
            cols = cols_of(h * ffh)

            @chunks(L, CH)
            def _(at, m):
                gu = (nt(gy[at, :], w[...].reshape(T, D)) * slo[at, :].astype(F32)).astype(BF)
                grad_up[at, cols] = gu
                sm[5:6, cols] += jnp.sum(gu.astype(F32), 0, keepdims=True)

        w = (down_all[h], (T // rdh, rdh, D), lambda i: (i, 0, 0))
        stream(body, (ffh // T,), [w, lanes(slope[h])], [])

    ends = 2 if mx.square else 8
    part = tok // ends
    tiles = lambda ref, lead: (ref, (lead, part, D), lambda i: (0, i, 0))
    mine = lambda ref: (ref, (part, D), lambda i: (i, 0))

    def total_of(own, came):
        total = own[0].astype(F32)
        for ref in came:
            for k in range(ref.shape[0]):
                total = total + ref[k].astype(F32)
        return total

    def mixed_end():
        def body(xb, own, *rest):
            rest[-1][0] = (xb[...].astype(F32) + vec[4:5, :] + total_of(own, rest[:-1])).astype(BF)

        stream(body, (ends,), [mine(x_own), tiles(mixed.at[pl.ds(s, 1)], 1)] + mx.ins(part), [tiles(mixed_out, 1)])

    def input_end():
        def body(xb, gb, own, *rest):
            at = pl.ds(pl.multiple_of(s * tok + pl.program_id(0) * part, part), part)
            inv = cols_v[at, inv_at]
            hat = (xb[...].astype(F32) - cols_v[at, mean_at]) * inv
            total = total_of(own, rest[:-1])
            total = total - jnp.mean(total, -1, keepdims=True) - hat * jnp.mean(total * hat, -1, keepdims=True)
            rest[-1][0] = gb[...].astype(F32) + inv * total

        ins = [mine(x_own), mine(gy_own), tiles(wide.at[pl.ds(s, 1)], 1)] + wx.ins(part)
        stream(body, (ends,), ins, [tiles(input_grad, 1)])

    def qkv_end():
        def body(a, *o):
            for j in range(3):
                o[j][...] = a[0, :, j * l : (j + 1) * l].astype(F32)

        targets = [qkv_out.at[:, pl.ds(j * S * l, S * l)] for j in range(3)]
        stream(body, (S,), [(qkv_red, (1, r, 3 * l), lambda k: (k, 0, 0))], [(t, (r, l), lambda k: (0, k)) for t in targets])

    def up_end():
        def body(a, b, o):
            for k in range(dp_n):
                for h, src in enumerate((a, b)):
                    o[:, k * rd + h * rdh : k * rd + (h + 1) * rdh] = src[0, :, k * rdh : (k + 1) * rdh].astype(F32)

        block = lambda ref: (ref, (1, r, ffh), lambda k: (k, 0, 0))
        stream(body, (S,), [block(up_red[0]), block(up_red[1])], [(up_out, (r, ff), lambda k: (0, k))])

    net.barrier()
    loc.start()
    small_first()
    o_g.early()
    o_g.start()
    sq.start()
    o_g.go(1)
    x_g.start()
    loc.finish()
    sq.wait()
    q_g.early()
    q_g.start()
    su[0].start()
    o_g.go(2)
    o_g.go(3)
    d_g[1].early()
    q_g.go(1)
    small_second()
    x_g.relay()
    gy_g.start()
    q_g.go(2)
    o_g.wait()
    su[0].wait()
    u_g[0].early()
    x_g.wait()
    unpack()
    norm_phase()
    d_g[1].start()
    u_g[0].start()
    q_g.go(3)
    gy_g.relay()
    su[1].start()
    d_g[0].early()
    d_g[0].start()
    q_g.wait()
    qkv_phase()
    gy_g.wait()
    gatt_phase()
    su[1].wait()
    u_g[1].early()
    att_phase()
    u_g[1].start()
    out_grad_phase()
    os.start()
    u_g[0].go(1)
    os.pair()
    d_g[0].go(1)
    qkv_grad_phase()
    qs.start()
    os.go(1)
    qs.pair()
    u_g[0].go(2)
    one_phase()
    d_g[0].go(2)
    u_g[0].go(3)
    u_g[1].go(1)
    u_g[0].wait()
    up_phase(0)
    qs.go(1)
    d_g[0].go(3)
    down_grad_phase(0)
    ds[0].start()
    d_g[0].wait()
    slope_phase(0)
    ds[0].pair()
    u_g[1].go(2)
    d_g[1].go(1)
    up_grad_phase(0)
    u_g[1].go(3)
    d_g[1].go(2)
    u_g[1].wait()
    us[0].start()
    up_phase(1)
    d_g[1].go(3)
    ds[0].go(1)
    qs.go(2)
    us[0].pair()
    d_g[1].wait()
    mixed_phase()
    os.go(2)
    mx.start()
    slope_phase(1)
    qs.go(3)
    us[0].go(1)
    up_grad_phase(1)
    us[1].start()
    qs.total()
    qx.start()
    ds[0].go(2)
    us[1].pair()
    mx.mid()
    us[0].go(2)
    two_phase()
    sums_first()
    ds[0].go(3)
    wx.start()
    us[1].go(1)
    down_grad_phase(1)
    ds[1].start()
    sums_second()
    ds[1].pair()
    us[0].go(3)
    mx.wait()
    us[0].total()
    ux[0].start()
    mixed_end()
    down_total(0)
    us[1].go(2)
    wx.mid()
    os.go(3)
    qx.wait()
    ds[1].go(1)
    out_total()
    ux[0].wait()
    us[1].go(3)
    qkv_end()
    us[1].total()
    ux[1].start()
    ds[1].go(2)
    wx.wait()
    input_end()
    ux[1].wait()
    up_end()
    ds[1].go(3)
    down_total(1)
    sm_x.wait()
    for copy in [out_copies[0]] + begun:
        copy.wait()
    net.drain()


def layer(seq_n, dp_n, dims, args):
    L, D, ff, H, r, ro, rd = dims
    l, Z, ffh, rdh = H * HD, dp_n // 2, ff // 2, rd // 2
    tok = L // seq_n
    seq_tok, up_slab, qkv_slab = (seq_n, tok, D), (seq_n, r, ffh), (seq_n, r, 3 * l)
    outs = [((1, tok, D), BF), ((1, tok, D), F32), ((r, seq_n * ff), F32), ((r, seq_n * 3 * l), F32)]
    outs += [((1, ro, D), F32), ((1, rd, D), F32), ((seq_n, 8, D), F32)]
    outs += [((L, D), BF), ((seq_n, dp_n, r, 3 * l), BF), ((dp_n, ro, D), BF), ((3 * H, L, HD), BF), ((H, L, HD), BF)]
    outs += [((L, D), F32), (seq_tok, BF), (seq_tok, BF), ((seq_n, dp_n, r, 3 * l), BF), ((dp_n, ro, D), BF), (qkv_slab, BF)]
    half = tok // 2
    if seq_n == 4:
        outs += [((4, half, D), BF), ((2, half, D), BF), ((2, half, D), BF)] * 2
    else:
        outs += [((seq_n - 1, tok, D), BF), ((16, 128), BF), ((16, 128), BF)] * 2
    up_full, down_full = (seq_n, dp_n, r, ffh), (dp_n, rdh, D)
    for v in (up_full, down_full, (L, ffh), up_full, down_full, up_slab):
        outs += [(v, BF)] * 2
    slabs = [(1, rdh, D)] * 2 + [up_slab] * 2 + [qkv_slab, (1, ro, D)]
    for slab in slabs:
        outs += [((Z - 1,) + slab, BF)] * 2
    out_shape = [shape(*o) for o in outs]
    n = 6 * (4 * Z - 3) + 6 * (3 * Z - 2) + 12 * (seq_n - 1) + 2 * max(4, seq_n - 1) + 2 * (dp_n - 1)
    vmem = [((seq_n, dp_n, 16, 128), F32), ((8, D), F32), ((8, ffh), F32), ((8, 3 * l), F32), ((8, L), F32), ((L, 128), F32)]
    vmem += [((8, D), F32), ((dp_n, 8, D), F32), ((8, D), F32), ((L, HD), F32), ((L, HD), F32)]
    vmem += [((1, ro, D), F32), ((1, rdh, D), F32), ((2, L, 128), F32)]
    vmem += [((L, D), BF), ((L, D), BF), ((L, D), BF), ((L, ff), BF), ((L, l), BF), ((3, L, l), BF)]
    for slab in slabs:
        vmem += [((Z,) + slab, BF)] * 2
    scratch = [pltpu.SemaphoreType.DMA((k,)) for k in (n, n, 32 + 6 * (3 * Z - 2))] + [pltpu.VMEM(*v) for v in vmem]
    return pl.pallas_call(
        functools.partial(layer_kernel, seq_n, dp_n, dims, len(args), len(outs)),
        out_shape=out_shape,
        in_specs=[ANY] * len(args),
        out_specs=[ANY] * len(outs),
        scratch_shapes=scratch,
        compiler_params=pltpu.CompilerParams(collective_id=0, has_side_effects=True, vmem_limit_bytes=62 * MIB),
        name="layer",
    )(*args)[:7]


def shards(
    tokens,
    doc_ids,
    ln1_gain,
    ln1_bias,
    ln2_gain,
    ln2_bias,
    qkv_weight,
    qkv_bias,
    out_weight,
    up_weight,
    up_bias,
    down_weight,
    out_bias,
    cotangent,
):
    seq_n = lax.axis_size("seq")
    dp_n = lax.axis_size("dp")
    seq_i = lax.axis_index("seq")
    tok_rows, width = tokens.shape[1:]
    length = tok_rows * seq_n
    head_dim = width // HEADS
    heads = HEADS // seq_n
    local = heads * head_dim
    ff = up_weight.shape[1] // seq_n
    rot_dims = head_dim // 4
    rows, ff_half = qkv_weight.shape[0], ff // 2
    per_down = down_weight.shape[0]
    qkv_cut = qkv_weight.reshape(rows, 3, seq_n, local).transpose(2, 0, 1, 3).reshape(seq_n, rows, 3 * local)
    up_cut = up_weight.reshape(rows, seq_n, dp_n, 2, per_down // 2).transpose(3, 1, 0, 2, 4)
    up_cut = up_cut.reshape(2, seq_n, rows, ff_half)
    pieces = jnp.concatenate([ln1_gain, ln1_bias, ln2_gain, ln2_bias, out_bias, qkv_bias, up_bias]).reshape(-1, rows)
    pieces = jnp.tile(pieces.astype(F32), (1, 128 // rows))
    docs = doc_ids.astype(F32).reshape(-1, 128)
    small = jnp.concatenate([pieces, docs, jnp.zeros((16 - pieces.shape[0] - docs.shape[0], 128), F32)])
    mixed, input_grad, up_grad, qkv_grad, out_grad, down_grad, sums = layer(
        seq_n,
        dp_n,
        (length, width, ff, heads, rows, out_weight.shape[0], per_down),
        (
            tokens[0],
            cotangent[0],
            up_cut,
            qkv_cut,
            out_weight,
            down_weight,
            small,
            jnp.asarray(rotary_rows(length, rot_dims)),
        ),
    )
    n = seq_n * dp_n
    place = seq_i * dp_n + lax.axis_index("dp")

    def mine(vector):
        return lax.dynamic_index_in_dim(vector.reshape(n, -1), place, 0, False)

    lns = jnp.sum(sums[:, :5], 0)
    g1, b1, g2, b2, ob = [mine(lns[k]) for k in range(5)]
    ub = mine(sums[:, 5, :ff].reshape(seq_n, 2, dp_n, -1).transpose(0, 2, 1, 3))
    qb = mine(sums[:, 6, : 3 * local].reshape(seq_n, 3, local).transpose(1, 0, 2))
    return (mixed, input_grad, g1, b1, g2, b2, qkv_grad, qb, out_grad[0], up_grad, ub, down_grad[0], ob)


def solution(mesh):
    in_specs = (
        P("dp", "seq", None),
        P("dp", "seq"),
        P(("seq", "dp")),
        P(("seq", "dp")),
        P(("seq", "dp")),
        P(("seq", "dp")),
        P(("seq", "dp"), None),
        P(("seq", "dp")),
        P(("seq", "dp"), None),
        P(("seq", "dp"), None),
        P(("seq", "dp")),
        P(("seq", "dp"), None),
        P(("seq", "dp")),
        P("dp", "seq", None),
    )
    out_specs = (
        P("dp", "seq", None),
        P("dp", "seq", None),
        P(("seq", "dp")),
        P(("seq", "dp")),
        P(("seq", "dp")),
        P(("seq", "dp")),
        P(("seq", "dp"), None),
        P(("seq", "dp")),
        P(("seq", "dp"), None),
        P(("seq", "dp"), None),
        P(("seq", "dp")),
        P(("seq", "dp"), None),
        P(("seq", "dp")),
    )
    return jax.shard_map(shards, mesh=mesh, in_specs=in_specs, out_specs=out_specs, check_vma=False)
```

```python
import functools
import math

import jax
import jax.numpy as jnp
import numpy as np
from jax import lax
from jax.experimental import pallas as pl
from jax.experimental.pallas import tpu as pltpu
from jax.sharding import PartitionSpec as P

HEADS = 8
BF = jnp.bfloat16
F32 = jnp.float32


epsilon = 1e-05


def rotary_rows(length, rot_dims):
    half = rot_dims // 2
    exponents = np.arange(half, dtype=np.float32) * np.float32(2.0 / rot_dims)
    inverse = np.power(np.float32(10000.0), -exponents).astype(np.float32)
    phase = (np.arange(length, dtype=np.float32)[:, None] * inverse[None, :]).astype(np.float64)
    tables = np.zeros((2, length, 128), np.float32)
    tables[0] = 1.0
    tables[0, :, :half] = tables[0, :, half:rot_dims] = np.cos(phase)
    tables[1, :, :half] = -np.sin(phase)
    tables[1, :, half:rot_dims] = np.sin(phase)
    return tables


def dot(left, right):
    return jnp.dot(left, right, preferred_element_type=F32)


MESH = pl.DeviceIdType.MESH


def run(when, action):
    if when is None:
        action()
    else:
        pl.when(when)(lambda: action())


class Net:
    def __init__(self, seq_n, dp_n, send_sems, recv_sems, local_sems):
        self.S, self.DP, self.Z = seq_n, dp_n, dp_n // 2
        self.s, self.d = lax.axis_index("seq"), lax.axis_index("dp")
        self.z, self.c = self.d // 2, lax.rem(self.d, 2)
        self.send_sems, self.recv_sems, self.used = send_sems, recv_sems, 0
        self.local_sems, self.local_used = local_sems, 0
        self.sent = []

    def seq_peer(self, s):
        return (s, self.d)

    def line_peer(self, z):
        return (self.s, 2 * jnp.clip(z, 0, self.Z - 1) + self.c)

    def partner(self):
        return (self.s, 2 * self.z + 1 - self.c)

    def copy(self, src, dst, device):
        self.used += 1
        return self.copy_at(self.used - 1, src, dst, device)

    def copy_at(self, i, src, dst, device):
        return pltpu.make_async_remote_copy(
            src_ref=src,
            dst_ref=dst,
            send_sem=self.send_sems.at[i],
            recv_sem=self.recv_sems.at[i],
            device_id=device,
            device_id_type=MESH,
        )

    def send(self, copy, when=None):
        self.sent.append((copy, when))
        run(when, copy.start)

    def drain(self):
        for copy, when in self.sent:
            run(when, copy.wait_send)

    def near(self, src, dst):
        self.local_used += 1
        return pltpu.make_async_copy(src, dst, self.local_sems.at[self.local_used - 1])

    def barrier(self):
        sem = pltpu.get_barrier_semaphore()
        peers = [self.seq_peer(lax.rem(self.s + k, self.S)) for k in range(1, self.S)]
        peers += [(self.s, lax.rem(self.d + k, self.DP)) for k in range(1, self.DP)]
        for device in peers:
            pl.semaphore_signal(sem, inc=1, device_id=device, device_id_type=MESH)
        pl.semaphore_wait(sem, len(peers))


class Place:
    def __init__(self, net, direct, through):
        self.direct = [net.near(src, dst) for src, dst in direct]
        self.loads = [net.near(src, buf) for src, buf, _ in through]
        self.stores = [net.near(buf, dst) for _, buf, dst in through]

    def start(self):
        for copy in self.loads + self.direct:
            copy.start()

    def finish(self):
        for load, store in zip(self.loads, self.stores):
            load.wait()
            store.start()
        for copy in self.stores + self.direct:
            copy.wait()


class Exchange:
    def __init__(self, net, src, slot, by_turn=False, own=False, settle=False):
        self.net, self.copies, self.settle = net, [], settle
        for k in range(1, net.S):
            to = lax.rem(net.s + k, net.S)
            self.copies.append(net.copy(src(to), slot(k - 1 if by_turn else net.s), net.seq_peer(to)))
        self.own = net.near(src(net.s), slot(net.s)) if own else None

    def start(self):
        for copy in self.copies:
            if self.settle:
                copy.start()
            else:
                self.net.send(copy)
        if self.own is not None:
            self.own.start()

    def wait(self):
        for copy in self.copies:
            copy.wait_recv()
            if self.settle:
                copy.wait_send()
        if self.own is not None:
            self.own.wait()


class GatherSeq:
    def __init__(self, net, src, slot):
        self.net, self.square = net, net.S == 4
        if self.square:
            s = net.s
            a, b = s + 1 - 2 * lax.rem(s, 2), lax.rem(s + 2, 4)
            self.first = [net.copy(src, slot(s, None), net.seq_peer(p)) for p in (a, b)]
            self.second = [
                net.copy(slot(a, 0), slot(a, 0), net.seq_peer(b)),
                net.copy(slot(b, 1), slot(b, 1), net.seq_peer(a)),
            ]
        else:
            self.direct = Exchange(net, lambda to: src, lambda k: slot(k, None))

    def start(self):
        if self.square:
            for copy in self.first:
                self.net.send(copy)
        else:
            self.direct.start()

    def relay(self):
        if self.square:
            for came, onward in zip(self.first, self.second):
                came.wait_recv()
                self.net.send(onward)

    def wait(self):
        if self.square:
            for copy in self.second:
                copy.wait_recv()
        else:
            self.direct.wait()


class SumSeq:
    def __init__(self, net, src, came, onward, held):
        self.net, self.src, self.came, self.onward, self.held, self.square = net, src, came, onward, held, net.S == 4
        if not self.square:
            self.direct = Exchange(net, lambda k: src.at[k], lambda k: came.at[k], by_turn=True)
            return
        s, half = net.s, src.shape[1] // 2
        a, b, across = s + 1 - 2 * lax.rem(s, 2), lax.rem(s + 2, 4), 3 - s
        self.ways = (b, a)
        part = lambda k, h: src.at[k, pl.ds(h * half, half)]
        self.first = []
        for h, near in ((0, a), (1, b)):
            for i, block in enumerate((near, across)):
                self.first.append(net.copy(part(block, h), came.at[2 * h + i], net.seq_peer(near)))
        self.second = [net.copy(held.at[h], onward.at[h], net.seq_peer(to)) for h, to in ((0, b), (1, a))]

    def start(self):
        if self.square:
            for i in (1, 3, 0, 2):
                self.net.send(self.first[i])
        else:
            self.direct.start()

    def mid(self):
        if not self.square:
            return
        b, a = self.ways
        half, width = self.held.shape[1:]
        for i in (1, 3):
            self.first[i].wait_recv()

        def body(own, other, o):
            o[...] = (own[...].astype(F32) + other[...].astype(F32)).astype(BF)

        block = (1, half, width)
        stream(
            body,
            (2,),
            [
                (self.src, block, lambda h: (jnp.where(h == 0, b, a), h, 0)),
                (self.came, block, lambda h: (2 * h + 1, 0, 0)),
            ],
            [(self.held, block, lambda h: (h, 0, 0))],
        )
        for copy in self.second:
            self.net.send(copy)

    def wait(self):
        if self.square:
            for i in (0, 2):
                self.first[i].wait_recv()
            for copy in self.second:
                copy.wait_recv()
        else:
            self.direct.wait()

    def ins(self, rows):
        if self.square:
            block = (1, rows, self.src.shape[2])
            return [(self.came, block, lambda i: (2 * i, 0, 0)), (self.onward, block, lambda i: (i, 0, 0))]
        return [(self.came, (self.net.S - 1, rows, self.src.shape[2]), lambda i: (0, i, 0))]


class Line:
    def go(self, part):
        last = self.net.Z - 1
        for t in ([1], range(2, last), [last])[part - 1]:
            self.step(t)


class GatherLine(Line):
    def __init__(self, net, slab, own=None):
        self.net = net
        z, c, last = net.z, net.c, net.Z - 1
        own = slab(net.d) if own is None else own
        self.right, self.left = [], []
        for t in range(net.Z):
            for side, hops in ((1, self.right), (-1, self.left)):
                place = slab(2 * jnp.clip(z - side * t, 0, last) + c)
                src = own if t == 0 else place
                there = z >= t if side == 1 else z <= last - t
                onward = z < last if side == 1 else z > 0
                copy = None if t == last else net.copy(src, place, net.line_peer(z + side))
                core = None if t == 0 and side == -1 else net.copy(src, place, net.partner())
                hops.append((copy, there & onward, core, None if t == 0 else there))

    def early(self):
        self.net.send(self.right[0][0], self.net.z == 0)
        self.net.send(self.left[0][0], self.net.z == self.net.Z - 1)

    def start(self):
        inside = (self.net.z > 0) & (self.net.z < self.net.Z - 1)
        self.net.send(self.right[0][0], inside)
        self.net.send(self.left[0][0], inside)
        self.net.send(self.right[0][2])

    def step(self, t):
        for hops in (self.right, self.left):
            copy, sends, core, there = hops[t]
            run(there, hops[t - 1][0].wait_recv)
            if copy is not None:
                self.net.send(copy, sends)
            self.net.send(core, there)

    def wait(self):
        for hops in (self.right, self.left):
            for _, _, core, there in hops:
                if core is not None:
                    run(there, core.wait_recv)


def add_slabs(dst, left, right):
    blocks, rows = dst.shape[0], dst.shape[1]
    per = rows // 16

    @pl.loop(0, blocks * per)
    def _(i):
        at = (i // per, pl.ds(pl.multiple_of(lax.rem(i, per) * 16, 16), 16), slice(None))
        dst[at] = (left[at].astype(F32) + right[at].astype(F32)).astype(dst.dtype)


class ReduceLine(Line):
    def __init__(self, net, part, own, mate, from_left, from_right):
        self.net, self.own, self.mate, self.bufs = net, own, mate, (from_left, from_right)
        z, c, Z = net.z, net.c, net.Z
        self.order = []
        for t in range((Z + 1) // 2):
            self.order += [Z - 1 - t] + ([t] if t != Z - 1 - t else [])
        self.swaps = {k: net.copy(part(2 * k + 1 - c), mate.at[k], net.partner()) for k in self.order}
        self.loads = {k: net.near(part(2 * k + c), own.at[k]) for k in self.order}
        self.base = net.used
        net.used += 2 * (Z - 1)
        ends = (jnp.clip(Z - 1 - z, 0, Z - 2), jnp.clip(z, 0, Z - 2))
        self.last = [net.near(buf.at[t], mate.at[i]) for i, (buf, t) in enumerate(zip(self.bufs, ends))]

    def start(self):
        for k in self.order:
            self.net.send(self.swaps[k])
            self.loads[k].start()

    def hop(self, side, t):
        net, last = self.net, self.net.Z - 1
        place, way = (last - t, 0) if side == 1 else (t, 1)
        return net.copy_at(
            self.base + way * last + t, self.own.at[place], self.bufs[way].at[t], net.line_peer(net.z + side)
        )

    def pair(self):
        net, done = self.net, set()
        last = net.Z - 1
        right, left = last, 0
        for k in self.order:
            self.loads[k].wait()
            self.swaps[k].wait_recv()
            add_slabs(self.own.at[k], self.own.at[k], self.mate.at[k])
            done.add(k)
            while right > 0 and right in done:
                net.send(self.hop(1, last - right), net.z == 0)
                right -= 1
            while left < last and left in done:
                net.send(self.hop(-1, left), net.z == last)
                left += 1

    def step(self, n):
        net = self.net
        z, last = net.z, net.Z - 1
        for side, far, way in ((1, z, 0), (-1, last - z, 1)):
            t = jnp.clip(n - far, 0, last - 1)
            here = (far >= 1) & (far <= n)
            hop = self.hop(side, t)
            run(here, hop.wait_recv)
            if n < last:
                place, held = last - t if side == 1 else t, self.mate.at[way]
                load = net.near(self.bufs[way].at[t], held)

                def add():
                    load.start()
                    load.wait()
                    add_slabs(self.own.at[place], self.own.at[place], held)

                run(here, add)
                net.send(hop, here)

    def total(self, out=None):
        z, last = self.net.z, self.net.Z - 1
        out = self.own.at[z] if out is None else out
        here = (z > 0, z < last)
        for copy, when in zip(self.last, here):
            run(when, copy.start)
        for copy, when in zip(self.last, here):
            run(when, copy.wait)
        per = out.shape[1] // 16

        def body(ways):
            @pl.loop(0, out.shape[0] * per)
            def _(i):
                at = (i // per, pl.ds(pl.multiple_of(lax.rem(i, per) * 16, 16), 16), slice(None))
                value = self.own.at[z][at].astype(F32)
                for way in ways:
                    value = value + self.mate[(way,) + at].astype(F32)
                out[at] = value.astype(out.dtype)

        run(z == 0, lambda: body((1,)))
        run(z == last, lambda: body((0,)))
        if last > 1:
            run((z > 0) & (z < last), lambda: body((0, 1)))


ANY = pl.BlockSpec(memory_space=pl.ANY)
MIB = 1024 * 1024
HD = 256
shape = jax.ShapeDtypeStruct


def nt(left, right):
    return lax.dot_general(left, right, (((1,), (1,)), ((), ())), preferred_element_type=F32)


def tn(left, right):
    return lax.dot_general(left, right, (((0,), (0,)), ((), ())), preferred_element_type=F32)


def turn(value, cosine, sine):
    half = HD // 8
    first = lax.broadcasted_iota(jnp.int32, value.shape, 1) < half
    other = jnp.where(first, pltpu.roll(value, 128 - half, 1), pltpu.roll(value, half, 1))
    return value * cosine + other * sine


def stream(body, grid, ins, outs):
    def spec(entry):
        block, index = entry[1:3]
        return pl.BlockSpec(block, index, pipeline_mode=pl.Buffered(1)) if len(entry) > 3 else pl.BlockSpec(block, index)

    pltpu.emit_pipeline(
        body, grid=grid, in_specs=[spec(e) for e in ins], out_specs=[spec(e) for e in outs]
    )(*[e[0] for e in ins], *[e[0] for e in outs])


def whole(ref):
    return (ref, ref.shape, lambda *i: (0,) * len(ref.shape), 1)


def chunks(rows, size):
    return lambda body: pl.loop(0, rows // size)(lambda i: body(pl.ds(pl.multiple_of(i * size, size), size), i))


def layer_kernel(seq_n, dp_n, dims, n_ins, n_outs, *refs):
    ins, outs = refs[:n_ins], refs[n_ins : n_ins + n_outs]
    scratch = refs[n_ins + n_outs :]
    x_own, gy_own, up_w, qkv_w, out_w, down_w, small, tables = ins
    mixed_out, input_grad, qkv_red, out_red, down_red, small_red = outs[:6]
    up_red, mixed_bufs, wide_bufs = outs[6:8], outs[8:11], outs[11:14]
    x, qkv_all, out_all, heads, gatt, wide_f, p_qkv, p_out, mixed, wide = outs[14:24]
    up_all, down_all, slope, p_up, p_down = [outs[24 + 2 * i : 26 + 2 * i] for i in range(5)]
    hops = outs[34:]
    sems, scratch = scratch[:3], scratch[3:]
    small_v, vec, up_b, qkv_b, doc_row, cols_v, sm, sm_dp, sm_sum, dk_acc, dv_acc = scratch[:11]
    out_f, down_f, tab, gy, n1, n2, hidden, att, gproj = scratch[11:20]
    scratch = scratch[20:]
    mean_at, inv_at, doc_at = [slice(k, k + 1) for k in range(3)]
    grad_up = n1
    L, D, ff, H, r, ro, rd = dims
    hd = HD
    T, CH = (HD, 512) if L <= 1024 else (HD // 2, 256)
    l, ffh, rdh, half_n = H * hd, ff // 2, rd // 2, 2
    net = Net(seq_n, dp_n, *sems)
    S, Z, s, d = net.S, net.Z, net.s, net.d
    tok = L // S
    scale = 1.0 / math.sqrt(hd)
    per = dp_n * r // T
    own_rows = pl.ds(pl.multiple_of(s * tok, tok), tok)

    def lanes(ref):
        return (ref, (ref.shape[0], T), lambda i: (0, i))

    def d_rows(ref):
        return (ref, (1, T // r, r, ref.shape[3]), lambda i: (lax.div(i, per), lax.rem(i, per), 0, 0))

    def reduce(i, part):
        return ReduceLine(net, part, scratch[2 * i], scratch[2 * i + 1], hops[2 * i], hops[2 * i + 1])

    def seq_rows(ref):
        def slot(k, h):
            size = tok if h is None else tok // 2
            return ref.at[pl.ds(pl.multiple_of(k * tok + (h or 0) * size, size), size)]

        return slot

    halves = range(half_n)
    x_g, gy_g = GatherSeq(net, x_own, seq_rows(x)), GatherSeq(net, gy_own, seq_rows(gy))
    up_cut = scratch[7]
    su = [
        Exchange(net, lambda k, h=h: up_cut.at[h, k], lambda k, h=h: up_all[h].at[k, d], own=True, settle=True)
        for h in halves
    ]
    sq = [
        Exchange(
            net,
            lambda k, j=j: qkv_w.at[:, pl.ds(pl.multiple_of((j * S + k) * l, 128), l)],
            lambda k, j=j: qkv_all.at[k, d, :, pl.ds(j * l, l)],
        )
        for j in range(3)
    ]
    o_g = GatherLine(net, lambda k: out_all.at[k], out_w)
    q_g = GatherLine(net, lambda k: qkv_all.at[:, k])
    u_g = [GatherLine(net, lambda k, h=h: up_all[h].at[:, k]) for h in halves]
    down_rows = [down_w.at[pl.ds(h * rdh, rdh)] for h in halves]
    d_g = [GatherLine(net, lambda k, h=h: down_all[h].at[k], down_rows[h]) for h in halves]
    ds = [reduce(h, lambda k, h=h: p_down[h].at[pl.ds(k, 1)]) for h in halves]
    us = [reduce(2 + h, lambda k, h=h: p_up[h].at[:, k]) for h in halves]
    qs = reduce(4, lambda k: p_qkv.at[:, k])
    os = reduce(5, lambda k: p_out.at[pl.ds(k, 1)])
    mx = SumSeq(net, mixed, *mixed_bufs)
    wx = SumSeq(net, wide, *wide_bufs)
    qx = Exchange(net, lambda k: qs.own.at[net.z, k], lambda k: qkv_red.at[k], own=True)
    ux = [Exchange(net, lambda k, h=h: us[h].own.at[net.z, k], lambda k, h=h: up_red[h].at[k], own=True) for h in halves]
    sf = Exchange(net, lambda k: small_v.at[s], lambda k: small_v.at[k])
    sm_x = Exchange(net, lambda k: sm_sum, lambda k: small_red.at[k], own=True)
    small_to = [lax.rem(d + k, dp_n) for k in range(1, dp_n)]
    small_from = [lax.rem(d + dp_n - k, dp_n) for k in range(1, dp_n)]
    sf_dp = [net.copy(small, small_v.at[s, d], (s, to)) for to in small_to]
    sm_to = [net.copy(sm, sm_dp.at[d], (s, to)) for to in small_to]
    sf_own = net.near(small, small_v.at[s, d])
    spot = lambda at, rows, base, width: n1.at[pl.ds(at, rows), pl.ds(base, width)]
    loc = Place(
        net,
        [(gy_own, gy.at[own_rows]), (tables, tab)],
        [
            (
                qkv_w.at[:, pl.ds(pl.multiple_of((j * S + s) * l, 128), l)],
                spot(tok + ro, r, j * l, l),
                qkv_all.at[s, d, :, pl.ds(j * l, l)],
            )
            for j in range(3)
        ]
        + [(x_own, spot(0, tok, 0, D), x.at[own_rows]), (out_w, spot(tok, ro, 0, D), out_all.at[d])]
        + [(down_rows[h], scratch[2 * h].at[0, 0], down_all[h].at[d]) for h in halves],
    )
    up_loads = [net.near(up_w.at[:, pl.ds(k * ff, ff)], n2.at[pl.ds(k * r, r), pl.ds(0, ff)]) for k in range(S)]
    out_copies = [net.near(out_f, out_red)] + [net.near(down_f, down_red.at[:, pl.ds(h * rdh, rdh)]) for h in halves]
    begun = []

    def out_total():
        os.total(out_f)
        out_copies[0].start()

    def down_total(h):
        for copy in begun:
            copy.wait()
        ds[h].total(down_f)
        out_copies[1 + h].start()
        begun[:] = [out_copies[1 + h]]

    def cut_up():
        for k, load in enumerate(up_loads):
            load.wait()
            rows = slice(k * r, (k + 1) * r)
            for m in range(dp_n):
                for h in halves:
                    up_cut[h, k, :, m * rdh : (m + 1) * rdh] = n2[rows, m * rd + h * rdh : m * rd + (h + 1) * rdh]

    def small_first():
        sf_own.start()
        for copy in sf_dp:
            net.send(copy)

    def small_second():
        sf_own.wait()
        for copy in sf_dp:
            copy.wait_recv()
        sf.start()

    def sums_first():
        for copy in sm_to:
            net.send(copy)

    def sums_second():
        sm_sum[...] = sm[...]
        for copy, source in zip(sm_to, small_from):
            copy.wait_recv()
            sm_sum[...] += sm_dp[source]
        sm_x.start()

    def pieces(out, row, found):
        lane = lax.broadcasted_iota(jnp.int32, (1, 128), 1) // r
        q = 128 // r
        for p in range(len(found) // q):
            value = small_v[found[p * q]]
            for k in range(1, q):
                value = jnp.where(lane == k, small_v[found[p * q + k]], value)
            out[row : row + 1, 128 * p : 128 * p + 128] = value

    def unpack():
        sf.wait()
        for j in range(5):
            pieces(vec, j, [(i // dp_n, i % dp_n, slice(j, j + 1)) for i in range(seq_n * dp_n)])
        for h in halves:
            pieces(up_b, h, [(s, m // 2, slice(8 + 2 * h + m % 2, 9 + 2 * h + m % 2)) for m in range(2 * dp_n)])
        found = []
        for j in range(3):
            for m in range(l // r):
                piece = j * (D // r) + s * (l // r) + m
                owner = lax.div(piece, 3)
                found.append((lax.div(owner, dp_n), lax.rem(owner, dp_n), pl.ds(5 + lax.rem(piece, 3), 1)))
        pieces(qkv_b, 0, found)
        for k in range(S):
            for j in range(tok // 128):
                row = small_v[k, d, 12 + j : 13 + j]
                at = k * tok + j * 128
                doc_row[0:1, at : at + 128] = row
                cols_v[at : at + 128, :] = jnp.transpose(jnp.broadcast_to(row, (128, 128)))
        sm[...] = jnp.zeros_like(sm)
        sm[4:5, :] = jnp.sum(gy[own_rows, :].astype(F32), 0, keepdims=True)

    def cols_of(base=0):
        return pl.ds(pl.multiple_of(base + pl.program_id(0) * T, T), T)

    def norm_phase():
        def body(xb):
            i = pl.program_id(0)
            at = pl.ds(pl.multiple_of(i * T, T), T)
            wide_x = xb[...].astype(F32)
            mean = jnp.mean(wide_x, -1, keepdims=True)
            center = wide_x - mean
            inv = lax.rsqrt(jnp.mean(center * center, -1, keepdims=True) + epsilon)
            cols_v[at, mean_at] = mean
            cols_v[at, inv_at] = inv
            hat = center * inv
            n1[at, :] = (hat * vec[0:1, :] + vec[1:2, :]).astype(BF)
            n2[at, :] = (hat * vec[2:3, :] + vec[3:4, :]).astype(BF)

        stream(body, (L // T,), [(x, (T, D), lambda i: (i, 0))], [])

    def up_phase(h):
        def body(w, slo):
            cols = cols_of(h * ffh)
            bias = up_b[h : h + 1, cols_of()]

            @chunks(L, CH)
            def _(at, i):
                u = dot(n2[at, :], w[...].reshape(D, T)) + bias
                phi = 0.5 + 0.5 * lax.erf(u * math.sqrt(0.5))
                hidden[at, cols] = (u * phi).astype(BF)
                slo[at, :] = (phi + u * (jnp.exp(-0.5 * u * u) * (1.0 / math.sqrt(2.0 * math.pi)))).astype(BF)

        stream(body, (ffh // T,), [(up_all[h], (S, dp_n, r, T), lambda i: (0, 0, 0, i))], [lanes(slope[h])])

    def outer_phase(left, base, n, right, out):
        def body(o):
            width = o.shape[-1]
            step = min(width, 1024)

            @chunks(width, step)
            def _(at, j):
                value = tn(left[:, cols_of(base)], right[:, at])
                o[(slice(None),) * (len(o.shape) - 1) + (at,)] = value.astype(BF).reshape(o.shape[:-1] + (step,))

        if len(out.shape) == 3:
            target = (out, (T // out.shape[1], out.shape[1], D), lambda i: (i, 0, 0))
        else:
            target = d_rows(out)
        stream(body, (n,), [], [target])

    def down_grad_phase(h):
        outer_phase(hidden, h * ffh, ffh // T, gy, p_down[h])

    def up_grad_phase(h):
        outer_phase(n2, 0, D // T, grad_up.at[:, pl.ds(h * ffh, ffh)], p_up[h])

    def out_grad_phase():
        outer_phase(att, 0, l // T, gy, p_out)

    def qkv_grad_phase():
        def body(o):
            for j in range(3):
                o[:, :, :, j * l : (j + 1) * l] = tn(n1[:, cols_of()], gproj[j]).astype(BF).reshape(o.shape[:-1] + (l,))

        for j in range(3):
            sm[6:7, j * l : (j + 1) * l] = jnp.sum(gproj[j].astype(F32), 0, keepdims=True)
        stream(body, (D // T,), [], [d_rows(p_qkv)])

    def gatt_phase():
        def body(w, o):
            @chunks(L, CH)
            def _(at, i):
                o[0, at, :] = nt(gy[at, :], w[...].reshape(hd, D)).astype(BF)

        w = (out_all, (hd // ro, ro, D), lambda i: (i, 0, 0))
        stream(body, (H,), [w], [(gatt, (1, L, hd), lambda i: (i, 0, 0))])

    def qkv_phase():
        def body(w, o):
            j = pl.program_id(0)
            bias = qkv_b[0:1, pl.ds(pl.multiple_of(j * hd, hd), hd)]

            @chunks(L, CH)
            def _(at, i):
                p = dot(n1[at, :], w[...].reshape(D, hd)) + bias
                o[0, at, 128:] = p[:, 128:].astype(BF)

                @pl.when(j < 2 * H)
                def _():
                    o[0, at, :128] = turn(p[:, :128], tab[0, at, :], tab[1, at, :]).astype(BF)

                @pl.when(j >= 2 * H)
                def _():
                    o[0, at, :128] = p[:, :128].astype(BF)

        w = (qkv_all, (S, dp_n, r, hd), lambda i: (0, 0, 0, i))
        stream(body, (3 * H,), [w], [(heads, (1, L, hd), lambda i: (i, 0, 0))])

    def att_phase():
        def body(q, k, v, ga):
            h, i = pl.program_id(0), pl.program_id(1)
            cols = pl.ds(pl.multiple_of(h * hd, hd), hd)
            low = pl.ds(pl.multiple_of(h * hd, hd), 128)
            high = pl.ds(pl.multiple_of(h * hd + 128, 128), 128)
            back = lambda t, rows: turn(t, tab[0, rows, :], -tab[1, rows, :])

            @pl.when(i == 0)
            def _():
                dk_acc[...] = jnp.zeros_like(dk_acc)
                dv_acc[...] = jnp.zeros_like(dv_acc)

            def tile(c):
                n = (c + 1) * T
                at = slice(c * T, n)
                qt, kt, vt, gt = q[0], k[0, :n], v[0, :n], ga[0]
                query = lax.broadcasted_iota(jnp.int32, (T, n), 0) + c * T
                key = lax.broadcasted_iota(jnp.int32, (T, n), 1)
                allowed = (cols_v[at, doc_at] == doc_row[0:1, :n]) & (key <= query)
                raw = jnp.where(allowed, nt(qt, kt) * scale, -1000000000.0)
                e = jnp.exp(raw - jnp.max(raw, -1, keepdims=True))
                p = e / jnp.sum(e, -1, keepdims=True)
                pb = p.astype(BF)
                att[at, cols] = dot(pb, vt).astype(BF)
                gp = nt(gt, vt)
                gs = (p * (gp - jnp.sum(gp * p, -1, keepdims=True))).astype(BF)
                gq = dot(gs, kt) * scale
                gproj[0, at, low] = back(gq[:, :128], at).astype(BF)
                gproj[0, at, high] = gq[:, 128:].astype(BF)
                dk_acc[:n, :] += tn(gs, qt)
                dv_acc[:n, :] += tn(pb, gt)

            for c in range(L // T):
                pl.when(i == c)(functools.partial(tile, c))

            @pl.when(i == L // T - 1)
            def _():
                gk = dk_acc[...] * scale
                gproj[1, :, low] = back(gk[:, :128], slice(None)).astype(BF)
                gproj[1, :, high] = gk[:, 128:].astype(BF)
                gproj[2, :, cols] = dv_acc[...].astype(BF)

        block = (1, T, hd)
        full = (1, L, hd)
        stream(
            body,
            (H, L // T),
            [
                (heads, block, lambda h, i: (h, i, 0)),
                (heads, full, lambda h, i: (H + h, 0, 0)),
                (heads, full, lambda h, i: (2 * H + h, 0, 0)),
                (gatt, block, lambda h, i: (h, i, 0)),
            ],
            [],
        )

    def norm_sums(grad, xb, at, row):
        cols = cols_of()
        hat = (xb[at, :].astype(F32) - cols_v[at, mean_at]) * cols_v[at, inv_at]
        sm[row : row + 1, cols] += jnp.sum(grad * hat, 0, keepdims=True)
        sm[row + 1 : row + 2, cols] += jnp.sum(grad, 0, keepdims=True)

    def one_phase():
        def body(w, xb, o):
            @chunks(L, CH)
            def _(at, m):
                grad = 0.0
                for j in range(3):
                    grad = grad + nt(gproj[j, at, :], w[:, :, :, j * l : (j + 1) * l].reshape(T, l))
                norm_sums(grad, xb, at, 0)
                o[at, :] = grad * vec[0:1, cols_of()]

        stream(body, (D // T,), [d_rows(qkv_all), lanes(x)], [lanes(wide_f)])

    per_ch = max(1, CH // tok)

    def two_phase():
        def body(wa, wb, xb, first, o):
            @chunks(L, per_ch * tok)
            def _(at, m):
                grad = nt(grad_up[at, :ffh], wa[...].reshape(T, ffh)) + nt(grad_up[at, ffh:ff], wb[...].reshape(T, ffh))
                norm_sums(grad, xb, at, 2)
                value = first[at, :] + grad * vec[2:3, cols_of()]
                o[pl.ds(m * per_ch, per_ch)] = value.astype(BF).reshape(per_ch, tok, T)

        stream(
            body,
            (D // T,),
            [d_rows(up_all[0]), d_rows(up_all[1]), lanes(x), lanes(wide_f)],
            [(wide, (S, tok, T), lambda i: (0, 0, i))],
        )

    def mixed_phase():
        def body(wa, wb, wo, o):
            @chunks(L, per_ch * tok)
            def _(at, m):
                value = dot(hidden[at, :ffh], wa[...].reshape(ffh, T)) + dot(hidden[at, ffh:], wb[...].reshape(ffh, T))
                value = value + dot(att[at, :], wo[...].reshape(l, T))
                o[pl.ds(m * per_ch, per_ch)] = value.astype(BF).reshape(per_ch, tok, T)

        cols = lambda ref: (ref, ref.shape[:2] + (T,), lambda i: (0, 0, i))
        ws = [cols(down_all[0]), cols(down_all[1]), cols(out_all)]
        stream(body, (D // T,), ws, [(mixed, (S, tok, T), lambda i: (0, 0, i))])

    def slope_phase(h):
        def body(w, slo):
            cols = cols_of(h * ffh)

            @chunks(L, CH)
            def _(at, m):
                gu = (nt(gy[at, :], w[...].reshape(T, D)) * slo[at, :].astype(F32)).astype(BF)
                grad_up[at, cols] = gu
                sm[5:6, cols] += jnp.sum(gu.astype(F32), 0, keepdims=True)

        w = (down_all[h], (T // rdh, rdh, D), lambda i: (i, 0, 0))
        stream(body, (ffh // T,), [w, lanes(slope[h])], [])

    ends = 2 if mx.square else 8
    part = tok // ends
    tiles = lambda ref, lead: (ref, (lead, part, D), lambda i: (0, i, 0))
    mine = lambda ref: (ref, (part, D), lambda i: (i, 0))

    def total_of(own, came):
        total = own[0].astype(F32)
        for ref in came:
            for k in range(ref.shape[0]):
                total = total + ref[k].astype(F32)
        return total

    def mixed_end():
        def body(xb, own, *rest):
            rest[-1][0] = (xb[...].astype(F32) + vec[4:5, :] + total_of(own, rest[:-1])).astype(BF)

        stream(body, (ends,), [mine(x_own), tiles(mixed.at[pl.ds(s, 1)], 1)] + mx.ins(part), [tiles(mixed_out, 1)])

    def input_end():
        def body(xb, gb, own, *rest):
            at = pl.ds(pl.multiple_of(s * tok + pl.program_id(0) * part, part), part)
            inv = cols_v[at, inv_at]
            hat = (xb[...].astype(F32) - cols_v[at, mean_at]) * inv
            total = total_of(own, rest[:-1])
            total = total - jnp.mean(total, -1, keepdims=True) - hat * jnp.mean(total * hat, -1, keepdims=True)
            rest[-1][0] = gb[...].astype(F32) + inv * total

        ins = [mine(x_own), mine(gy_own), tiles(wide.at[pl.ds(s, 1)], 1)] + wx.ins(part)
        stream(body, (ends,), ins, [tiles(input_grad, 1)])

    net.barrier()
    loc.start()
    for load in up_loads:
        load.start()
    small_first()
    o_g.early()
    o_g.start()
    for x_sq in sq:
        x_sq.start()
    o_g.go(1)
    x_g.start()
    loc.finish()
    for x_sq in sq:
        x_sq.wait()
    q_g.early()
    q_g.start()
    cut_up()
    su[0].start()
    o_g.go(2)
    o_g.go(3)
    d_g[1].early()
    q_g.go(1)
    small_second()
    x_g.relay()
    gy_g.start()
    q_g.go(2)
    o_g.wait()
    su[0].wait()
    u_g[0].early()
    x_g.wait()
    unpack()
    norm_phase()
    d_g[1].start()
    u_g[0].start()
    q_g.go(3)
    gy_g.relay()
    su[1].start()
    d_g[0].early()
    d_g[0].start()
    q_g.wait()
    qkv_phase()
    gy_g.wait()
    gatt_phase()
    su[1].wait()
    u_g[1].early()
    att_phase()
    u_g[1].start()
    out_grad_phase()
    os.start()
    u_g[0].go(1)
    os.pair()
    d_g[0].go(1)
    qkv_grad_phase()
    qs.start()
    os.go(1)
    qs.pair()
    u_g[0].go(2)
    one_phase()
    d_g[0].go(2)
    u_g[0].go(3)
    u_g[1].go(1)
    u_g[0].wait()
    up_phase(0)
    qs.go(1)
    d_g[0].go(3)
    down_grad_phase(0)
    ds[0].start()
    d_g[0].wait()
    slope_phase(0)
    ds[0].pair()
    u_g[1].go(2)
    d_g[1].go(1)
    up_grad_phase(0)
    u_g[1].go(3)
    d_g[1].go(2)
    u_g[1].wait()
    us[0].start()
    up_phase(1)
    d_g[1].go(3)
    ds[0].go(1)
    qs.go(2)
    us[0].pair()
    d_g[1].wait()
    mixed_phase()
    os.go(2)
    mx.start()
    slope_phase(1)
    qs.go(3)
    us[0].go(1)
    up_grad_phase(1)
    us[1].start()
    qs.total()
    qx.start()
    ds[0].go(2)
    us[1].pair()
    mx.mid()
    us[0].go(2)
    two_phase()
    sums_first()
    ds[0].go(3)
    wx.start()
    us[1].go(1)
    down_grad_phase(1)
    ds[1].start()
    sums_second()
    ds[1].pair()
    us[0].go(3)
    mx.wait()
    us[0].total()
    ux[0].start()
    mixed_end()
    down_total(0)
    us[1].go(2)
    wx.mid()
    os.go(3)
    qx.wait()
    ds[1].go(1)
    out_total()
    ux[0].wait()
    us[1].go(3)
    us[1].total()
    ux[1].start()
    ds[1].go(2)
    wx.wait()
    input_end()
    ux[1].wait()
    ds[1].go(3)
    down_total(1)
    sm_x.wait()
    for copy in [out_copies[0]] + begun:
        copy.wait()
    net.drain()


def layer(seq_n, dp_n, dims, args):
    L, D, ff, H, r, ro, rd = dims
    l, Z, ffh, rdh = H * HD, dp_n // 2, ff // 2, rd // 2
    tok = L // seq_n
    seq_tok, up_slab, qkv_slab = (seq_n, tok, D), (seq_n, r, ffh), (seq_n, r, 3 * l)
    outs = [((1, tok, D), BF), ((1, tok, D), F32), (qkv_slab, BF), ((1, ro, D), F32), ((1, rd, D), F32), ((seq_n, 8, D), F32)]
    outs += [(up_slab, BF)] * 2
    half = tok // 2
    if seq_n == 4:
        outs += [((4, half, D), BF), ((2, half, D), BF), ((2, half, D), BF)] * 2
    else:
        outs += [((seq_n - 1, tok, D), BF), ((16, 128), BF), ((16, 128), BF)] * 2
    outs += [((L, D), BF), ((seq_n, dp_n, r, 3 * l), BF), ((dp_n, ro, D), BF), ((3 * H, L, HD), BF), ((H, L, HD), BF)]
    outs += [((L, D), F32), ((seq_n, dp_n, r, 3 * l), BF), ((dp_n, ro, D), BF), (seq_tok, BF), (seq_tok, BF)]
    up_full, down_full = (seq_n, dp_n, r, ffh), (dp_n, rdh, D)
    for v in (up_full, down_full, (L, ffh), up_full, down_full):
        outs += [(v, BF)] * 2
    slabs = [(1, rdh, D)] * 2 + [up_slab] * 2 + [qkv_slab, (1, ro, D)]
    for slab in slabs:
        outs += [((Z - 1,) + slab, BF)] * 2
    out_shape = [shape(*o) for o in outs]
    n = 6 * (4 * Z - 3) + 6 * (3 * Z - 2) + 14 * (seq_n - 1) + 2 * max(4, seq_n - 1) + 2 * (dp_n - 1)
    vmem = [((seq_n, dp_n, 16, 128), F32), ((8, D), F32), ((8, ffh), F32), ((8, 3 * l), F32), ((8, L), F32), ((L, 128), F32)]
    vmem += [((8, D), F32), ((dp_n, 8, D), F32), ((8, D), F32), ((L, HD), F32), ((L, HD), F32)]
    vmem += [((1, ro, D), F32), ((1, rdh, D), F32), ((2, L, 128), F32)]
    vmem += [((L, D), BF), ((L, D), BF), ((L, D), BF), ((L, ff), BF), ((L, l), BF), ((3, L, l), BF)]
    for slab in slabs:
        vmem += [((Z,) + slab, BF)] * 2
    scratch = [pltpu.SemaphoreType.DMA((k,)) for k in (n, n, 40 + seq_n + 6 * (3 * Z - 2))] + [pltpu.VMEM(*v) for v in vmem]
    return pl.pallas_call(
        functools.partial(layer_kernel, seq_n, dp_n, dims, len(args), len(outs)),
        out_shape=out_shape,
        in_specs=[ANY] * len(args),
        out_specs=[ANY] * len(outs),
        scratch_shapes=scratch,
        compiler_params=pltpu.CompilerParams(collective_id=0, has_side_effects=True, vmem_limit_bytes=63 * MIB),
        name="layer",
    )(*args)[:8]


def last_kernel(dims, seq_n, dp_n, places, *refs):
    L, D, ff, H, r, ro, rd = dims
    l, ffh, rdh = H * HD, ff // 2, rd // 2
    ins, outs, acc = refs[:8], refs[8:-1], refs[-1]
    mixed, grad, qkv, out_w, down, sums, up_a, up_b = ins
    mixed_out, grad_out, up_out, qkv_out, out_out, down_out = outs[:6]
    small = outs[6:]
    mixed_out[...] = mixed[...]
    grad_out[...] = grad[...]
    out_out[...] = out_w[0]
    down_out[...] = down[0]
    for k in range(seq_n):
        for m in range(dp_n):
            for h, src in enumerate((up_a, up_b)):
                at = k * ff + m * rd + h * rdh
                up_out[:, at : at + rdh] = src[k, :, m * rdh : (m + 1) * rdh].astype(F32)
        for j in range(3):
            at = (j * seq_n + k) * l
            qkv_out[:, at : at + l] = qkv[k, :, j * l : (j + 1) * l].astype(F32)

    @pl.when(pl.program_id(0) == 0)
    def _():
        s, d = places[0], places[1]
        place = s * dp_n + d
        acc[...] = sums[0]
        for k in range(1, seq_n):
            acc[...] += sums[k]

        def piece(load, lane):
            start = pl.multiple_of(lax.div(lane, 128) * 128, 128)
            return pltpu.roll(load(pl.ds(start, 128)), lax.rem(128 - lax.rem(lane, 128), 128), 1)

        for j in range(5):
            small[j][...] = piece(lambda at, j=j: acc[j : j + 1, at], place * r)[:, :r]
        for t in range(3):
            at = place * 3 + t
            j, rest = lax.div(at, D // r), lax.rem(at, D // r)
            of, m = lax.div(rest, l // r), lax.rem(rest, l // r)
            small[5][:, t * r : (t + 1) * r] = piece(lambda at, of=of: sums[of, 6:7, at], j * l + m * r)[:, :r]
        for h in range(2):
            small[6][:, h * rdh : (h + 1) * rdh] = piece(lambda at: sums[s, 5:6, at], h * ffh + d * rdh)[:, :rdh]


def finish(seq_n, dp_n, dims, got):
    L, D, ff, H, r, ro, rd = dims
    tok = L // seq_n
    steps = 4 if r % 64 == 0 else 1
    places = jnp.stack([lax.axis_index("seq"), lax.axis_index("dp")]).astype(jnp.int32)

    def spec(v, axis):
        block = tuple(n // steps if k == axis else n for k, n in enumerate(v.shape))
        return pl.BlockSpec(block, lambda i, p: tuple(i if k == axis else 0 for k in range(v.ndim)))

    outs = [((1, tok, D), BF, 1), ((1, tok, D), F32, 1), ((r, seq_n * ff), F32, 0), ((r, 3 * D), F32, 0), ((ro, D), F32, 0), ((rd, D), F32, 0)]
    outs += [((1, r), F32, None)] * 5 + [((1, 3 * r), F32, None), ((1, rd), F32, None)]
    out_shape = [shape(*o[:2]) for o in outs]
    return pl.pallas_call(
        functools.partial(last_kernel, dims, seq_n, dp_n),
        grid_spec=pltpu.PrefetchScalarGridSpec(
            num_scalar_prefetch=1,
            grid=(steps,),
            in_specs=[spec(v, axis) for v, axis in zip(got, (1, 1, 1, 1, 1, None, 1, 1))],
            out_specs=[spec(v, o[2]) for v, o in zip(out_shape, outs)],
            scratch_shapes=[pltpu.VMEM((8, D), F32)],
        ),
        out_shape=out_shape,
        compiler_params=pltpu.CompilerParams(vmem_limit_bytes=63 * MIB),
        name="finish",
    )(places, *got)
def shards(
    tokens,
    doc_ids,
    ln1_gain,
    ln1_bias,
    ln2_gain,
    ln2_bias,
    qkv_weight,
    qkv_bias,
    out_weight,
    up_weight,
    up_bias,
    down_weight,
    out_bias,
    cotangent,
):
    seq_n = lax.axis_size("seq")
    dp_n = lax.axis_size("dp")
    seq_i = lax.axis_index("seq")
    tok_rows, width = tokens.shape[1:]
    length = tok_rows * seq_n
    head_dim = width // HEADS
    heads = HEADS // seq_n
    local = heads * head_dim
    ff = up_weight.shape[1] // seq_n
    rot_dims = head_dim // 4
    rows, per_down = qkv_weight.shape[0], down_weight.shape[0]
    vectors = (ln1_gain, ln1_bias, ln2_gain, ln2_bias, out_bias, qkv_bias, up_bias)
    total, at, flat = sum(v.shape[0] for v in vectors), 0, 0.0
    for v in vectors:
        flat = flat + jnp.pad(v.astype(F32), (at, total - at - v.shape[0]))
        at += v.shape[0]
    pieces = jnp.tile(flat.reshape(-1, rows), (1, 128 // rows))
    docs = doc_ids.astype(F32).reshape(-1, 128)
    over = 16 - pieces.shape[0]
    small = jnp.pad(pieces, ((0, over), (0, 0))) + jnp.pad(docs, ((16 - over, over - docs.shape[0]), (0, 0)))
    dims = (length, width, ff, heads, rows, out_weight.shape[0], per_down)
    tables = jnp.asarray(rotary_rows(length, rot_dims))
    x, gy = tokens[0], cotangent[0]
    got = layer(seq_n, dp_n, dims, (x, gy, up_weight, qkv_weight, out_weight, down_weight, small, tables))
    mixed, input_grad, up_grad, qkv_grad, out_grad, down_grad, *small = finish(seq_n, dp_n, dims, got)
    g1, b1, g2, b2, ob, qb, ub = [v.reshape(-1) for v in small]
    return (mixed, input_grad, g1, b1, g2, b2, qkv_grad, qb, out_grad, up_grad, ub, down_grad, ob)


def solution(mesh):
    in_specs = (
        P("dp", "seq", None),
        P("dp", "seq"),
        P(("seq", "dp")),
        P(("seq", "dp")),
        P(("seq", "dp")),
        P(("seq", "dp")),
        P(("seq", "dp"), None),
        P(("seq", "dp")),
        P(("seq", "dp"), None),
        P(("seq", "dp"), None),
        P(("seq", "dp")),
        P(("seq", "dp"), None),
        P(("seq", "dp")),
        P("dp", "seq", None),
    )
    out_specs = (
        P("dp", "seq", None),
        P("dp", "seq", None),
        P(("seq", "dp")),
        P(("seq", "dp")),
        P(("seq", "dp")),
        P(("seq", "dp")),
        P(("seq", "dp"), None),
        P(("seq", "dp")),
        P(("seq", "dp"), None),
        P(("seq", "dp"), None),
        P(("seq", "dp")),
        P(("seq", "dp"), None),
        P(("seq", "dp")),
    )
    return jax.shard_map(shards, mesh=mesh, in_specs=in_specs, out_specs=out_specs, check_vma=False)
```

```python
import functools
import math

import jax
import jax.numpy as jnp
import numpy as np
from jax import lax
from jax.experimental import pallas as pl
from jax.experimental.pallas import tpu as pltpu
from jax.sharding import PartitionSpec as P

HEADS = 8
BF = jnp.bfloat16
F32 = jnp.float32


epsilon = 1e-05


def rotary_rows(length, rot_dims):
    half = rot_dims // 2
    exponents = np.arange(half, dtype=np.float32) * np.float32(2.0 / rot_dims)
    inverse = np.power(np.float32(10000.0), -exponents).astype(np.float32)
    phase = (np.arange(length, dtype=np.float32)[:, None] * inverse[None, :]).astype(np.float64)
    tables = np.zeros((2, length, 128), np.float32)
    tables[0] = 1.0
    tables[0, :, :half] = tables[0, :, half:rot_dims] = np.cos(phase)
    tables[1, :, :half] = -np.sin(phase)
    tables[1, :, half:rot_dims] = np.sin(phase)
    return tables


def dot(left, right):
    return jnp.dot(left, right, preferred_element_type=F32)


MESH = pl.DeviceIdType.MESH


def run(when, action):
    if when is None:
        action()
    else:
        pl.when(when)(lambda: action())


class Net:
    def __init__(self, seq_n, dp_n, send_sems, recv_sems, local_sems):
        self.S, self.DP, self.Z = seq_n, dp_n, dp_n // 2
        self.s, self.d = lax.axis_index("seq"), lax.axis_index("dp")
        self.z, self.c = self.d // 2, lax.rem(self.d, 2)
        self.send_sems, self.recv_sems, self.used = send_sems, recv_sems, 0
        self.local_sems, self.local_used = local_sems, 0
        self.sent = []

    def seq_peer(self, s):
        return (s, self.d)

    def line_peer(self, z):
        return (self.s, 2 * jnp.clip(z, 0, self.Z - 1) + self.c)

    def partner(self):
        return (self.s, 2 * self.z + 1 - self.c)

    def copy(self, src, dst, device):
        self.used += 1
        return self.copy_at(self.used - 1, src, dst, device)

    def copy_at(self, i, src, dst, device):
        return pltpu.make_async_remote_copy(
            src_ref=src,
            dst_ref=dst,
            send_sem=self.send_sems.at[i],
            recv_sem=self.recv_sems.at[i],
            device_id=device,
            device_id_type=MESH,
        )

    def send(self, copy, when=None):
        self.sent.append((copy, when))
        run(when, copy.start)

    def drain(self):
        for copy, when in self.sent:
            run(when, copy.wait_send)

    def near(self, src, dst):
        self.local_used += 1
        return pltpu.make_async_copy(src, dst, self.local_sems.at[self.local_used - 1])

    def barrier(self):
        sem = pltpu.get_barrier_semaphore()
        peers = [self.seq_peer(lax.rem(self.s + k, self.S)) for k in range(1, self.S)]
        peers += [(self.s, lax.rem(self.d + k, self.DP)) for k in range(1, self.DP)]
        for device in peers:
            pl.semaphore_signal(sem, inc=1, device_id=device, device_id_type=MESH)
        pl.semaphore_wait(sem, len(peers))


class Place:
    def __init__(self, net, direct, through):
        self.direct = [net.near(src, dst) for src, dst in direct]
        self.loads = [net.near(src, buf) for src, buf, _ in through]
        self.stores = [net.near(buf, dst) for _, buf, dst in through]

    def start(self):
        for copy in self.loads + self.direct:
            copy.start()

    def finish(self):
        for load, store in zip(self.loads, self.stores):
            load.wait()
            store.start()
        for copy in self.stores + self.direct:
            copy.wait()


class Exchange:
    def __init__(self, net, src, slot, by_turn=False, own=False, settle=False):
        self.net, self.copies, self.settle = net, [], settle
        for k in range(1, net.S):
            to = lax.rem(net.s + k, net.S)
            self.copies.append(net.copy(src(to), slot(k - 1 if by_turn else net.s), net.seq_peer(to)))
        self.own = net.near(src(net.s), slot(net.s)) if own else None

    def start(self):
        for copy in self.copies:
            if self.settle:
                copy.start()
            else:
                self.net.send(copy)
        if self.own is not None:
            self.own.start()

    def wait(self):
        for copy in self.copies:
            copy.wait_recv()
            if self.settle:
                copy.wait_send()
        if self.own is not None:
            self.own.wait()


class GatherSeq:
    def __init__(self, net, src, slot):
        self.net, self.square = net, net.S == 4
        if self.square:
            s = net.s
            a, b = s + 1 - 2 * lax.rem(s, 2), lax.rem(s + 2, 4)
            self.first = [net.copy(src, slot(s, None), net.seq_peer(p)) for p in (a, b)]
            self.second = [
                net.copy(slot(a, 0), slot(a, 0), net.seq_peer(b)),
                net.copy(slot(b, 1), slot(b, 1), net.seq_peer(a)),
            ]
        else:
            self.direct = Exchange(net, lambda to: src, lambda k: slot(k, None))

    def start(self):
        if self.square:
            for copy in self.first:
                self.net.send(copy)
        else:
            self.direct.start()

    def relay(self):
        if self.square:
            for came, onward in zip(self.first, self.second):
                came.wait_recv()
                self.net.send(onward)

    def wait(self):
        if self.square:
            for copy in self.second:
                copy.wait_recv()
        else:
            self.direct.wait()


class SumSeq:
    def __init__(self, net, src, came, onward, held):
        self.net, self.src, self.came, self.onward, self.held, self.square = net, src, came, onward, held, net.S == 4
        if not self.square:
            self.direct = Exchange(net, lambda k: src.at[k], lambda k: came.at[k], by_turn=True)
            return
        s, half = net.s, src.shape[1] // 2
        a, b, across = s + 1 - 2 * lax.rem(s, 2), lax.rem(s + 2, 4), 3 - s
        self.ways = (b, a)
        part = lambda k, h: src.at[k, pl.ds(h * half, half)]
        self.first = []
        for h, near in ((0, a), (1, b)):
            for i, block in enumerate((near, across)):
                self.first.append(net.copy(part(block, h), came.at[2 * h + i], net.seq_peer(near)))
        self.second = [net.copy(held.at[h], onward.at[h], net.seq_peer(to)) for h, to in ((0, b), (1, a))]

    def start(self):
        if self.square:
            for i in (1, 3, 0, 2):
                self.net.send(self.first[i])
        else:
            self.direct.start()

    def mid(self):
        if not self.square:
            return
        b, a = self.ways
        half, width = self.held.shape[1:]
        for i in (1, 3):
            self.first[i].wait_recv()

        def body(own, other, o):
            o[...] = (own[...].astype(F32) + other[...].astype(F32)).astype(BF)

        block = (1, half, width)
        stream(
            body,
            (2,),
            [
                (self.src, block, lambda h: (jnp.where(h == 0, b, a), h, 0)),
                (self.came, block, lambda h: (2 * h + 1, 0, 0)),
            ],
            [(self.held, block, lambda h: (h, 0, 0))],
        )
        for copy in self.second:
            self.net.send(copy)

    def wait(self):
        if self.square:
            for i in (0, 2):
                self.first[i].wait_recv()
            for copy in self.second:
                copy.wait_recv()
        else:
            self.direct.wait()

    def ins(self, rows):
        if self.square:
            block = (1, rows, self.src.shape[2])
            return [(self.came, block, lambda i: (2 * i, 0, 0)), (self.onward, block, lambda i: (i, 0, 0))]
        return [(self.came, (self.net.S - 1, rows, self.src.shape[2]), lambda i: (0, i, 0))]


class Line:
    def go(self, part):
        last = self.net.Z - 1
        for t in ([1], range(2, last), [last])[part - 1]:
            self.step(t)


class GatherLine(Line):
    def __init__(self, net, slab, own=None):
        self.net = net
        z, c, last = net.z, net.c, net.Z - 1
        own = slab(net.d) if own is None else own
        self.right, self.left = [], []
        for t in range(net.Z):
            for side, hops in ((1, self.right), (-1, self.left)):
                place = slab(2 * jnp.clip(z - side * t, 0, last) + c)
                src = own if t == 0 else place
                there = z >= t if side == 1 else z <= last - t
                onward = z < last if side == 1 else z > 0
                copy = None if t == last else net.copy(src, place, net.line_peer(z + side))
                core = None if t == 0 and side == -1 else net.copy(src, place, net.partner())
                hops.append((copy, there & onward, core, None if t == 0 else there))

    def early(self):
        self.net.send(self.right[0][0], self.net.z == 0)
        self.net.send(self.left[0][0], self.net.z == self.net.Z - 1)

    def start(self):
        inside = (self.net.z > 0) & (self.net.z < self.net.Z - 1)
        self.net.send(self.right[0][0], inside)
        self.net.send(self.left[0][0], inside)
        self.net.send(self.right[0][2])

    def step(self, t):
        for hops in (self.right, self.left):
            copy, sends, core, there = hops[t]
            run(there, hops[t - 1][0].wait_recv)
            if copy is not None:
                self.net.send(copy, sends)
            self.net.send(core, there)

    def wait(self):
        for hops in (self.right, self.left):
            for _, _, core, there in hops:
                if core is not None:
                    run(there, core.wait_recv)


def add_slabs(dst, left, right):
    blocks, rows = dst.shape[0], dst.shape[1]
    per = rows // 16

    @pl.loop(0, blocks * per)
    def _(i):
        at = (i // per, pl.ds(pl.multiple_of(lax.rem(i, per) * 16, 16), 16), slice(None))
        dst[at] = (left[at].astype(F32) + right[at].astype(F32)).astype(dst.dtype)


class ReduceLine(Line):
    def __init__(self, net, part, own, mate, from_left, from_right):
        self.net, self.own, self.mate, self.bufs = net, own, mate, (from_left, from_right)
        z, c, Z = net.z, net.c, net.Z
        self.order = []
        for t in range((Z + 1) // 2):
            self.order += [Z - 1 - t] + ([t] if t != Z - 1 - t else [])
        self.swaps = {k: net.copy(part(2 * k + 1 - c), mate.at[k], net.partner()) for k in self.order}
        self.loads = {k: net.near(part(2 * k + c), own.at[k]) for k in self.order}
        self.base = net.used
        net.used += 2 * (Z - 1)
        ends = (jnp.clip(Z - 1 - z, 0, Z - 2), jnp.clip(z, 0, Z - 2))
        self.last = [net.near(buf.at[t], mate.at[i]) for i, (buf, t) in enumerate(zip(self.bufs, ends))]

    def start(self):
        for k in self.order:
            self.net.send(self.swaps[k])
            self.loads[k].start()

    def hop(self, side, t):
        net, last = self.net, self.net.Z - 1
        place, way = (last - t, 0) if side == 1 else (t, 1)
        return net.copy_at(
            self.base + way * last + t, self.own.at[place], self.bufs[way].at[t], net.line_peer(net.z + side)
        )

    def pair(self):
        net, done = self.net, set()
        last = net.Z - 1
        right, left = last, 0
        for k in self.order:
            self.loads[k].wait()
            self.swaps[k].wait_recv()
            add_slabs(self.own.at[k], self.own.at[k], self.mate.at[k])
            done.add(k)
            while right > 0 and right in done:
                net.send(self.hop(1, last - right), net.z == 0)
                right -= 1
            while left < last and left in done:
                net.send(self.hop(-1, left), net.z == last)
                left += 1

    def step(self, n):
        net = self.net
        z, last = net.z, net.Z - 1
        for side, far, way in ((1, z, 0), (-1, last - z, 1)):
            t = jnp.clip(n - far, 0, last - 1)
            here = (far >= 1) & (far <= n)
            hop = self.hop(side, t)
            run(here, hop.wait_recv)
            if n < last:
                place, held = last - t if side == 1 else t, self.mate.at[way]
                load = net.near(self.bufs[way].at[t], held)

                def add():
                    load.start()
                    load.wait()
                    add_slabs(self.own.at[place], self.own.at[place], held)

                run(here, add)
                net.send(hop, here)

    def total(self, out=None):
        z, last = self.net.z, self.net.Z - 1
        out = self.own.at[z] if out is None else out
        here = (z > 0, z < last)
        for copy, when in zip(self.last, here):
            run(when, copy.start)
        for copy, when in zip(self.last, here):
            run(when, copy.wait)
        per = out.shape[1] // 16

        def body(ways):
            @pl.loop(0, out.shape[0] * per)
            def _(i):
                at = (i // per, pl.ds(pl.multiple_of(lax.rem(i, per) * 16, 16), 16), slice(None))
                value = self.own.at[z][at].astype(F32)
                for way in ways:
                    value = value + self.mate[(way,) + at].astype(F32)
                out[at] = value.astype(out.dtype)

        run(z == 0, lambda: body((1,)))
        run(z == last, lambda: body((0,)))
        if last > 1:
            run((z > 0) & (z < last), lambda: body((0, 1)))


ANY = pl.BlockSpec(memory_space=pl.ANY)
MIB = 1024 * 1024
HD = 256
shape = jax.ShapeDtypeStruct


def nt(left, right):
    return lax.dot_general(left, right, (((1,), (1,)), ((), ())), preferred_element_type=F32)


def tn(left, right):
    return lax.dot_general(left, right, (((0,), (0,)), ((), ())), preferred_element_type=F32)


def turn(value, cosine, sine):
    half = HD // 8
    first = lax.broadcasted_iota(jnp.int32, value.shape, 1) < half
    other = jnp.where(first, pltpu.roll(value, 128 - half, 1), pltpu.roll(value, half, 1))
    return value * cosine + other * sine


def stream(body, grid, ins, outs):
    def spec(entry):
        block, index = entry[1:3]
        return pl.BlockSpec(block, index, pipeline_mode=pl.Buffered(1)) if len(entry) > 3 else pl.BlockSpec(block, index)

    pltpu.emit_pipeline(
        body, grid=grid, in_specs=[spec(e) for e in ins], out_specs=[spec(e) for e in outs]
    )(*[e[0] for e in ins], *[e[0] for e in outs])


def whole(ref):
    return (ref, ref.shape, lambda *i: (0,) * len(ref.shape), 1)


def chunks(rows, size):
    return lambda body: pl.loop(0, rows // size)(lambda i: body(pl.ds(pl.multiple_of(i * size, size), size), i))


def layer_kernel(seq_n, dp_n, dims, n_ins, n_outs, *refs):
    ins, outs = refs[:n_ins], refs[n_ins : n_ins + n_outs]
    scratch = refs[n_ins + n_outs :]
    x_own, gy_own, up_w, qkv_w, out_w, down_w, small, tables = ins
    mixed_out, input_grad, qkv_red, out_red, down_red, small_red = outs[:6]
    up_red, mixed_bufs, wide_bufs = outs[6:8], outs[8:11], outs[11:14]
    x, qkv_all, out_all, heads, gatt, wide_f, p_qkv, p_out, mixed, wide = outs[14:24]
    up_all, down_all, slope, p_up, p_down = [outs[24 + 2 * i : 26 + 2 * i] for i in range(5)]
    hops = outs[34:]
    sems, scratch = scratch[:3], scratch[3:]
    small_v, vec, up_b, qkv_b, doc_row, cols_v, sm, sm_dp, sm_sum, dk_acc, dv_acc = scratch[:11]
    out_f, down_f, tab, gy, n1, n2, hidden, att, gproj = scratch[11:20]
    scratch = scratch[20:]
    mean_at, inv_at, doc_at = [slice(k, k + 1) for k in range(3)]
    grad_up = n1
    L, D, ff, H, r, ro, rd = dims
    hd = HD
    T, CH = (HD, 512) if L <= 1024 else (HD // 2, 256)
    l, ffh, rdh, half_n = H * hd, ff // 2, rd // 2, 2
    net = Net(seq_n, dp_n, *sems)
    S, Z, s, d = net.S, net.Z, net.s, net.d
    tok = L // S
    scale = 1.0 / math.sqrt(hd)
    per = dp_n * r // T
    own_rows = pl.ds(pl.multiple_of(s * tok, tok), tok)

    def lanes(ref):
        return (ref, (ref.shape[0], T), lambda i: (0, i))

    def d_rows(ref):
        return (ref, (1, T // r, r, ref.shape[3]), lambda i: (lax.div(i, per), lax.rem(i, per), 0, 0))

    def reduce(i, part):
        return ReduceLine(net, part, scratch[2 * i], scratch[2 * i + 1], hops[2 * i], hops[2 * i + 1])

    def seq_rows(ref):
        def slot(k, h):
            size = tok if h is None else tok // 2
            return ref.at[pl.ds(pl.multiple_of(k * tok + (h or 0) * size, size), size)]

        return slot

    halves = range(half_n)
    x_g, gy_g = GatherSeq(net, x_own, seq_rows(x)), GatherSeq(net, gy_own, seq_rows(gy))
    up_cut = scratch[7]
    su = [
        Exchange(net, lambda k, h=h: up_cut.at[h, k], lambda k, h=h: up_all[h].at[k, d], own=True, settle=True)
        for h in halves
    ]
    sq = [
        Exchange(
            net,
            lambda k, j=j: qkv_w.at[:, pl.ds(pl.multiple_of((j * S + k) * l, 128), l)],
            lambda k, j=j: qkv_all.at[k, d, :, pl.ds(j * l, l)],
        )
        for j in range(3)
    ]
    o_g = GatherLine(net, lambda k: out_all.at[k], out_w)
    q_g = GatherLine(net, lambda k: qkv_all.at[:, k])
    u_g = [GatherLine(net, lambda k, h=h: up_all[h].at[:, k]) for h in halves]
    down_rows = [down_w.at[pl.ds(h * rdh, rdh)] for h in halves]
    d_g = [GatherLine(net, lambda k, h=h: down_all[h].at[k], down_rows[h]) for h in halves]
    ds = [reduce(h, lambda k, h=h: p_down[h].at[pl.ds(k, 1)]) for h in halves]
    us = [reduce(2 + h, lambda k, h=h: p_up[h].at[:, k]) for h in halves]
    qs = reduce(4, lambda k: p_qkv.at[:, k])
    os = reduce(5, lambda k: p_out.at[pl.ds(k, 1)])
    mx = SumSeq(net, mixed, *mixed_bufs)
    wx = SumSeq(net, wide, *wide_bufs)
    qx = Exchange(net, lambda k: qs.own.at[net.z, k], lambda k: qkv_red.at[k], own=True)
    ux = [Exchange(net, lambda k, h=h: us[h].own.at[net.z, k], lambda k, h=h: up_red[h].at[k], own=True) for h in halves]
    sf = Exchange(net, lambda k: small_v.at[s], lambda k: small_v.at[k])
    sm_x = Exchange(net, lambda k: sm_sum, lambda k: small_red.at[k], own=True)
    small_to = [lax.rem(d + k, dp_n) for k in range(1, dp_n)]
    small_from = [lax.rem(d + dp_n - k, dp_n) for k in range(1, dp_n)]
    sf_dp = [net.copy(small, small_v.at[s, d], (s, to)) for to in small_to]
    sm_to = [net.copy(sm, sm_dp.at[d], (s, to)) for to in small_to]
    sf_own = net.near(small, small_v.at[s, d])
    spot = lambda at, rows, base, width: n1.at[pl.ds(at, rows), pl.ds(base, width)]
    loc = Place(
        net,
        [(gy_own, gy.at[own_rows]), (tables, tab)],
        [
            (
                qkv_w.at[:, pl.ds(pl.multiple_of((j * S + s) * l, 128), l)],
                spot(tok + ro, r, j * l, l),
                qkv_all.at[s, d, :, pl.ds(j * l, l)],
            )
            for j in range(3)
        ]
        + [(x_own, spot(0, tok, 0, D), x.at[own_rows]), (out_w, spot(tok, ro, 0, D), out_all.at[d])]
        + [(down_rows[h], scratch[2 * h].at[0, 0], down_all[h].at[d]) for h in halves],
    )
    up_loads = [net.near(up_w.at[:, pl.ds(k * ff, ff)], n2.at[pl.ds(k * r, r), pl.ds(0, ff)]) for k in range(S)]
    out_copies = [net.near(out_f, out_red)] + [net.near(down_f, down_red.at[:, pl.ds(h * rdh, rdh)]) for h in halves]
    begun = []

    def out_total():
        os.total(out_f)
        out_copies[0].start()

    def down_total(h):
        for copy in begun:
            copy.wait()
        ds[h].total(down_f)
        out_copies[1 + h].start()
        begun[:] = [out_copies[1 + h]]

    def cut_up():
        for k, load in enumerate(up_loads):
            load.wait()
            rows = slice(k * r, (k + 1) * r)
            for m in range(dp_n):
                for h in halves:
                    up_cut[h, k, :, m * rdh : (m + 1) * rdh] = n2[rows, m * rd + h * rdh : m * rd + (h + 1) * rdh]

    def small_first():
        sf_own.start()
        for copy in sf_dp:
            net.send(copy)

    def small_second():
        sf_own.wait()
        for copy in sf_dp:
            copy.wait_recv()
        sf.start()

    def sums_first():
        for copy in sm_to:
            net.send(copy)

    def sums_second():
        sm_sum[...] = sm[...]
        for copy, source in zip(sm_to, small_from):
            copy.wait_recv()
            sm_sum[...] += sm_dp[source]
        sm_x.start()

    def pieces(out, row, found):
        lane = lax.broadcasted_iota(jnp.int32, (1, 128), 1) // r
        q = 128 // r
        for p in range(len(found) // q):
            value = small_v[found[p * q]]
            for k in range(1, q):
                value = jnp.where(lane == k, small_v[found[p * q + k]], value)
            out[row : row + 1, 128 * p : 128 * p + 128] = value

    def unpack():
        sf.wait()
        for j in range(5):
            pieces(vec, j, [(i // dp_n, i % dp_n, slice(j, j + 1)) for i in range(seq_n * dp_n)])
        for h in halves:
            pieces(up_b, h, [(s, m // 2, slice(8 + 2 * h + m % 2, 9 + 2 * h + m % 2)) for m in range(2 * dp_n)])
        found = []
        for j in range(3):
            for m in range(l // r):
                piece = j * (D // r) + s * (l // r) + m
                owner = lax.div(piece, 3)
                found.append((lax.div(owner, dp_n), lax.rem(owner, dp_n), pl.ds(5 + lax.rem(piece, 3), 1)))
        pieces(qkv_b, 0, found)
        for k in range(S):
            for j in range(tok // 128):
                row = small_v[k, d, 12 + j : 13 + j]
                at = k * tok + j * 128
                doc_row[0:1, at : at + 128] = row
                cols_v[at : at + 128, :] = jnp.transpose(jnp.broadcast_to(row, (128, 128)))
        sm[...] = jnp.zeros_like(sm)
        sm[4:5, :] = jnp.sum(gy[own_rows, :].astype(F32), 0, keepdims=True)

    def cols_of(base=0):
        return pl.ds(pl.multiple_of(base + pl.program_id(0) * T, T), T)

    def norm_phase():
        def body(xb):
            i = pl.program_id(0)
            at = pl.ds(pl.multiple_of(i * T, T), T)
            wide_x = xb[...].astype(F32)
            mean = jnp.mean(wide_x, -1, keepdims=True)
            center = wide_x - mean
            inv = lax.rsqrt(jnp.mean(center * center, -1, keepdims=True) + epsilon)
            cols_v[at, mean_at] = mean
            cols_v[at, inv_at] = inv
            hat = center * inv
            n1[at, :] = (hat * vec[0:1, :] + vec[1:2, :]).astype(BF)
            n2[at, :] = (hat * vec[2:3, :] + vec[3:4, :]).astype(BF)

        stream(body, (L // T,), [(x, (T, D), lambda i: (i, 0))], [])

    def up_phase(h):
        def body(w, slo):
            cols = cols_of(h * ffh)
            bias = up_b[h : h + 1, cols_of()]

            @chunks(L, CH)
            def _(at, i):
                u = dot(n2[at, :], w[...].reshape(D, T)) + bias
                phi = 0.5 + 0.5 * lax.erf(u * math.sqrt(0.5))
                hidden[at, cols] = (u * phi).astype(BF)
                slo[at, :] = (phi + u * (jnp.exp(-0.5 * u * u) * (1.0 / math.sqrt(2.0 * math.pi)))).astype(BF)

        stream(body, (ffh // T,), [(up_all[h], (S, dp_n, r, T), lambda i: (0, 0, 0, i))], [lanes(slope[h])])

    def outer_phase(left, base, n, right, out):
        def body(o):
            width = o.shape[-1]
            step = min(width, 1024)

            @chunks(width, step)
            def _(at, j):
                value = tn(left[:, cols_of(base)], right[:, at])
                o[(slice(None),) * (len(o.shape) - 1) + (at,)] = value.astype(BF).reshape(o.shape[:-1] + (step,))

        if len(out.shape) == 3:
            target = (out, (T // out.shape[1], out.shape[1], D), lambda i: (i, 0, 0))
        else:
            target = d_rows(out)
        stream(body, (n,), [], [target])

    def down_grad_phase(h):
        outer_phase(hidden, h * ffh, ffh // T, gy, p_down[h])

    def up_grad_phase(h):
        outer_phase(n2, 0, D // T, grad_up.at[:, pl.ds(h * ffh, ffh)], p_up[h])

    def out_grad_phase():
        outer_phase(att, 0, l // T, gy, p_out)

    def qkv_grad_phase():
        def body(o):
            for j in range(3):
                o[:, :, :, j * l : (j + 1) * l] = tn(n1[:, cols_of()], gproj[j]).astype(BF).reshape(o.shape[:-1] + (l,))

        for j in range(3):
            sm[6:7, j * l : (j + 1) * l] = jnp.sum(gproj[j].astype(F32), 0, keepdims=True)
        stream(body, (D // T,), [], [d_rows(p_qkv)])

    def gatt_phase():
        def body(w, o):
            @chunks(L, CH)
            def _(at, i):
                o[0, at, :] = nt(gy[at, :], w[...].reshape(hd, D)).astype(BF)

        w = (out_all, (hd // ro, ro, D), lambda i: (i, 0, 0))
        stream(body, (H,), [w], [(gatt, (1, L, hd), lambda i: (i, 0, 0))])

    def qkv_phase():
        def body(w, o):
            j = pl.program_id(0)
            bias = qkv_b[0:1, pl.ds(pl.multiple_of(j * hd, hd), hd)]

            @chunks(L, CH)
            def _(at, i):
                p = dot(n1[at, :], w[...].reshape(D, hd)) + bias
                o[0, at, 128:] = p[:, 128:].astype(BF)

                @pl.when(j < 2 * H)
                def _():
                    o[0, at, :128] = turn(p[:, :128], tab[0, at, :], tab[1, at, :]).astype(BF)

                @pl.when(j >= 2 * H)
                def _():
                    o[0, at, :128] = p[:, :128].astype(BF)

        w = (qkv_all, (S, dp_n, r, hd), lambda i: (0, 0, 0, i))
        stream(body, (3 * H,), [w], [(heads, (1, L, hd), lambda i: (i, 0, 0))])

    def att_phase():
        def body(q, k, v, ga):
            h, i = pl.program_id(0), pl.program_id(1)
            cols = pl.ds(pl.multiple_of(h * hd, hd), hd)
            low = pl.ds(pl.multiple_of(h * hd, hd), 128)
            high = pl.ds(pl.multiple_of(h * hd + 128, 128), 128)
            back = lambda t, rows: turn(t, tab[0, rows, :], -tab[1, rows, :])

            @pl.when(i == 0)
            def _():
                dk_acc[...] = jnp.zeros_like(dk_acc)
                dv_acc[...] = jnp.zeros_like(dv_acc)

            def tile(c):
                n = (c + 1) * T
                at = slice(c * T, n)
                qt, kt, vt, gt = q[0], k[0, :n], v[0, :n], ga[0]
                query = lax.broadcasted_iota(jnp.int32, (T, n), 0) + c * T
                key = lax.broadcasted_iota(jnp.int32, (T, n), 1)
                allowed = (cols_v[at, doc_at] == doc_row[0:1, :n]) & (key <= query)
                raw = jnp.where(allowed, nt(qt, kt) * scale, -1000000000.0)
                e = jnp.exp(raw - jnp.max(raw, -1, keepdims=True))
                p = e / jnp.sum(e, -1, keepdims=True)
                pb = p.astype(BF)
                att[at, cols] = dot(pb, vt).astype(BF)
                gp = nt(gt, vt)
                gs = (p * (gp - jnp.sum(gp * p, -1, keepdims=True))).astype(BF)
                gq = dot(gs, kt) * scale
                gproj[0, at, low] = back(gq[:, :128], at).astype(BF)
                gproj[0, at, high] = gq[:, 128:].astype(BF)
                dk_acc[:n, :] += tn(gs, qt)
                dv_acc[:n, :] += tn(pb, gt)

            for c in range(L // T):
                pl.when(i == c)(functools.partial(tile, c))

            @pl.when(i == L // T - 1)
            def _():
                gk = dk_acc[...] * scale
                gproj[1, :, low] = back(gk[:, :128], slice(None)).astype(BF)
                gproj[1, :, high] = gk[:, 128:].astype(BF)
                gproj[2, :, cols] = dv_acc[...].astype(BF)

        block = (1, T, hd)
        full = (1, L, hd)
        stream(
            body,
            (H, L // T),
            [
                (heads, block, lambda h, i: (h, i, 0)),
                (heads, full, lambda h, i: (H + h, 0, 0)),
                (heads, full, lambda h, i: (2 * H + h, 0, 0)),
                (gatt, block, lambda h, i: (h, i, 0)),
            ],
            [],
        )

    def norm_sums(grad, xb, at, row):
        cols = cols_of()
        hat = (xb[at, :].astype(F32) - cols_v[at, mean_at]) * cols_v[at, inv_at]
        sm[row : row + 1, cols] += jnp.sum(grad * hat, 0, keepdims=True)
        sm[row + 1 : row + 2, cols] += jnp.sum(grad, 0, keepdims=True)

    def one_phase():
        def body(w, xb, o):
            @chunks(L, CH)
            def _(at, m):
                grad = 0.0
                for j in range(3):
                    grad = grad + nt(gproj[j, at, :], w[:, :, :, j * l : (j + 1) * l].reshape(T, l))
                norm_sums(grad, xb, at, 0)
                o[at, :] = grad * vec[0:1, cols_of()]

        stream(body, (D // T,), [d_rows(qkv_all), lanes(x)], [lanes(wide_f)])

    per_ch = max(1, CH // tok)

    def two_phase():
        def body(wa, wb, xb, first, o):
            @chunks(L, per_ch * tok)
            def _(at, m):
                grad = nt(grad_up[at, :ffh], wa[...].reshape(T, ffh)) + nt(grad_up[at, ffh:ff], wb[...].reshape(T, ffh))
                norm_sums(grad, xb, at, 2)
                value = first[at, :] + grad * vec[2:3, cols_of()]
                o[pl.ds(m * per_ch, per_ch)] = value.astype(BF).reshape(per_ch, tok, T)

        stream(
            body,
            (D // T,),
            [d_rows(up_all[0]), d_rows(up_all[1]), lanes(x), lanes(wide_f)],
            [(wide, (S, tok, T), lambda i: (0, 0, i))],
        )

    def mixed_phase():
        def body(wa, wb, wo, o):
            @chunks(L, per_ch * tok)
            def _(at, m):
                value = dot(hidden[at, :ffh], wa[...].reshape(ffh, T)) + dot(hidden[at, ffh:], wb[...].reshape(ffh, T))
                value = value + dot(att[at, :], wo[...].reshape(l, T))
                o[pl.ds(m * per_ch, per_ch)] = value.astype(BF).reshape(per_ch, tok, T)

        cols = lambda ref: (ref, ref.shape[:2] + (T,), lambda i: (0, 0, i))
        ws = [cols(down_all[0]), cols(down_all[1]), cols(out_all)]
        stream(body, (D // T,), ws, [(mixed, (S, tok, T), lambda i: (0, 0, i))])

    def slope_phase(h):
        def body(w, slo):
            cols = cols_of(h * ffh)

            @chunks(L, CH)
            def _(at, m):
                gu = (nt(gy[at, :], w[...].reshape(T, D)) * slo[at, :].astype(F32)).astype(BF)
                grad_up[at, cols] = gu
                sm[5:6, cols] += jnp.sum(gu.astype(F32), 0, keepdims=True)

        w = (down_all[h], (T // rdh, rdh, D), lambda i: (i, 0, 0))
        stream(body, (ffh // T,), [w, lanes(slope[h])], [])

    ends = 2 if mx.square else 8
    part = tok // ends
    tiles = lambda ref, lead: (ref, (lead, part, D), lambda i: (0, i, 0))
    mine = lambda ref: (ref, (part, D), lambda i: (i, 0))

    def total_of(own, came):
        total = own[0].astype(F32)
        for ref in came:
            for k in range(ref.shape[0]):
                total = total + ref[k].astype(F32)
        return total

    def mixed_end():
        def body(xb, own, *rest):
            rest[-1][0] = (xb[...].astype(F32) + vec[4:5, :] + total_of(own, rest[:-1])).astype(BF)

        stream(body, (ends,), [mine(x_own), tiles(mixed.at[pl.ds(s, 1)], 1)] + mx.ins(part), [tiles(mixed_out, 1)])

    def input_end():
        def body(xb, gb, own, *rest):
            at = pl.ds(pl.multiple_of(s * tok + pl.program_id(0) * part, part), part)
            inv = cols_v[at, inv_at]
            hat = (xb[...].astype(F32) - cols_v[at, mean_at]) * inv
            total = total_of(own, rest[:-1])
            total = total - jnp.mean(total, -1, keepdims=True) - hat * jnp.mean(total * hat, -1, keepdims=True)
            rest[-1][0] = gb[...].astype(F32) + inv * total

        ins = [mine(x_own), mine(gy_own), tiles(wide.at[pl.ds(s, 1)], 1)] + wx.ins(part)
        stream(body, (ends,), ins, [tiles(input_grad, 1)])

    net.barrier()
    loc.start()
    for load in up_loads:
        load.start()
    small_first()
    o_g.early()
    o_g.start()
    for x_sq in sq:
        x_sq.start()
    cut_up()
    su[0].start()
    o_g.go(1)
    loc.finish()
    for x_sq in sq:
        x_sq.wait()
    q_g.early()
    q_g.start()
    x_g.start()
    su[0].wait()
    u_g[0].early()
    o_g.go(2)
    u_g[0].start()
    o_g.go(3)
    small_second()
    x_g.relay()
    gy_g.start()
    u_g[0].go(1)
    u_g[0].go(2)
    x_g.wait()
    unpack()
    norm_phase()
    u_g[0].go(3)
    d_g[1].early()
    q_g.go(1)
    gy_g.relay()
    su[1].start()
    u_g[0].wait()
    up_phase(0)
    d_g[0].early()
    q_g.go(2)
    gy_g.wait()
    down_grad_phase(0)
    su[1].wait()
    u_g[1].early()
    ds[0].start()
    u_g[1].start()
    o_g.wait()
    d_g[1].start()
    ds[0].pair()
    d_g[0].start()
    q_g.go(3)
    gatt_phase()
    q_g.wait()
    qkv_phase()
    att_phase()
    out_grad_phase()
    os.start()
    d_g[0].go(1)
    u_g[1].go(1)
    os.pair()
    qkv_grad_phase()
    qs.start()
    ds[0].go(1)
    qs.pair()
    d_g[0].go(2)
    one_phase()
    d_g[0].go(3)
    u_g[1].go(2)
    d_g[1].go(1)
    d_g[0].wait()
    slope_phase(0)
    qs.go(1)
    up_grad_phase(0)
    u_g[1].go(3)
    u_g[1].wait()
    d_g[1].go(2)
    os.go(1)
    us[0].start()
    up_phase(1)
    ds[0].go(2)
    d_g[1].go(3)
    us[0].pair()
    d_g[1].wait()
    mixed_phase()
    qs.go(2)
    mx.start()
    slope_phase(1)
    up_grad_phase(1)
    us[1].start()
    os.go(2)
    qs.go(3)
    qs.total()
    qx.start()
    us[0].go(1)
    us[1].pair()
    down_grad_phase(1)
    mx.mid()
    us[0].go(2)
    us[1].go(1)
    two_phase()
    sums_first()
    wx.start()
    us[0].go(3)
    us[0].total()
    ds[1].start()
    us[1].go(2)
    sums_second()
    ds[0].go(3)
    ds[1].pair()
    ds[1].go(1)
    down_total(0)
    qx.wait()
    us[1].go(3)
    mx.wait()
    mixed_end()
    us[1].total()
    ux[1].start()
    wx.mid()
    ds[1].go(2)
    ux[0].start()
    wx.wait()
    os.go(3)
    ux[1].wait()
    input_end()
    ds[1].go(3)
    out_total()
    down_total(1)
    ux[0].wait()
    sm_x.wait()
    for copy in [out_copies[0]] + begun:
        copy.wait()
    net.drain()


def layer(seq_n, dp_n, dims, args):
    L, D, ff, H, r, ro, rd = dims
    l, Z, ffh, rdh = H * HD, dp_n // 2, ff // 2, rd // 2
    tok = L // seq_n
    seq_tok, up_slab, qkv_slab = (seq_n, tok, D), (seq_n, r, ffh), (seq_n, r, 3 * l)
    outs = [((1, tok, D), BF), ((1, tok, D), F32), (qkv_slab, BF), ((1, ro, D), F32), ((1, rd, D), F32), ((seq_n, 8, D), F32)]
    outs += [(up_slab, BF)] * 2
    half = tok // 2
    if seq_n == 4:
        outs += [((4, half, D), BF), ((2, half, D), BF), ((2, half, D), BF)] * 2
    else:
        outs += [((seq_n - 1, tok, D), BF), ((16, 128), BF), ((16, 128), BF)] * 2
    outs += [((L, D), BF), ((seq_n, dp_n, r, 3 * l), BF), ((dp_n, ro, D), BF), ((3 * H, L, HD), BF), ((H, L, HD), BF)]
    outs += [((L, D), F32), ((seq_n, dp_n, r, 3 * l), BF), ((dp_n, ro, D), BF), (seq_tok, BF), (seq_tok, BF)]
    up_full, down_full = (seq_n, dp_n, r, ffh), (dp_n, rdh, D)
    for v in (up_full, down_full, (L, ffh), up_full, down_full):
        outs += [(v, BF)] * 2
    slabs = [(1, rdh, D)] * 2 + [up_slab] * 2 + [qkv_slab, (1, ro, D)]
    for slab in slabs:
        outs += [((Z - 1,) + slab, BF)] * 2
    out_shape = [shape(*o) for o in outs]
    n = 6 * (4 * Z - 3) + 6 * (3 * Z - 2) + 14 * (seq_n - 1) + 2 * max(4, seq_n - 1) + 2 * (dp_n - 1)
    vmem = [((seq_n, dp_n, 16, 128), F32), ((8, D), F32), ((8, ffh), F32), ((8, 3 * l), F32), ((8, L), F32), ((L, 128), F32)]
    vmem += [((8, D), F32), ((dp_n, 8, D), F32), ((8, D), F32), ((L, HD), F32), ((L, HD), F32)]
    vmem += [((1, ro, D), F32), ((1, rdh, D), F32), ((2, L, 128), F32)]
    vmem += [((L, D), BF), ((L, D), BF), ((L, D), BF), ((L, ff), BF), ((L, l), BF), ((3, L, l), BF)]
    for slab in slabs:
        vmem += [((Z,) + slab, BF)] * 2
    scratch = [pltpu.SemaphoreType.DMA((k,)) for k in (n, n, 40 + seq_n + 6 * (3 * Z - 2))] + [pltpu.VMEM(*v) for v in vmem]
    return pl.pallas_call(
        functools.partial(layer_kernel, seq_n, dp_n, dims, len(args), len(outs)),
        out_shape=out_shape,
        in_specs=[ANY] * len(args),
        out_specs=[ANY] * len(outs),
        scratch_shapes=scratch,
        compiler_params=pltpu.CompilerParams(collective_id=0, has_side_effects=True, vmem_limit_bytes=63 * MIB),
        name="layer",
    )(*args)[:8]


def last_kernel(dims, seq_n, dp_n, places, *refs):
    L, D, ff, H, r, ro, rd = dims
    l, ffh, rdh = H * HD, ff // 2, rd // 2
    ins, outs, acc = refs[:8], refs[8:-1], refs[-1]
    mixed, grad, qkv, out_w, down, sums, up_a, up_b = ins
    mixed_out, grad_out, up_out, qkv_out, out_out, down_out = outs[:6]
    small = outs[6:]
    mixed_out[...] = mixed[...]
    grad_out[...] = grad[...]
    out_out[...] = out_w[0]
    down_out[...] = down[0]
    for k in range(seq_n):
        for m in range(dp_n):
            for h, src in enumerate((up_a, up_b)):
                at = k * ff + m * rd + h * rdh
                up_out[:, at : at + rdh] = src[k, :, m * rdh : (m + 1) * rdh].astype(F32)
        for j in range(3):
            at = (j * seq_n + k) * l
            qkv_out[:, at : at + l] = qkv[k, :, j * l : (j + 1) * l].astype(F32)

    @pl.when(pl.program_id(0) == 0)
    def _():
        s, d = places[0], places[1]
        place = s * dp_n + d
        acc[...] = sums[0]
        for k in range(1, seq_n):
            acc[...] += sums[k]

        def piece(load, lane):
            start = pl.multiple_of(lax.div(lane, 128) * 128, 128)
            return pltpu.roll(load(pl.ds(start, 128)), lax.rem(128 - lax.rem(lane, 128), 128), 1)

        for j in range(5):
            small[j][...] = piece(lambda at, j=j: acc[j : j + 1, at], place * r)[:, :r]
        for t in range(3):
            at = place * 3 + t
            j, rest = lax.div(at, D // r), lax.rem(at, D // r)
            of, m = lax.div(rest, l // r), lax.rem(rest, l // r)
            small[5][:, t * r : (t + 1) * r] = piece(lambda at, of=of: sums[of, 6:7, at], j * l + m * r)[:, :r]
        for h in range(2):
            small[6][:, h * rdh : (h + 1) * rdh] = piece(lambda at: sums[s, 5:6, at], h * ffh + d * rdh)[:, :rdh]


def finish(seq_n, dp_n, dims, got):
    L, D, ff, H, r, ro, rd = dims
    tok = L // seq_n
    steps = 4 if r % 64 == 0 else 1
    places = jnp.stack([lax.axis_index("seq"), lax.axis_index("dp")]).astype(jnp.int32)

    def spec(v, axis):
        block = tuple(n // steps if k == axis else n for k, n in enumerate(v.shape))
        return pl.BlockSpec(block, lambda i, p: tuple(i if k == axis else 0 for k in range(v.ndim)))

    outs = [((1, tok, D), BF, 1), ((1, tok, D), F32, 1), ((r, seq_n * ff), F32, 0), ((r, 3 * D), F32, 0), ((ro, D), F32, 0), ((rd, D), F32, 0)]
    outs += [((1, r), F32, None)] * 5 + [((1, 3 * r), F32, None), ((1, rd), F32, None)]
    out_shape = [shape(*o[:2]) for o in outs]
    return pl.pallas_call(
        functools.partial(last_kernel, dims, seq_n, dp_n),
        grid_spec=pltpu.PrefetchScalarGridSpec(
            num_scalar_prefetch=1,
            grid=(steps,),
            in_specs=[spec(v, axis) for v, axis in zip(got, (1, 1, 1, 1, 1, None, 1, 1))],
            out_specs=[spec(v, o[2]) for v, o in zip(out_shape, outs)],
            scratch_shapes=[pltpu.VMEM((8, D), F32)],
        ),
        out_shape=out_shape,
        compiler_params=pltpu.CompilerParams(vmem_limit_bytes=63 * MIB),
        name="finish",
    )(places, *got)
def shards(
    tokens,
    doc_ids,
    ln1_gain,
    ln1_bias,
    ln2_gain,
    ln2_bias,
    qkv_weight,
    qkv_bias,
    out_weight,
    up_weight,
    up_bias,
    down_weight,
    out_bias,
    cotangent,
):
    seq_n = lax.axis_size("seq")
    dp_n = lax.axis_size("dp")
    seq_i = lax.axis_index("seq")
    tok_rows, width = tokens.shape[1:]
    length = tok_rows * seq_n
    head_dim = width // HEADS
    heads = HEADS // seq_n
    local = heads * head_dim
    ff = up_weight.shape[1] // seq_n
    rot_dims = head_dim // 4
    rows, per_down = qkv_weight.shape[0], down_weight.shape[0]
    vectors = (ln1_gain, ln1_bias, ln2_gain, ln2_bias, out_bias, qkv_bias, up_bias)
    total, at, flat = sum(v.shape[0] for v in vectors), 0, 0.0
    for v in vectors:
        flat = flat + jnp.pad(v.astype(F32), (at, total - at - v.shape[0]))
        at += v.shape[0]
    pieces = jnp.tile(flat.reshape(-1, rows), (1, 128 // rows))
    docs = doc_ids.astype(F32).reshape(-1, 128)
    over = 16 - pieces.shape[0]
    small = jnp.pad(pieces, ((0, over), (0, 0))) + jnp.pad(docs, ((16 - over, over - docs.shape[0]), (0, 0)))
    dims = (length, width, ff, heads, rows, out_weight.shape[0], per_down)
    tables = jnp.asarray(rotary_rows(length, rot_dims))
    x, gy = tokens[0], cotangent[0]
    got = layer(seq_n, dp_n, dims, (x, gy, up_weight, qkv_weight, out_weight, down_weight, small, tables))
    mixed, input_grad, up_grad, qkv_grad, out_grad, down_grad, *small = finish(seq_n, dp_n, dims, got)
    g1, b1, g2, b2, ob, qb, ub = [v.reshape(-1) for v in small]
    return (mixed, input_grad, g1, b1, g2, b2, qkv_grad, qb, out_grad, up_grad, ub, down_grad, ob)


def solution(mesh):
    in_specs = (
        P("dp", "seq", None),
        P("dp", "seq"),
        P(("seq", "dp")),
        P(("seq", "dp")),
        P(("seq", "dp")),
        P(("seq", "dp")),
        P(("seq", "dp"), None),
        P(("seq", "dp")),
        P(("seq", "dp"), None),
        P(("seq", "dp"), None),
        P(("seq", "dp")),
        P(("seq", "dp"), None),
        P(("seq", "dp")),
        P("dp", "seq", None),
    )
    out_specs = (
        P("dp", "seq", None),
        P("dp", "seq", None),
        P(("seq", "dp")),
        P(("seq", "dp")),
        P(("seq", "dp")),
        P(("seq", "dp")),
        P(("seq", "dp"), None),
        P(("seq", "dp")),
        P(("seq", "dp"), None),
        P(("seq", "dp"), None),
        P(("seq", "dp")),
        P(("seq", "dp"), None),
        P(("seq", "dp")),
    )
    return jax.shard_map(shards, mesh=mesh, in_specs=in_specs, out_specs=out_specs, check_vma=False)
```

```python
import functools
import math

import jax
import jax.numpy as jnp
import numpy as np
from jax import lax
from jax.experimental import pallas as pl
from jax.experimental.pallas import tpu as pltpu
from jax.sharding import PartitionSpec as P

HEADS = 8
BF = jnp.bfloat16
F32 = jnp.float32


epsilon = 1e-05


def rotary_rows(length, rot_dims):
    half = rot_dims // 2
    exponents = np.arange(half, dtype=np.float32) * np.float32(2.0 / rot_dims)
    inverse = np.power(np.float32(10000.0), -exponents).astype(np.float32)
    phase = (np.arange(length, dtype=np.float32)[:, None] * inverse[None, :]).astype(np.float64)
    tables = np.zeros((2, length, 128), np.float32)
    tables[0] = 1.0
    tables[0, :, :half] = tables[0, :, half:rot_dims] = np.cos(phase)
    tables[1, :, :half] = -np.sin(phase)
    tables[1, :, half:rot_dims] = np.sin(phase)
    return tables


def dot(left, right):
    return jnp.dot(left, right, preferred_element_type=F32)


MESH = pl.DeviceIdType.MESH


def run(when, action):
    if when is None:
        action()
    else:
        pl.when(when)(lambda: action())


class Net:
    def __init__(self, seq_n, dp_n, send_sems, recv_sems, local_sems):
        self.S, self.DP, self.Z = seq_n, dp_n, dp_n // 2
        self.s, self.d = lax.axis_index("seq"), lax.axis_index("dp")
        self.z, self.c = self.d // 2, lax.rem(self.d, 2)
        self.send_sems, self.recv_sems, self.used = send_sems, recv_sems, 0
        self.local_sems, self.local_used = local_sems, 0
        self.sent = []

    def seq_peer(self, s):
        return (s, self.d)

    def line_peer(self, z):
        return (self.s, 2 * jnp.clip(z, 0, self.Z - 1) + self.c)

    def partner(self):
        return (self.s, 2 * self.z + 1 - self.c)

    def copy(self, src, dst, device):
        self.used += 1
        return self.copy_at(self.used - 1, src, dst, device)

    def copy_at(self, i, src, dst, device):
        return pltpu.make_async_remote_copy(
            src_ref=src,
            dst_ref=dst,
            send_sem=self.send_sems.at[i],
            recv_sem=self.recv_sems.at[i],
            device_id=device,
            device_id_type=MESH,
        )

    def send(self, copy, when=None):
        self.sent.append((copy, when))
        run(when, copy.start)

    def drain(self):
        for copy, when in self.sent:
            run(when, copy.wait_send)

    def near(self, src, dst):
        self.local_used += 1
        return pltpu.make_async_copy(src, dst, self.local_sems.at[self.local_used - 1])

    def barrier(self):
        sem = pltpu.get_barrier_semaphore()
        peers = [self.seq_peer(lax.rem(self.s + k, self.S)) for k in range(1, self.S)]
        peers += [(self.s, lax.rem(self.d + k, self.DP)) for k in range(1, self.DP)]
        for device in peers:
            pl.semaphore_signal(sem, inc=1, device_id=device, device_id_type=MESH)
        pl.semaphore_wait(sem, len(peers))


class Place:
    def __init__(self, net, direct, through):
        self.direct = [net.near(src, dst) for src, dst in direct]
        self.loads = [net.near(src, buf) for src, buf, _ in through]
        self.stores = [net.near(buf, dst) for _, buf, dst in through]

    def start(self):
        for copy in self.loads + self.direct:
            copy.start()

    def finish(self):
        for load, store in zip(self.loads, self.stores):
            load.wait()
            store.start()
        for copy in self.stores + self.direct:
            copy.wait()


class Exchange:
    def __init__(self, net, src, slot, by_turn=False, own=False, settle=False):
        self.net, self.copies, self.settle = net, [], settle
        for k in range(1, net.S):
            to = lax.rem(net.s + k, net.S)
            self.copies.append(net.copy(src(to), slot(k - 1 if by_turn else net.s), net.seq_peer(to)))
        self.own = net.near(src(net.s), slot(net.s)) if own else None

    def start(self):
        for copy in self.copies:
            if self.settle:
                copy.start()
            else:
                self.net.send(copy)
        if self.own is not None:
            self.own.start()

    def wait(self):
        for copy in self.copies:
            copy.wait_recv()
            if self.settle:
                copy.wait_send()
        if self.own is not None:
            self.own.wait()


class GatherSeq:
    def __init__(self, net, src, slot):
        self.net, self.square = net, net.S == 4
        if self.square:
            s = net.s
            a, b = s + 1 - 2 * lax.rem(s, 2), lax.rem(s + 2, 4)
            self.first = [net.copy(src, slot(s, None), net.seq_peer(p)) for p in (a, b)]
            self.second = [
                net.copy(slot(a, 0), slot(a, 0), net.seq_peer(b)),
                net.copy(slot(b, 1), slot(b, 1), net.seq_peer(a)),
            ]
        else:
            self.direct = Exchange(net, lambda to: src, lambda k: slot(k, None))

    def start(self):
        if self.square:
            for copy in self.first:
                self.net.send(copy)
        else:
            self.direct.start()

    def relay(self):
        if self.square:
            for came, onward in zip(self.first, self.second):
                came.wait_recv()
                self.net.send(onward)

    def wait(self):
        if self.square:
            for copy in self.second:
                copy.wait_recv()
        else:
            self.direct.wait()


class SumSeq:
    def __init__(self, net, src, came, onward, held):
        self.net, self.src, self.came, self.onward, self.held, self.square = net, src, came, onward, held, net.S == 4
        if not self.square:
            self.direct = Exchange(net, lambda k: src.at[k], lambda k: came.at[k], by_turn=True)
            return
        s, half = net.s, src.shape[1] // 2
        a, b, across = s + 1 - 2 * lax.rem(s, 2), lax.rem(s + 2, 4), 3 - s
        self.ways = (b, a)
        part = lambda k, h: src.at[k, pl.ds(h * half, half)]
        self.first = []
        for h, near in ((0, a), (1, b)):
            for i, block in enumerate((near, across)):
                self.first.append(net.copy(part(block, h), came.at[2 * h + i], net.seq_peer(near)))
        self.second = [net.copy(held.at[h], onward.at[h], net.seq_peer(to)) for h, to in ((0, b), (1, a))]

    def start(self):
        if self.square:
            for i in (1, 3, 0, 2):
                self.net.send(self.first[i])
        else:
            self.direct.start()

    def mid(self):
        if not self.square:
            return
        b, a = self.ways
        half, width = self.held.shape[1:]
        for i in (1, 3):
            self.first[i].wait_recv()

        def body(own, other, o):
            o[...] = (own[...].astype(F32) + other[...].astype(F32)).astype(BF)

        block = (1, half, width)
        stream(
            body,
            (2,),
            [
                (self.src, block, lambda h: (jnp.where(h == 0, b, a), h, 0)),
                (self.came, block, lambda h: (2 * h + 1, 0, 0)),
            ],
            [(self.held, block, lambda h: (h, 0, 0))],
        )
        for copy in self.second:
            self.net.send(copy)

    def wait(self):
        if self.square:
            for i in (0, 2):
                self.first[i].wait_recv()
            for copy in self.second:
                copy.wait_recv()
        else:
            self.direct.wait()

    def ins(self, rows):
        if self.square:
            block = (1, rows, self.src.shape[2])
            return [(self.came, block, lambda i: (2 * i, 0, 0)), (self.onward, block, lambda i: (i, 0, 0))]
        return [(self.came, (self.net.S - 1, rows, self.src.shape[2]), lambda i: (0, i, 0))]


class Line:
    def go(self, part):
        last = self.net.Z - 1
        for t in ([1], range(2, last), [last])[part - 1]:
            self.step(t)


class GatherLine(Line):
    def __init__(self, net, slab, own=None):
        self.net = net
        z, c, last = net.z, net.c, net.Z - 1
        own = slab(net.d) if own is None else own
        self.right, self.left = [], []
        for t in range(net.Z):
            for side, hops in ((1, self.right), (-1, self.left)):
                place = slab(2 * jnp.clip(z - side * t, 0, last) + c)
                src = own if t == 0 else place
                there = z >= t if side == 1 else z <= last - t
                onward = z < last if side == 1 else z > 0
                copy = None if t == last else net.copy(src, place, net.line_peer(z + side))
                core = None if t == 0 and side == -1 else net.copy(src, place, net.partner())
                hops.append((copy, there & onward, core, None if t == 0 else there))

    def early(self):
        self.net.send(self.right[0][0], self.net.z == 0)
        self.net.send(self.left[0][0], self.net.z == self.net.Z - 1)

    def start(self):
        inside = (self.net.z > 0) & (self.net.z < self.net.Z - 1)
        self.net.send(self.right[0][0], inside)
        self.net.send(self.left[0][0], inside)
        self.net.send(self.right[0][2])

    def step(self, t):
        for hops in (self.right, self.left):
            copy, sends, core, there = hops[t]
            run(there, hops[t - 1][0].wait_recv)
            if copy is not None:
                self.net.send(copy, sends)
            self.net.send(core, there)

    def wait(self):
        for hops in (self.right, self.left):
            for _, _, core, there in hops:
                if core is not None:
                    run(there, core.wait_recv)


def add_slabs(dst, left, right):
    blocks, rows = dst.shape[0], dst.shape[1]
    per = rows // 16

    @pl.loop(0, blocks * per)
    def _(i):
        at = (i // per, pl.ds(pl.multiple_of(lax.rem(i, per) * 16, 16), 16), slice(None))
        dst[at] = (left[at].astype(F32) + right[at].astype(F32)).astype(dst.dtype)


class ReduceLine(Line):
    def __init__(self, net, part, own, mate, from_left, from_right):
        self.net, self.own, self.mate, self.bufs = net, own, mate, (from_left, from_right)
        z, c, Z = net.z, net.c, net.Z
        self.order = []
        for t in range((Z + 1) // 2):
            self.order += [Z - 1 - t] + ([t] if t != Z - 1 - t else [])
        self.swaps = {k: net.copy(part(2 * k + 1 - c), mate.at[k], net.partner()) for k in self.order}
        self.loads = {k: net.near(part(2 * k + c), own.at[k]) for k in self.order}
        self.base = net.used
        net.used += 2 * (Z - 1)
        ends = (jnp.clip(Z - 1 - z, 0, Z - 2), jnp.clip(z, 0, Z - 2))
        self.last = [net.near(buf.at[t], mate.at[i]) for i, (buf, t) in enumerate(zip(self.bufs, ends))]

    def start(self):
        for k in self.order:
            self.net.send(self.swaps[k])
            self.loads[k].start()

    def hop(self, side, t):
        net, last = self.net, self.net.Z - 1
        place, way = (last - t, 0) if side == 1 else (t, 1)
        return net.copy_at(
            self.base + way * last + t, self.own.at[place], self.bufs[way].at[t], net.line_peer(net.z + side)
        )

    def pair(self):
        net, done = self.net, set()
        last = net.Z - 1
        right, left = last, 0
        for k in self.order:
            self.loads[k].wait()
            self.swaps[k].wait_recv()
            add_slabs(self.own.at[k], self.own.at[k], self.mate.at[k])
            done.add(k)
            while right > 0 and right in done:
                net.send(self.hop(1, last - right), net.z == 0)
                right -= 1
            while left < last and left in done:
                net.send(self.hop(-1, left), net.z == last)
                left += 1

    def step(self, n):
        net = self.net
        z, last = net.z, net.Z - 1
        for side, far, way in ((1, z, 0), (-1, last - z, 1)):
            t = jnp.clip(n - far, 0, last - 1)
            here = (far >= 1) & (far <= n)
            hop = self.hop(side, t)
            run(here, hop.wait_recv)
            if n < last:
                place, held = last - t if side == 1 else t, self.mate.at[way]
                load = net.near(self.bufs[way].at[t], held)

                def add():
                    load.start()
                    load.wait()
                    add_slabs(self.own.at[place], self.own.at[place], held)

                run(here, add)
                net.send(hop, here)

    def total(self, out=None):
        z, last = self.net.z, self.net.Z - 1
        out = self.own.at[z] if out is None else out
        here = (z > 0, z < last)
        for copy, when in zip(self.last, here):
            run(when, copy.start)
        for copy, when in zip(self.last, here):
            run(when, copy.wait)
        per = out.shape[1] // 16

        def body(ways):
            @pl.loop(0, out.shape[0] * per)
            def _(i):
                at = (i // per, pl.ds(pl.multiple_of(lax.rem(i, per) * 16, 16), 16), slice(None))
                value = self.own.at[z][at].astype(F32)
                for way in ways:
                    value = value + self.mate[(way,) + at].astype(F32)
                out[at] = value.astype(out.dtype)

        run(z == 0, lambda: body((1,)))
        run(z == last, lambda: body((0,)))
        if last > 1:
            run((z > 0) & (z < last), lambda: body((0, 1)))


ANY = pl.BlockSpec(memory_space=pl.ANY)
MIB = 1024 * 1024
HD = 256
shape = jax.ShapeDtypeStruct


def nt(left, right):
    return lax.dot_general(left, right, (((1,), (1,)), ((), ())), preferred_element_type=F32)


def tn(left, right):
    return lax.dot_general(left, right, (((0,), (0,)), ((), ())), preferred_element_type=F32)


def turn(value, cosine, sine):
    half = HD // 8
    first = lax.broadcasted_iota(jnp.int32, value.shape, 1) < half
    other = jnp.where(first, pltpu.roll(value, 128 - half, 1), pltpu.roll(value, half, 1))
    return value * cosine + other * sine


def stream(body, grid, ins, outs):
    def spec(entry):
        block, index = entry[1:3]
        return pl.BlockSpec(block, index, pipeline_mode=pl.Buffered(1)) if len(entry) > 3 else pl.BlockSpec(block, index)

    pltpu.emit_pipeline(
        body, grid=grid, in_specs=[spec(e) for e in ins], out_specs=[spec(e) for e in outs]
    )(*[e[0] for e in ins], *[e[0] for e in outs])


def whole(ref):
    return (ref, ref.shape, lambda *i: (0,) * len(ref.shape), 1)


def chunks(rows, size):
    return lambda body: pl.loop(0, rows // size)(lambda i: body(pl.ds(pl.multiple_of(i * size, size), size), i))


def layer_kernel(seq_n, dp_n, dims, n_ins, n_outs, *refs):
    ins, outs = refs[:n_ins], refs[n_ins : n_ins + n_outs]
    scratch = refs[n_ins + n_outs :]
    x_own, gy_own, up_w, qkv_w, out_w, down_w, small, tables = ins
    mixed_out, input_grad, qkv_red, out_red, down_red, small_red = outs[:6]
    up_red, mixed_bufs, wide_bufs = outs[6:8], outs[8:11], outs[11:14]
    x, qkv_all, out_all, heads, gatt, wide_f, p_qkv, p_out, mixed, wide = outs[14:24]
    up_all, down_all, slope, p_up, p_down = [outs[24 + 2 * i : 26 + 2 * i] for i in range(5)]
    hops = outs[34:]
    sems, scratch = scratch[:3], scratch[3:]
    small_v, vec, up_b, qkv_b, doc_row, cols_v, sm, sm_dp, sm_sum, dk_acc, dv_acc = scratch[:11]
    out_f, down_f, tab, gy, n1, n2, hidden, att, gproj = scratch[11:20]
    scratch = scratch[20:]
    mean_at, inv_at, doc_at = [slice(k, k + 1) for k in range(3)]
    grad_up = n1
    L, D, ff, H, r, ro, rd = dims
    hd = HD
    T, CH = (HD, 512) if L <= 1024 else (HD // 2, 256)
    l, ffh, rdh, half_n = H * hd, ff // 2, rd // 2, 2
    net = Net(seq_n, dp_n, *sems)
    S, Z, s, d = net.S, net.Z, net.s, net.d
    tok = L // S
    scale = 1.0 / math.sqrt(hd)
    per = dp_n * r // T
    own_rows = pl.ds(pl.multiple_of(s * tok, tok), tok)

    def lanes(ref):
        return (ref, (ref.shape[0], T), lambda i: (0, i))

    def d_rows(ref):
        return (ref, (1, T // r, r, ref.shape[3]), lambda i: (lax.div(i, per), lax.rem(i, per), 0, 0))

    def reduce(i, part):
        return ReduceLine(net, part, scratch[2 * i], scratch[2 * i + 1], hops[2 * i], hops[2 * i + 1])

    def seq_rows(ref):
        def slot(k, h):
            size = tok if h is None else tok // 2
            return ref.at[pl.ds(pl.multiple_of(k * tok + (h or 0) * size, size), size)]

        return slot

    halves = range(half_n)
    x_g, gy_g = GatherSeq(net, x_own, seq_rows(x)), GatherSeq(net, gy_own, seq_rows(gy))
    up_cut = scratch[7]
    su = [
        Exchange(net, lambda k, h=h: up_cut.at[h, k], lambda k, h=h: up_all[h].at[k, d], own=True, settle=True)
        for h in halves
    ]
    sq = [
        Exchange(
            net,
            lambda k, j=j: qkv_w.at[:, pl.ds(pl.multiple_of((j * S + k) * l, 128), l)],
            lambda k, j=j: qkv_all.at[k, d, :, pl.ds(j * l, l)],
        )
        for j in range(3)
    ]
    o_g = GatherLine(net, lambda k: out_all.at[k], out_w)
    q_g = GatherLine(net, lambda k: qkv_all.at[:, k])
    u_g = [GatherLine(net, lambda k, h=h: up_all[h].at[:, k]) for h in halves]
    down_rows = [down_w.at[pl.ds(h * rdh, rdh)] for h in halves]
    d_g = [GatherLine(net, lambda k, h=h: down_all[h].at[k], down_rows[h]) for h in halves]
    ds = [reduce(h, lambda k, h=h: p_down[h].at[pl.ds(k, 1)]) for h in halves]
    us = [reduce(2 + h, lambda k, h=h: p_up[h].at[:, k]) for h in halves]
    qs = reduce(4, lambda k: p_qkv.at[:, k])
    os = reduce(5, lambda k: p_out.at[pl.ds(k, 1)])
    mx = SumSeq(net, mixed, *mixed_bufs)
    wx = SumSeq(net, wide, *wide_bufs)
    qx = Exchange(net, lambda k: qs.own.at[net.z, k], lambda k: qkv_red.at[k], own=True)
    ux = [Exchange(net, lambda k, h=h: us[h].own.at[net.z, k], lambda k, h=h: up_red[h].at[k], own=True) for h in halves]
    sf = Exchange(net, lambda k: small_v.at[s], lambda k: small_v.at[k])
    sm_x = Exchange(net, lambda k: sm_sum, lambda k: small_red.at[k], own=True)
    small_to = [lax.rem(d + k, dp_n) for k in range(1, dp_n)]
    small_from = [lax.rem(d + dp_n - k, dp_n) for k in range(1, dp_n)]
    sf_dp = [net.copy(small, small_v.at[s, d], (s, to)) for to in small_to]
    sm_to = [net.copy(sm, sm_dp.at[d], (s, to)) for to in small_to]
    sf_own = net.near(small, small_v.at[s, d])
    spot = lambda at, rows, base, width: n1.at[pl.ds(at, rows), pl.ds(base, width)]
    loc = Place(
        net,
        [(gy_own, gy.at[own_rows]), (tables, tab)],
        [
            (
                qkv_w.at[:, pl.ds(pl.multiple_of((j * S + s) * l, 128), l)],
                spot(tok + ro, r, j * l, l),
                qkv_all.at[s, d, :, pl.ds(j * l, l)],
            )
            for j in range(3)
        ]
        + [(x_own, spot(0, tok, 0, D), x.at[own_rows]), (out_w, spot(tok, ro, 0, D), out_all.at[d])]
        + [(down_rows[h], scratch[2 * h].at[0, 0], down_all[h].at[d]) for h in halves],
    )
    up_loads = [net.near(up_w.at[:, pl.ds(k * ff, ff)], n2.at[pl.ds(k * r, r), pl.ds(0, ff)]) for k in range(S)]
    out_copies = [net.near(out_f, out_red)] + [net.near(down_f, down_red.at[:, pl.ds(h * rdh, rdh)]) for h in halves]
    begun = []

    def out_total():
        os.total(out_f)
        out_copies[0].start()

    def down_total(h):
        for copy in begun:
            copy.wait()
        ds[h].total(down_f)
        out_copies[1 + h].start()
        begun[:] = [out_copies[1 + h]]

    def cut_up():
        for k, load in enumerate(up_loads):
            load.wait()
            rows = slice(k * r, (k + 1) * r)
            for m in range(dp_n):
                for h in halves:
                    up_cut[h, k, :, m * rdh : (m + 1) * rdh] = n2[rows, m * rd + h * rdh : m * rd + (h + 1) * rdh]

    def small_first():
        sf_own.start()
        for copy in sf_dp:
            net.send(copy)

    def small_second():
        sf_own.wait()
        for copy in sf_dp:
            copy.wait_recv()
        sf.start()

    def sums_first():
        for copy in sm_to:
            net.send(copy)

    def sums_second():
        sm_sum[...] = sm[...]
        for copy, source in zip(sm_to, small_from):
            copy.wait_recv()
            sm_sum[...] += sm_dp[source]
        sm_x.start()

    def pieces(out, row, found):
        lane = lax.broadcasted_iota(jnp.int32, (1, 128), 1) // r
        q = 128 // r
        for p in range(len(found) // q):
            value = small_v[found[p * q]]
            for k in range(1, q):
                value = jnp.where(lane == k, small_v[found[p * q + k]], value)
            out[row : row + 1, 128 * p : 128 * p + 128] = value

    def unpack():
        sf.wait()
        for j in range(5):
            pieces(vec, j, [(i // dp_n, i % dp_n, slice(j, j + 1)) for i in range(seq_n * dp_n)])
        for h in halves:
            pieces(up_b, h, [(s, m // 2, slice(8 + 2 * h + m % 2, 9 + 2 * h + m % 2)) for m in range(2 * dp_n)])
        found = []
        for j in range(3):
            for m in range(l // r):
                piece = j * (D // r) + s * (l // r) + m
                owner = lax.div(piece, 3)
                found.append((lax.div(owner, dp_n), lax.rem(owner, dp_n), pl.ds(5 + lax.rem(piece, 3), 1)))
        pieces(qkv_b, 0, found)
        for k in range(S):
            for j in range(tok // 128):
                row = small_v[k, d, 12 + j : 13 + j]
                at = k * tok + j * 128
                doc_row[0:1, at : at + 128] = row
                cols_v[at : at + 128, :] = jnp.transpose(jnp.broadcast_to(row, (128, 128)))
        sm[...] = jnp.zeros_like(sm)
        sm[4:5, :] = jnp.sum(gy[own_rows, :].astype(F32), 0, keepdims=True)

    def cols_of(base=0):
        return pl.ds(pl.multiple_of(base + pl.program_id(0) * T, T), T)

    def norm_phase():
        def body(xb):
            i = pl.program_id(0)
            at = pl.ds(pl.multiple_of(i * T, T), T)
            wide_x = xb[...].astype(F32)
            mean = jnp.mean(wide_x, -1, keepdims=True)
            center = wide_x - mean
            inv = lax.rsqrt(jnp.mean(center * center, -1, keepdims=True) + epsilon)
            cols_v[at, mean_at] = mean
            cols_v[at, inv_at] = inv
            hat = center * inv
            n1[at, :] = (hat * vec[0:1, :] + vec[1:2, :]).astype(BF)
            n2[at, :] = (hat * vec[2:3, :] + vec[3:4, :]).astype(BF)

        stream(body, (L // T,), [(x, (T, D), lambda i: (i, 0))], [])

    def up_phase(h):
        def body(w, slo):
            cols = cols_of(h * ffh)
            bias = up_b[h : h + 1, cols_of()]

            @chunks(L, CH)
            def _(at, i):
                u = dot(n2[at, :], w[...].reshape(D, T)) + bias
                phi = 0.5 + 0.5 * lax.erf(u * math.sqrt(0.5))
                hidden[at, cols] = (u * phi).astype(BF)
                slo[at, :] = (phi + u * (jnp.exp(-0.5 * u * u) * (1.0 / math.sqrt(2.0 * math.pi)))).astype(BF)

        stream(body, (ffh // T,), [(up_all[h], (S, dp_n, r, T), lambda i: (0, 0, 0, i))], [lanes(slope[h])])

    def outer_phase(left, base, n, right, out):
        def body(o):
            width = o.shape[-1]
            step = min(width, 1024)

            @chunks(width, step)
            def _(at, j):
                value = tn(left[:, cols_of(base)], right[:, at])
                o[(slice(None),) * (len(o.shape) - 1) + (at,)] = value.astype(BF).reshape(o.shape[:-1] + (step,))

        if len(out.shape) == 3:
            target = (out, (T // out.shape[1], out.shape[1], D), lambda i: (i, 0, 0))
        else:
            target = d_rows(out)
        stream(body, (n,), [], [target])

    def down_grad_phase(h):
        outer_phase(hidden, h * ffh, ffh // T, gy, p_down[h])

    def up_grad_phase(h):
        outer_phase(n2, 0, D // T, grad_up.at[:, pl.ds(h * ffh, ffh)], p_up[h])

    def out_grad_phase():
        outer_phase(att, 0, l // T, gy, p_out)

    def qkv_grad_phase():
        def body(o):
            for j in range(3):
                o[:, :, :, j * l : (j + 1) * l] = tn(n1[:, cols_of()], gproj[j]).astype(BF).reshape(o.shape[:-1] + (l,))

        for j in range(3):
            sm[6:7, j * l : (j + 1) * l] = jnp.sum(gproj[j].astype(F32), 0, keepdims=True)
        stream(body, (D // T,), [], [d_rows(p_qkv)])

    def gatt_phase():
        def body(w, o):
            @chunks(L, CH)
            def _(at, i):
                o[0, at, :] = nt(gy[at, :], w[...].reshape(hd, D)).astype(BF)

        w = (out_all, (hd // ro, ro, D), lambda i: (i, 0, 0))
        stream(body, (H,), [w], [(gatt, (1, L, hd), lambda i: (i, 0, 0))])

    def qkv_phase():
        def body(w, o):
            j = pl.program_id(0)
            bias = qkv_b[0:1, pl.ds(pl.multiple_of(j * hd, hd), hd)]

            @chunks(L, CH)
            def _(at, i):
                p = dot(n1[at, :], w[...].reshape(D, hd)) + bias
                o[0, at, 128:] = p[:, 128:].astype(BF)

                @pl.when(j < 2 * H)
                def _():
                    o[0, at, :128] = turn(p[:, :128], tab[0, at, :], tab[1, at, :]).astype(BF)

                @pl.when(j >= 2 * H)
                def _():
                    o[0, at, :128] = p[:, :128].astype(BF)

        w = (qkv_all, (S, dp_n, r, hd), lambda i: (0, 0, 0, i))
        stream(body, (3 * H,), [w], [(heads, (1, L, hd), lambda i: (i, 0, 0))])

    def att_phase():
        def body(q, k, v, ga):
            h, i = pl.program_id(0), pl.program_id(1)
            cols = pl.ds(pl.multiple_of(h * hd, hd), hd)
            low = pl.ds(pl.multiple_of(h * hd, hd), 128)
            high = pl.ds(pl.multiple_of(h * hd + 128, 128), 128)
            back = lambda t, rows: turn(t, tab[0, rows, :], -tab[1, rows, :])

            @pl.when(i == 0)
            def _():
                dk_acc[...] = jnp.zeros_like(dk_acc)
                dv_acc[...] = jnp.zeros_like(dv_acc)

            def tile(c):
                n = (c + 1) * T
                at = slice(c * T, n)
                qt, kt, vt, gt = q[0], k[0, :n], v[0, :n], ga[0]
                query = lax.broadcasted_iota(jnp.int32, (T, n), 0) + c * T
                key = lax.broadcasted_iota(jnp.int32, (T, n), 1)
                allowed = (cols_v[at, doc_at] == doc_row[0:1, :n]) & (key <= query)
                raw = jnp.where(allowed, nt(qt, kt) * scale, -1000000000.0)
                e = jnp.exp(raw - jnp.max(raw, -1, keepdims=True))
                p = e / jnp.sum(e, -1, keepdims=True)
                pb = p.astype(BF)
                att[at, cols] = dot(pb, vt).astype(BF)
                gp = nt(gt, vt)
                gs = (p * (gp - jnp.sum(gp * p, -1, keepdims=True))).astype(BF)
                gq = dot(gs, kt) * scale
                gproj[0, at, low] = back(gq[:, :128], at).astype(BF)
                gproj[0, at, high] = gq[:, 128:].astype(BF)
                dk_acc[:n, :] += tn(gs, qt)
                dv_acc[:n, :] += tn(pb, gt)

            for c in range(L // T):
                pl.when(i == c)(functools.partial(tile, c))

            @pl.when(i == L // T - 1)
            def _():
                gk = dk_acc[...] * scale
                gproj[1, :, low] = back(gk[:, :128], slice(None)).astype(BF)
                gproj[1, :, high] = gk[:, 128:].astype(BF)
                gproj[2, :, cols] = dv_acc[...].astype(BF)

        block = (1, T, hd)
        full = (1, L, hd)
        stream(
            body,
            (H, L // T),
            [
                (heads, block, lambda h, i: (h, i, 0)),
                (heads, full, lambda h, i: (H + h, 0, 0)),
                (heads, full, lambda h, i: (2 * H + h, 0, 0)),
                (gatt, block, lambda h, i: (h, i, 0)),
            ],
            [],
        )

    def norm_sums(grad, xb, at, row):
        cols = cols_of()
        hat = (xb[at, :].astype(F32) - cols_v[at, mean_at]) * cols_v[at, inv_at]
        sm[row : row + 1, cols] += jnp.sum(grad * hat, 0, keepdims=True)
        sm[row + 1 : row + 2, cols] += jnp.sum(grad, 0, keepdims=True)

    def one_phase():
        def body(w, xb, o):
            @chunks(L, CH)
            def _(at, m):
                grad = 0.0
                for j in range(3):
                    grad = grad + nt(gproj[j, at, :], w[:, :, :, j * l : (j + 1) * l].reshape(T, l))
                norm_sums(grad, xb, at, 0)
                o[at, :] = grad * vec[0:1, cols_of()]

        stream(body, (D // T,), [d_rows(qkv_all), lanes(x)], [lanes(wide_f)])

    per_ch = max(1, CH // tok)

    def two_phase():
        def body(wa, wb, xb, first, o):
            @chunks(L, per_ch * tok)
            def _(at, m):
                grad = nt(grad_up[at, :ffh], wa[...].reshape(T, ffh)) + nt(grad_up[at, ffh:ff], wb[...].reshape(T, ffh))
                norm_sums(grad, xb, at, 2)
                value = first[at, :] + grad * vec[2:3, cols_of()]
                o[pl.ds(m * per_ch, per_ch)] = value.astype(BF).reshape(per_ch, tok, T)

        stream(
            body,
            (D // T,),
            [d_rows(up_all[0]), d_rows(up_all[1]), lanes(x), lanes(wide_f)],
            [(wide, (S, tok, T), lambda i: (0, 0, i))],
        )

    def mixed_phase():
        def body(wa, wb, wo, o):
            @chunks(L, per_ch * tok)
            def _(at, m):
                value = dot(hidden[at, :ffh], wa[...].reshape(ffh, T)) + dot(hidden[at, ffh:], wb[...].reshape(ffh, T))
                value = value + dot(att[at, :], wo[...].reshape(l, T))
                o[pl.ds(m * per_ch, per_ch)] = value.astype(BF).reshape(per_ch, tok, T)

        cols = lambda ref: (ref, ref.shape[:2] + (T,), lambda i: (0, 0, i))
        ws = [cols(down_all[0]), cols(down_all[1]), cols(out_all)]
        stream(body, (D // T,), ws, [(mixed, (S, tok, T), lambda i: (0, 0, i))])

    def slope_phase(h):
        def body(w, slo):
            cols = cols_of(h * ffh)

            @chunks(L, CH)
            def _(at, m):
                gu = (nt(gy[at, :], w[...].reshape(T, D)) * slo[at, :].astype(F32)).astype(BF)
                grad_up[at, cols] = gu
                sm[5:6, cols] += jnp.sum(gu.astype(F32), 0, keepdims=True)

        w = (down_all[h], (T // rdh, rdh, D), lambda i: (i, 0, 0))
        stream(body, (ffh // T,), [w, lanes(slope[h])], [])

    ends = 2 if mx.square else 8
    part = tok // ends
    tiles = lambda ref, lead: (ref, (lead, part, D), lambda i: (0, i, 0))
    mine = lambda ref: (ref, (part, D), lambda i: (i, 0))

    def total_of(own, came):
        total = own[0].astype(F32)
        for ref in came:
            for k in range(ref.shape[0]):
                total = total + ref[k].astype(F32)
        return total

    def mixed_end():
        def body(xb, own, *rest):
            rest[-1][0] = (xb[...].astype(F32) + vec[4:5, :] + total_of(own, rest[:-1])).astype(BF)

        stream(body, (ends,), [mine(x_own), tiles(mixed.at[pl.ds(s, 1)], 1)] + mx.ins(part), [tiles(mixed_out, 1)])

    def input_end():
        def body(xb, gb, own, *rest):
            at = pl.ds(pl.multiple_of(s * tok + pl.program_id(0) * part, part), part)
            inv = cols_v[at, inv_at]
            hat = (xb[...].astype(F32) - cols_v[at, mean_at]) * inv
            total = total_of(own, rest[:-1])
            total = total - jnp.mean(total, -1, keepdims=True) - hat * jnp.mean(total * hat, -1, keepdims=True)
            rest[-1][0] = gb[...].astype(F32) + inv * total

        ins = [mine(x_own), mine(gy_own), tiles(wide.at[pl.ds(s, 1)], 1)] + wx.ins(part)
        stream(body, (ends,), ins, [tiles(input_grad, 1)])

    net.barrier()
    loc.start()
    for load in up_loads:
        load.start()
    small_first()
    o_g.early()
    o_g.start()
    cut_up()
    su[0].start()
    o_g.go(1)
    x_g.start()
    for x_sq in sq:
        x_sq.start()
    loc.finish()
    su[0].wait()
    u_g[0].early()
    u_g[0].start()
    o_g.go(2)
    d_g[0].early()
    u_g[0].go(1)
    small_second()
    x_g.relay()
    for x_sq in sq:
        x_sq.wait()
    q_g.early()
    gy_g.start()
    u_g[0].go(2)
    u_g[0].go(3)
    d_g[1].early()
    u_g[0].wait()
    q_g.start()
    x_g.wait()
    unpack()
    norm_phase()
    o_g.go(3)
    q_g.go(1)
    gy_g.relay()
    up_phase(0)
    q_g.go(2)
    su[1].start()
    d_g[1].start()
    gy_g.wait()
    down_grad_phase(0)
    su[1].wait()
    u_g[1].early()
    ds[0].start()
    o_g.wait()
    gatt_phase()
    q_g.go(3)
    q_g.wait()
    u_g[1].start()
    ds[0].pair()
    qkv_phase()
    d_g[0].start()
    att_phase()
    out_grad_phase()
    os.start()
    os.pair()
    d_g[0].go(1)
    u_g[1].go(1)
    qkv_grad_phase()
    qs.start()
    os.go(1)
    d_g[0].go(2)
    ds[0].go(1)
    qs.pair()
    one_phase()
    d_g[0].go(3)
    u_g[1].go(2)
    d_g[1].go(1)
    d_g[0].wait()
    slope_phase(0)
    u_g[1].go(3)
    qs.go(1)
    up_grad_phase(0)
    us[0].start()
    u_g[1].wait()
    d_g[1].go(2)
    up_phase(1)
    us[0].pair()
    d_g[1].go(3)
    d_g[1].wait()
    slope_phase(1)
    qs.go(2)
    two_phase()
    sums_first()
    us[0].go(1)
    wx.start()
    ds[0].go(2)
    up_grad_phase(1)
    us[1].start()
    sums_second()
    qs.go(3)
    qs.total()
    qx.start()
    us[0].go(2)
    us[1].pair()
    mixed_phase()
    mx.start()
    us[1].go(1)
    down_grad_phase(1)
    us[0].go(3)
    os.go(2)
    us[1].go(2)
    ds[1].start()
    us[0].total()
    wx.mid()
    os.go(3)
    out_total()
    ds[1].pair()
    ux[0].start()
    ds[1].go(1)
    mx.mid()
    us[1].go(3)
    ds[1].go(2)
    ux[0].wait()
    qx.wait()
    wx.wait()
    us[1].total()
    ds[0].go(3)
    ux[1].start()
    input_end()
    down_total(0)
    mx.wait()
    mixed_end()
    ds[1].go(3)
    down_total(1)
    ux[1].wait()
    sm_x.wait()
    for copy in [out_copies[0]] + begun:
        copy.wait()
    net.drain()


def layer(seq_n, dp_n, dims, args):
    L, D, ff, H, r, ro, rd = dims
    l, Z, ffh, rdh = H * HD, dp_n // 2, ff // 2, rd // 2
    tok = L // seq_n
    seq_tok, up_slab, qkv_slab = (seq_n, tok, D), (seq_n, r, ffh), (seq_n, r, 3 * l)
    outs = [((1, tok, D), BF), ((1, tok, D), F32), (qkv_slab, BF), ((1, ro, D), F32), ((1, rd, D), F32), ((seq_n, 8, D), F32)]
    outs += [(up_slab, BF)] * 2
    half = tok // 2
    if seq_n == 4:
        outs += [((4, half, D), BF), ((2, half, D), BF), ((2, half, D), BF)] * 2
    else:
        outs += [((seq_n - 1, tok, D), BF), ((16, 128), BF), ((16, 128), BF)] * 2
    outs += [((L, D), BF), ((seq_n, dp_n, r, 3 * l), BF), ((dp_n, ro, D), BF), ((3 * H, L, HD), BF), ((H, L, HD), BF)]
    outs += [((L, D), F32), ((seq_n, dp_n, r, 3 * l), BF), ((dp_n, ro, D), BF), (seq_tok, BF), (seq_tok, BF)]
    up_full, down_full = (seq_n, dp_n, r, ffh), (dp_n, rdh, D)
    for v in (up_full, down_full, (L, ffh), up_full, down_full):
        outs += [(v, BF)] * 2
    slabs = [(1, rdh, D)] * 2 + [up_slab] * 2 + [qkv_slab, (1, ro, D)]
    for slab in slabs:
        outs += [((Z - 1,) + slab, BF)] * 2
    out_shape = [shape(*o) for o in outs]
    n = 6 * (4 * Z - 3) + 6 * (3 * Z - 2) + 14 * (seq_n - 1) + 2 * max(4, seq_n - 1) + 2 * (dp_n - 1)
    vmem = [((seq_n, dp_n, 16, 128), F32), ((8, D), F32), ((8, ffh), F32), ((8, 3 * l), F32), ((8, L), F32), ((L, 128), F32)]
    vmem += [((8, D), F32), ((dp_n, 8, D), F32), ((8, D), F32), ((L, HD), F32), ((L, HD), F32)]
    vmem += [((1, ro, D), F32), ((1, rdh, D), F32), ((2, L, 128), F32)]
    vmem += [((L, D), BF), ((L, D), BF), ((L, D), BF), ((L, ff), BF), ((L, l), BF), ((3, L, l), BF)]
    for slab in slabs:
        vmem += [((Z,) + slab, BF)] * 2
    scratch = [pltpu.SemaphoreType.DMA((k,)) for k in (n, n, 40 + seq_n + 6 * (3 * Z - 2))] + [pltpu.VMEM(*v) for v in vmem]
    return pl.pallas_call(
        functools.partial(layer_kernel, seq_n, dp_n, dims, len(args), len(outs)),
        out_shape=out_shape,
        in_specs=[ANY] * len(args),
        out_specs=[ANY] * len(outs),
        scratch_shapes=scratch,
        compiler_params=pltpu.CompilerParams(collective_id=0, has_side_effects=True, vmem_limit_bytes=63 * MIB),
        name="layer",
    )(*args)[:8]


def last_kernel(dims, seq_n, dp_n, places, *refs):
    L, D, ff, H, r, ro, rd = dims
    l, ffh, rdh = H * HD, ff // 2, rd // 2
    ins, outs, acc = refs[:8], refs[8:-1], refs[-1]
    mixed, grad, qkv, out_w, down, sums, up_a, up_b = ins
    mixed_out, grad_out, up_out, qkv_out, out_out, down_out = outs[:6]
    small = outs[6:]
    mixed_out[...] = mixed[...]
    grad_out[...] = grad[...]
    out_out[...] = out_w[0]
    down_out[...] = down[0]
    for k in range(seq_n):
        for m in range(dp_n):
            for h, src in enumerate((up_a, up_b)):
                at = k * ff + m * rd + h * rdh
                up_out[:, at : at + rdh] = src[k, :, m * rdh : (m + 1) * rdh].astype(F32)
        for j in range(3):
            at = (j * seq_n + k) * l
            qkv_out[:, at : at + l] = qkv[k, :, j * l : (j + 1) * l].astype(F32)

    @pl.when(pl.program_id(0) == 0)
    def _():
        s, d = places[0], places[1]
        place = s * dp_n + d
        acc[...] = sums[0]
        for k in range(1, seq_n):
            acc[...] += sums[k]

        def piece(load, lane):
            start = pl.multiple_of(lax.div(lane, 128) * 128, 128)
            return pltpu.roll(load(pl.ds(start, 128)), lax.rem(128 - lax.rem(lane, 128), 128), 1)

        for j in range(5):
            small[j][...] = piece(lambda at, j=j: acc[j : j + 1, at], place * r)[:, :r]
        for t in range(3):
            at = place * 3 + t
            j, rest = lax.div(at, D // r), lax.rem(at, D // r)
            of, m = lax.div(rest, l // r), lax.rem(rest, l // r)
            small[5][:, t * r : (t + 1) * r] = piece(lambda at, of=of: sums[of, 6:7, at], j * l + m * r)[:, :r]
        for h in range(2):
            small[6][:, h * rdh : (h + 1) * rdh] = piece(lambda at: sums[s, 5:6, at], h * ffh + d * rdh)[:, :rdh]


def finish(seq_n, dp_n, dims, got):
    L, D, ff, H, r, ro, rd = dims
    tok = L // seq_n
    steps = 4 if r % 64 == 0 else 1
    places = jnp.stack([lax.axis_index("seq"), lax.axis_index("dp")]).astype(jnp.int32)

    def spec(v, axis):
        block = tuple(n // steps if k == axis else n for k, n in enumerate(v.shape))
        return pl.BlockSpec(block, lambda i, p: tuple(i if k == axis else 0 for k in range(v.ndim)))

    outs = [((1, tok, D), BF, 1), ((1, tok, D), F32, 1), ((r, seq_n * ff), F32, 0), ((r, 3 * D), F32, 0), ((ro, D), F32, 0), ((rd, D), F32, 0)]
    outs += [((1, r), F32, None)] * 5 + [((1, 3 * r), F32, None), ((1, rd), F32, None)]
    out_shape = [shape(*o[:2]) for o in outs]
    return pl.pallas_call(
        functools.partial(last_kernel, dims, seq_n, dp_n),
        grid_spec=pltpu.PrefetchScalarGridSpec(
            num_scalar_prefetch=1,
            grid=(steps,),
            in_specs=[spec(v, axis) for v, axis in zip(got, (1, 1, 1, 1, 1, None, 1, 1))],
            out_specs=[spec(v, o[2]) for v, o in zip(out_shape, outs)],
            scratch_shapes=[pltpu.VMEM((8, D), F32)],
        ),
        out_shape=out_shape,
        compiler_params=pltpu.CompilerParams(vmem_limit_bytes=63 * MIB),
        name="finish",
    )(places, *got)
def shards(
    tokens,
    doc_ids,
    ln1_gain,
    ln1_bias,
    ln2_gain,
    ln2_bias,
    qkv_weight,
    qkv_bias,
    out_weight,
    up_weight,
    up_bias,
    down_weight,
    out_bias,
    cotangent,
):
    seq_n = lax.axis_size("seq")
    dp_n = lax.axis_size("dp")
    seq_i = lax.axis_index("seq")
    tok_rows, width = tokens.shape[1:]
    length = tok_rows * seq_n
    head_dim = width // HEADS
    heads = HEADS // seq_n
    local = heads * head_dim
    ff = up_weight.shape[1] // seq_n
    rot_dims = head_dim // 4
    rows, per_down = qkv_weight.shape[0], down_weight.shape[0]
    vectors = (ln1_gain, ln1_bias, ln2_gain, ln2_bias, out_bias, qkv_bias, up_bias)
    total, at, flat = sum(v.shape[0] for v in vectors), 0, 0.0
    for v in vectors:
        flat = flat + jnp.pad(v.astype(F32), (at, total - at - v.shape[0]))
        at += v.shape[0]
    pieces = jnp.tile(flat.reshape(-1, rows), (1, 128 // rows))
    docs = doc_ids.astype(F32).reshape(-1, 128)
    over = 16 - pieces.shape[0]
    small = jnp.pad(pieces, ((0, over), (0, 0))) + jnp.pad(docs, ((16 - over, over - docs.shape[0]), (0, 0)))
    dims = (length, width, ff, heads, rows, out_weight.shape[0], per_down)
    tables = jnp.asarray(rotary_rows(length, rot_dims))
    x, gy = tokens[0], cotangent[0]
    got = layer(seq_n, dp_n, dims, (x, gy, up_weight, qkv_weight, out_weight, down_weight, small, tables))
    mixed, input_grad, up_grad, qkv_grad, out_grad, down_grad, *small = finish(seq_n, dp_n, dims, got)
    g1, b1, g2, b2, ob, qb, ub = [v.reshape(-1) for v in small]
    return (mixed, input_grad, g1, b1, g2, b2, qkv_grad, qb, out_grad, up_grad, ub, down_grad, ob)


def solution(mesh):
    in_specs = (
        P("dp", "seq", None),
        P("dp", "seq"),
        P(("seq", "dp")),
        P(("seq", "dp")),
        P(("seq", "dp")),
        P(("seq", "dp")),
        P(("seq", "dp"), None),
        P(("seq", "dp")),
        P(("seq", "dp"), None),
        P(("seq", "dp"), None),
        P(("seq", "dp")),
        P(("seq", "dp"), None),
        P(("seq", "dp")),
        P("dp", "seq", None),
    )
    out_specs = (
        P("dp", "seq", None),
        P("dp", "seq", None),
        P(("seq", "dp")),
        P(("seq", "dp")),
        P(("seq", "dp")),
        P(("seq", "dp")),
        P(("seq", "dp"), None),
        P(("seq", "dp")),
        P(("seq", "dp"), None),
        P(("seq", "dp"), None),
        P(("seq", "dp")),
        P(("seq", "dp"), None),
        P(("seq", "dp")),
    )
    return jax.shard_map(shards, mesh=mesh, in_specs=in_specs, out_specs=out_specs, check_vma=False)
```
